512 devices in a mesh: seq: 128 (over y, z, core), fsdp: 4 (over x).
Axes of the slice: x: 4, y: 8, z: 8, core: 2. Of those that a mesh axis runs over, the one named last changes fastest.
Arguments:
- tokens: bfloat16 [4, 16384, 2048], P('fsdp', 'seq'), may hold values from -14 to 14
- w_qkv: bfloat16 [2048, 3, 1024], P(None, None, 'fsdp'), may hold values from -0.125 to 0.125
- w_feature: bfloat16 [8, 128, 16], replicated, may hold values from -2 to 2
- norm_gain: float32 [1024], replicated, may hold values from 0.5 to 1.5
- log_decay: float32 [4, 8, 16384], P('fsdp', None, 'seq'), may hold values from -1.5 to 0
- pattern: int32 [4, 256, 3], P('fsdp', 'seq'), may hold values from 1 to 255, as said below
Outputs:
- mixed: bfloat16 [4, 16384, 1024], P('fsdp', 'seq')
The draws below stay inside these ranges and needn't reach their ends.
Inputs may be any that keep to these rules, and one draw needn't show every extreme that they name: `pattern`: the 3 blocks of query block b are distinct, none is among the first 1 block or equal to b - 1, b or b + 1, and each lies in a segment at most 3 segments from b's segment; the first lies exactly 3 segments later where that segment exists, else 3 segments earlier.
All inputs are finite; a program needn't handle non-finite values.
Results may differ from the reference program's by a relative error of at most 0.0097.
The reference program's roundings to bfloat16 on the way count: a program that leaves them out, or rounds other values in their place, can miss the bound.
Values may be sent and summed in bfloat16 or wider, within the bound.
No kernel may reach another device: no remote copies, remote signals or barrier semaphores. Data moves between devices by JAX's collectives and lax.ppermute only.
A program may use at most 64 MiB of HBM per device.

```python
import math
import jax
import jax.numpy as jnp
from jax import lax

D = 2048
HALF_HEADS = 8
DH = 128
F = 16
HD = 1024
BS = 64
G = 1
R = 3
RD = 3
TOK_DEV = 128
DOCUMENT_COUNT = 4
DOCUMENT_LENGTH = 16384
NB_DEV = 2
NBLOCKS = 256


def draw_tokens(key, part):
    key_base = jax.random.fold_in(key, 0)
    full_shape = (DOCUMENT_COUNT, DOCUMENT_LENGTH, D)
    drawn = jnp.clip(jax.random.normal(key_base, full_shape, jnp.float32), -5.0, 5.0)
    return drawn.astype(jnp.bfloat16)


def draw_log_decay(key, part):
    divided_keys = jax.random.split(key, 7)
    fast_share = 0.5
    fast_head = jax.random.uniform(divided_keys[0], (DOCUMENT_COUNT, HALF_HEADS, 1), jnp.float32) < fast_share
    fast_rate = jnp.exp(jax.random.uniform(divided_keys[1], (DOCUMENT_COUNT, HALF_HEADS, 1), jnp.float32, math.log(1.0 / 50.0), math.log(1.0 / 30.0)))
    slow_rate = jax.random.uniform(divided_keys[2], (DOCUMENT_COUNT, HALF_HEADS, 1), jnp.float32, 0.2, 0.5) / DOCUMENT_LENGTH
    segment_log = jax.random.uniform(divided_keys[3], (DOCUMENT_COUNT, HALF_HEADS, DOCUMENT_LENGTH // TOK_DEV), jnp.float32, -0.4, 0.4)
    segment_factor = jnp.exp(jnp.repeat(segment_log, TOK_DEV, axis=2))
    jitter = jax.random.uniform(divided_keys[4], (DOCUMENT_COUNT, HALF_HEADS, DOCUMENT_LENGTH), jnp.float32, 0.7, 1.3)
    decay_per_step = jnp.where(fast_head, fast_rate, slow_rate) * segment_factor * jitter
    spike_location = jax.random.randint(divided_keys[5], (DOCUMENT_COUNT, HALF_HEADS, 2, 1), 0, DOCUMENT_LENGTH)
    spike_keep_mask = jnp.log(jax.random.uniform(divided_keys[6], (DOCUMENT_COUNT, HALF_HEADS, 2, 1), jnp.float32, 0.5, 0.8))
    token_positions = jnp.arange(DOCUMENT_LENGTH, dtype=jnp.int32)
    spike_events = jnp.sum(jnp.where(token_positions == spike_location, spike_keep_mask, 0.0), axis=2)
    return (spike_events - decay_per_step).astype(jnp.float32)


def draw_pattern(key, part):
    block_index = jnp.arange(NBLOCKS, dtype=jnp.int32)[:, None]
    segment = block_index // NB_DEV
    window_size = (2 * RD + 1) * NB_DEV
    offset = jnp.arange(window_size, dtype=jnp.int32)[None, :]
    candidate = (segment - RD) * NB_DEV + offset
    allowed = (candidate >= G) & (candidate < NBLOCKS) & (jnp.abs(candidate - block_index) > 1)
    segment_total = NBLOCKS // NB_DEV
    far_segment = jnp.where(segment + RD < segment_total, segment + RD, segment - RD)
    distant = allowed & (jnp.floor_divide(candidate, NB_DEV) == far_segment)
    scores = jax.random.randint(key, (DOCUMENT_COUNT, NBLOCKS, window_size), 0, 1 << 20) * window_size + offset[None]
    first_score = jnp.where(distant[None], scores, -1)
    _, first_pos = lax.top_k(first_score, 1)
    rest_score = jnp.where(allowed[None] & (offset[None] != first_pos), scores, -1)
    _, rest_pos = lax.top_k(rest_score, R - 1)
    token_positions = jnp.concatenate([first_pos, rest_pos], axis=-1)
    chosen = jnp.take_along_axis(jnp.broadcast_to(candidate[None], scores.shape), token_positions, axis=-1)
    return chosen.astype(jnp.int32)


def level_of(rng, extent, cuts, low, high):
    def one(position, shards_of):
        heights = jax.random.uniform(jax.random.fold_in(jax.random.fold_in(rng, 6), position), (shards_of,), jnp.float32, low / len(cuts), high / len(cuts))
        return jnp.repeat(jnp.exp(heights), extent[position] // shards_of).reshape((-1,) + (1,) * (len(extent) - position - 1))

    level = one(*cuts[0])
    for cut in cuts[1:]:
        level = level * one(*cut)
    return level


def centred(own_key, shape, deviation, reach, cuts=(), kind=jnp.bfloat16):
    values = deviation * jax.random.normal(own_key, shape, jnp.float32)
    if cuts:
        values = values * level_of(own_key, shape, cuts, -0.22, 0.18)
    return jnp.clip(values, -reach, reach).astype(kind)


def setup_inputs(seed: int = 0) -> dict:
    keys = jax.random.split(jax.random.key(seed), 7)
    return {
        "tokens": draw_tokens(jax.random.fold_in(keys[6], 71), 0),
        "w_qkv": centred(keys[1], (D, 3, HD), D ** -0.5, 0.125, ((2, 4),)),
        "w_feature": centred(keys[2], (HALF_HEADS, DH, F), (DH // 16) ** -0.5, 2.0),
        "norm_gain": jnp.clip(1.0 + 0.1 * jax.random.normal(keys[3], (HD,), jnp.float32), 0.5, 1.5),
        "log_decay": draw_log_decay(jax.random.fold_in(keys[6], 71), 0),
        "pattern": draw_pattern(jax.random.fold_in(keys[6], 71), 0),
    }


epsilon = 1e-06
masked_score = -1e+30

def feature_map(projected_head, w_feature):
    logits = jnp.einsum('thd,hdf->htf', projected_head.astype(jnp.float32), w_feature.astype(jnp.float32))
    return jax.nn.softmax(logits, axis=-1).astype(jnp.bfloat16)

def segment_step(carried, inputs):
    phi_query, phi_key, values, log_steps = inputs
    cumulative = jnp.cumsum(log_steps, axis=1)
    final_log = cumulative[:, -1:]
    weighted_key = (jnp.exp(final_log - cumulative)[:, :, None] * phi_key.astype(jnp.float32)).astype(jnp.bfloat16)
    values_wide = values.astype(jnp.float32)
    local_state = jnp.einsum('htf,thd->hfd', weighted_key.astype(jnp.float32), values_wide)
    scores = jnp.einsum('htf,hsf->hts', phi_query.astype(jnp.float32), phi_key.astype(jnp.float32))
    log_gap = cumulative[:, :, None] - cumulative[:, None, :]
    length = log_steps.shape[1]
    causal = jnp.arange(length)[:, None] >= jnp.arange(length)[None, :]
    decay_matrix = jnp.where(causal[None], jnp.exp(jnp.minimum(log_gap, 0.0)), 0.0)
    mixing = (scores * decay_matrix).astype(jnp.bfloat16)
    local_term = jnp.einsum('hts,shd->thd', mixing.astype(jnp.float32), values_wide)
    carried_term = jnp.einsum('htf,hfd->thd', phi_query.astype(jnp.float32), carried, precision=lax.Precision.HIGHEST)
    carried_term = carried_term * jnp.exp(cumulative).T[:, :, None]
    new_state = jnp.exp(final_log)[:, :, None] * carried + local_state
    return (new_state, local_term + carried_term)

def sparse_block(query_block, near_keys, near_values, far_keys, far_values, usable_keys):
    score_scale = DH ** (-0.5)
    query_wide = query_block.astype(jnp.float32)
    near_scores = jnp.einsum('qhd,khd->hqk', query_wide, near_keys.astype(jnp.float32)) * score_scale
    near_scores = jnp.where(usable_keys[None, None, :], near_scores, masked_score)
    far_scores = jnp.einsum('qhd,khd->hqk', query_wide, far_keys.astype(jnp.float32)) * score_scale
    scores_all = jnp.concatenate([near_scores, far_scores], axis=-1)
    highest = lax.optimization_barrier(jnp.max(scores_all, axis=-1, keepdims=True))
    exponent = jnp.exp(scores_all - highest)
    denominator = lax.optimization_barrier(jnp.sum(exponent, axis=-1, keepdims=True))
    soft_weights = (exponent / denominator).astype(jnp.bfloat16).astype(jnp.float32)
    near_count = near_keys.shape[0]
    result = jnp.einsum('hqk,khd->qhd', soft_weights[..., :near_count], near_values.astype(jnp.float32))
    return result + jnp.einsum('hqk,khd->qhd', soft_weights[..., near_count:], far_values.astype(jnp.float32))

def one_document(document, decay_row, pattern_row, w_qkv, w_feature, norm_gain):
    projected = jnp.dot(document, w_qkv.reshape(D, 3 * HD), preferred_element_type=jnp.float32)
    projected = projected.astype(jnp.bfloat16).reshape(DOCUMENT_LENGTH, 3, HALF_HEADS, DH)
    queries = projected[:, 0]
    key_rows = projected[:, 1]
    values = projected[:, 2]
    phi_query = feature_map(queries, w_feature)
    phi_key = feature_map(key_rows, w_feature)
    segment_count = DOCUMENT_LENGTH // TOK_DEV
    inputs = (phi_query.reshape(HALF_HEADS, segment_count, TOK_DEV, F).transpose(1, 0, 2, 3), phi_key.reshape(HALF_HEADS, segment_count, TOK_DEV, F).transpose(1, 0, 2, 3), values.reshape(segment_count, TOK_DEV, HALF_HEADS, DH), decay_row.reshape(HALF_HEADS, segment_count, TOK_DEV).transpose(1, 0, 2))
    _, linear = lax.scan(segment_step, jnp.zeros((HALF_HEADS, F, DH), jnp.float32), inputs)
    linear = linear.reshape(DOCUMENT_LENGTH, HALF_HEADS, DH)
    normed = linear * lax.rsqrt(lax.optimization_barrier(jnp.mean(linear * linear, axis=-1, keepdims=True)) + epsilon)
    normed = normed * norm_gain.reshape(HALF_HEADS, DH)
    key_blocks = key_rows.reshape(NBLOCKS, BS, HALF_HEADS, DH)
    value_blocks = values.reshape(NBLOCKS, BS, HALF_HEADS, DH)
    far_keys = key_rows[:G * BS]
    far_values = values[:G * BS]

    def attend(block_index):
        near_blocks = block_index + jnp.arange(-1, 2, dtype=jnp.int32)
        usable_near = (near_blocks >= G) & (near_blocks < NBLOCKS)
        chosen = jnp.concatenate([near_blocks, pattern_row[block_index].astype(jnp.int32)])
        chosen = jnp.clip(chosen, 0, NBLOCKS - 1)
        usable = jnp.concatenate([usable_near, jnp.ones((R,), dtype=bool)])
        near_keys = key_blocks[chosen].reshape((3 + R) * BS, HALF_HEADS, DH)
        near_values = value_blocks[chosen].reshape((3 + R) * BS, HALF_HEADS, DH)
        query_block = lax.dynamic_slice_in_dim(queries, (block_index * BS).astype(jnp.int32), BS, 0)
        return sparse_block(query_block, near_keys, near_values, far_keys, far_values, jnp.repeat(usable, BS))
    sparse = lax.map(attend, jnp.arange(NBLOCKS, dtype=jnp.int32)).reshape(DOCUMENT_LENGTH, HALF_HEADS, DH)
    return (normed + sparse).astype(jnp.bfloat16).reshape(DOCUMENT_LENGTH, HD)

def reference(tokens, w_qkv, w_feature, norm_gain, log_decay, pattern):

    def per_document(inputs):
        return one_document(inputs[0], inputs[1], inputs[2], w_qkv, w_feature, norm_gain)
    return lax.map(per_document, (tokens, log_decay, pattern))
```

```python
import jax
import jax.numpy as jnp
from jax import lax
from jax.experimental import pallas as pl
from jax.experimental.pallas import tpu as pltpu
from jax.sharding import PartitionSpec as P

HALF_HEADS = 8
DH = 128
F = 16
HD = 1024
D = 2048
BS = 64
R = 3
TOK = 128
NB = 2
DOCS = 4
EPS = 1e-06
MASKED = -1e30
CHIPS = 64
ROWS = 208
BF = jnp.bfloat16
F32 = jnp.float32
HIGH = lax.Precision.HIGHEST


def nt(a, b):
    return lax.dot_general(a, b, (((1,), (1,)), ((), ())), preferred_element_type=F32)


def mm(a, b, precision=None):
    return jnp.dot(a, b, preferred_element_type=F32, precision=precision)


def softmax0(logits):
    top = jnp.max(logits, axis=0, keepdims=True)
    e = jnp.exp(logits - top)
    return e / jnp.sum(e, axis=0, keepdims=True)


def split2(a):
    hi = a.astype(BF)
    return hi, (a - hi.astype(F32)).astype(BF)


def split3(a):
    hi, rest = a.astype(BF), None
    rest = a - hi.astype(F32)
    mid = rest.astype(BF)
    return hi, mid, (rest - mid.astype(F32)).astype(BF)


def cumulative_of(steps):
    row = lax.broadcasted_iota(jnp.int32, (TOK, TOK), 0)
    col = lax.broadcasted_iota(jnp.int32, (TOK, TOK), 1)
    return mm(steps, jnp.where(row <= col, 1.0, 0.0).astype(F32), HIGH)


def project_kernel(scal, t0, ta, tb, td1, td2, w, kv_own, kv_other, kvq_other, q_own, rows):
    c, x = scal[0], scal[1]
    rows[0:128] = t0[...]
    rows[128:256] = ta[...]
    rows[256:320] = td1[...]
    rows[320:384] = td2[...]
    rows[384:512] = tb[...]
    parts = [mm(rows[...], w[k]).astype(BF) for k in range(3)]
    first = c == 0
    for r in range(DOCS):
        n = lax.rem(x - r + DOCS, DOCS)
        own, other = [], []
        for k in range(3):
            lo = parts[k][r * TOK : (r + 1) * TOK, :DH]
            hi = parts[k][r * TOK : (r + 1) * TOK, DH:]
            own.append(jnp.where(first, lo, hi))
            other.append(jnp.where(first, hi, lo))
        q_own[n] = own[0]
        kv_own[n, :, :DH] = own[1]
        kv_own[n, :, DH:] = own[2]
        kv_other[n, :, :DH] = other[1]
        kv_other[n, :, DH:] = other[2]
        kvq_other[n, :, :DH] = other[1]
        kvq_other[n, :, DH : 2 * DH] = other[2]
        kvq_other[n, :, 2 * DH :] = other[0]


def states_kernel(scal, kv_own, kvq_mate, steps, wft, out, state0):
    c, h = scal[0], scal[5]
    first = c == 0
    cum = cumulative_of(steps[...])
    feature = wft[h]
    states, decays = [], []
    for n in range(DOCS):
        own = kv_own[n]
        mate = kvq_mate[n, :, : 2 * DH]
        segs = (jnp.where(first, own, mate), jnp.where(first, mate, own))
        local = []
        for s in range(2):
            phi = softmax0(nt(feature, segs[s][:, :DH])).astype(BF).astype(F32)
            line = cum[2 * n + s : 2 * n + s + 1]
            final = line[:, TOK - 1 :]
            weighted = (jnp.exp(final - line) * phi).astype(BF)
            local.append(mm(weighted, segs[s][:, DH:]))
        last0 = jnp.broadcast_to(cum[2 * n : 2 * n + 1, TOK - 1 :], (1, TOK))
        last1 = jnp.broadcast_to(cum[2 * n + 1 : 2 * n + 2, TOK - 1 :], (1, TOK))
        state0[n] = local[0]
        states.append(jnp.exp(last1) * local[0] + local[1])
        decays.append(last0 + last1)
        for half in range(2):
            out[2 * n + half, 144:176] = segs[0][32 * half : 32 * half + 32, :DH]
            out[2 * n + half, 176:208] = segs[0][32 * half : 32 * half + 32, DH:]
    put_states(out, jnp.concatenate(states, axis=0), decays)


def put_states(out, state, decays):
    hi, lo = split2(state)
    three = split3(jnp.concatenate(decays, axis=0))
    tail = jnp.concatenate(
        [p.astype(F32) for p in three] + [jnp.zeros((4, TOK), F32)], axis=0
    ).astype(BF)
    for peer in range(8):
        out[peer, 0:64] = hi
        out[peer, 64:128] = lo
        out[peer, 128:144] = tail


def get_states(got, peer):
    state = got[peer, 0:64].astype(F32) + got[peer, 64:128].astype(F32)
    tail = got[peer, 128:144].astype(F32)
    decay = (tail[0:4] + tail[4:8]) + tail[8:12]
    wide = jnp.concatenate(
        [jnp.broadcast_to(decay[n : n + 1], (F, TOK)) for n in range(DOCS)], axis=0
    )
    return state, decay, wide


def row_kernel(scal, got, out, inner, outer):
    z = scal[3]
    total = jnp.zeros((64, TOK), F32)
    before = jnp.zeros((64, TOK), F32)
    decays = jnp.zeros((4, TOK), F32)
    reach = jnp.zeros((64, TOK), F32)
    for peer in range(8):
        state, decay, wide = get_states(got, peer)
        grow = jnp.exp(wide)
        use = peer < z
        before = jnp.where(use, before * grow + state, before)
        reach = jnp.where(use, reach + wide, reach)
        total = total * grow + state
        decays = decays + decay
    inner[...] = before
    outer[...] = jnp.exp(reach)
    put_states(out, total, [decays])
    for peer in range(8):
        out[peer, 144:208] = got[0, 144:208]


def attend_kernel(
    scal, pat, kv_own, q_own, kvq_mate, zps, zpx, zms, zmx, tws, twx, glob, got, inner, outer,
    state0, steps, wft, gain, out, win, qs,
):
    c, q, y, h = scal[0], scal[2], scal[4], scal[5]
    mate = 1 - c
    for n in range(DOCS):
        win[n, 3 + c] = kv_own[n]
        win[n, 3 + mate] = kvq_mate[n, :, : 2 * DH]
        win[n, 1 + c] = zps[n]
        win[n, 1 + mate] = zpx[n]
        win[n, 5 + c] = zms[n]
        win[n, 5 + mate] = zmx[n]
        win[n, 7 * mate] = tws[n]
        win[n, 7 * c] = twx[n]
        qs[n, c] = q_own[n]
        qs[n, mate] = kvq_mate[n, :, 2 * DH :]

    before = jnp.zeros((64, TOK), F32)
    for peer in range(8):
        state, _, wide = get_states(got, peer)
        before = jnp.where(peer < y, before * jnp.exp(wide) + state, before)
    entering = inner[...] + outer[...] * before

    cum = cumulative_of(steps[...])
    cum_t = cum.T
    feature = wft[h]
    row = lax.broadcasted_iota(jnp.int32, (TOK, TOK), 0)
    col = lax.broadcasted_iota(jnp.int32, (TOK, TOK), 1)
    causal = row >= col
    gains = gain[h]
    lane = lax.broadcasted_iota(jnp.int32, (1, 7 * BS), 1)
    scale = DH ** (-0.5)
    for n in range(DOCS):
        carried = entering[F * n : F * n + F]
        for s in range(2):
            line = cum[2 * n + s : 2 * n + s + 1]
            column = cum_t[:, 2 * n + s : 2 * n + s + 1]
            queries = qs[n, s]
            keys = win[n, 3 + s, :, :DH]
            values = win[n, 3 + s, :, DH:]
            phi_q = softmax0(nt(feature, queries)).astype(BF).astype(F32).T
            phi_k = softmax0(nt(feature, keys)).astype(BF)
            decay = jnp.where(causal, jnp.exp(jnp.minimum(column - line, 0.0)), 0.0)
            mixing = (mm(phi_q.astype(BF), phi_k) * decay).astype(BF)
            linear = mm(mixing, values) + mm(phi_q, carried, HIGH) * jnp.exp(column)
            carried = jnp.exp(line[:, TOK - 1 :]) * carried + state0[n]
            square = jnp.mean(linear * linear, axis=1, keepdims=True)
            normed = linear * lax.rsqrt(square + EPS) * gains
            for half in range(2):
                j = 2 * s + half
                block = 4 * q + j
                picks = [win[n, 3 + (j + d) // 2 if j + d >= 0 else 2, pl.ds(BS * ((j + d) % 2), BS)] for d in (-1, 0, 1)]
                for k in range(R):
                    place = pat[12 * n + 3 * j + k]
                    picks.append(
                        win[n, lax.div(place, 2), pl.ds(pl.multiple_of(BS * lax.rem(place, 2), BS), BS)]
                    )
                near = jnp.concatenate(picks, axis=0)
                gk = jnp.concatenate([glob[2 * n, 0:32], glob[2 * n + 1, 0:32]], axis=0)
                gv = jnp.concatenate([glob[2 * n, 32:64], glob[2 * n + 1, 32:64]], axis=0)
                all_k = jnp.concatenate([near[:, :DH], gk], axis=0)
                all_v = jnp.concatenate([near[:, DH:], gv], axis=0)
                scores = nt(queries[half * BS : half * BS + BS], all_k) * scale
                bad = (
                    ((lane < BS) & (block < 2))
                    | ((lane >= BS) & (lane < 2 * BS) & (block < 1))
                    | ((lane >= 2 * BS) & (lane < 3 * BS) & (block > 4 * CHIPS - 2))
                )
                scores = jnp.where(bad, MASKED, scores)
                top = jnp.max(scores, axis=1, keepdims=True)
                e = jnp.exp(scores - top)
                soft = (e / jnp.sum(e, axis=1, keepdims=True)).astype(BF)
                sparse = mm(soft, all_v)
                out[2 * n + s, half * BS : half * BS + BS] = (
                    normed[half * BS : half * BS + BS] + sparse
                ).astype(BF)


def call(kernel, outs, scratch, n_smem, *args):
    vmem = pl.BlockSpec(memory_space=pltpu.VMEM)
    smem = pl.BlockSpec(memory_space=pltpu.SMEM)
    return pl.pallas_call(
        kernel,
        out_shape=outs,
        in_specs=[smem] * n_smem + [vmem] * (len(args) - n_smem),
        out_specs=[vmem] * len(outs),
        scratch_shapes=scratch,
        compiler_params=pltpu.CompilerParams(vmem_limit_bytes=28 * 2**20),
    )(*args)


def shape(dims, dtype):
    return jax.ShapeDtypeStruct(dims, dtype)


def pairs(move):
    found = []
    for q in range(CHIPS):
        for c in range(2):
            to, core = move(q, c)
            if 0 <= to < CHIPS:
                found.append((2 * q + c, 2 * to + core))
    return found


XC = [[(2 * q + c) * 4 + x for x in range(4) for c in range(2)] for q in range(CHIPS)]
ZS = [[(8 * y + z) * 2 + c for z in range(8)] for y in range(8) for c in range(2)]
YS = [[(8 * y + z) * 2 + c for y in range(8)] for z in range(8) for c in range(2)]


def exchange(a, axis, groups):
    return lax.all_to_all(a, axis, 0, 0, tiled=True, axis_index_groups=groups)


def per_device(tokens, w_qkv, w_feature, norm_gain, log_decay, pattern):
    x = lax.axis_index("fsdp")
    s = lax.axis_index("seq")
    c, q = s % 2, s // 2
    z, y = q % 8, q // 8
    h = 2 * x + c
    scal = jnp.stack([c, x, q, z, y, h]).astype(jnp.int32)
    t0 = tokens[0]
    up = [(i, (i + 1) % 4) for i in range(4)]
    down = [(i, (i - 1) % 4) for i in range(4)]
    ta = lax.ppermute(t0, "fsdp", up)
    tb = lax.ppermute(t0, "fsdp", down)
    td1 = lax.ppermute(ta[:64], "fsdp", up)
    td2 = lax.ppermute(tb[64:], "fsdp", down)

    small = jnp.concatenate(
        [
            log_decay[0][:, None, :],
            jnp.broadcast_to(
                jnp.pad(pattern.reshape(1, 1, 6).astype(F32), ((0, 0), (0, 0), (0, 122))),
                (8, 1, TOK),
            ),
            jnp.zeros((8, 6, TOK), F32),
        ],
        axis=1,
    )
    got0 = exchange(small, ("seq", "fsdp"), XC)
    steps = got0[:, 0]
    pat = got0[:, 1, :6].astype(jnp.int32).reshape(48) - (4 * q - 6)
    pat = jnp.clip(pat, 0, 15).astype(jnp.int32)

    w3 = w_qkv.transpose(1, 0, 2)
    wft = w_feature.transpose(0, 2, 1)
    kv_own, kv_other, kvq_other, q_own = call(
        project_kernel,
        [
            shape((DOCS, TOK, 2 * DH), BF),
            shape((DOCS, TOK, 2 * DH), BF),
            shape((DOCS, TOK, 3 * DH), BF),
            shape((DOCS, TOK, DH), BF),
        ],
        [pltpu.VMEM((4 * TOK, D), BF)],
        1,
        scal, t0, ta, tb, td1, td2, w3,
    )
    kvq_mate = lax.ppermute(kvq_other, "seq", pairs(lambda q, c: (q, 1 - c)))
    zps = lax.ppermute(kv_own, "seq", pairs(lambda q, c: (q + 1, c)))
    zms = lax.ppermute(kv_own, "seq", pairs(lambda q, c: (q - 1, c)))
    zpx = lax.ppermute(kv_other, "seq", pairs(lambda q, c: (q + 1, 1 - c)))
    zmx = lax.ppermute(kv_other, "seq", pairs(lambda q, c: (q - 1, 1 - c)))
    tws = lax.ppermute(kv_own, "seq", pairs(lambda q, c: (q + 2, 1) if c else (q - 2, 0)))
    twx = lax.ppermute(kv_other, "seq", pairs(lambda q, c: (q + 2, 0) if c else (q - 2, 1)))

    send1, state0 = call(
        states_kernel,
        [shape((8, ROWS, TOK), BF), shape((DOCS, F, DH), F32)],
        [],
        1,
        scal, kv_own, kvq_mate, steps, wft,
    )
    got1 = exchange(send1, "seq", ZS)
    send2, inner, outer = call(
        row_kernel,
        [shape((8, ROWS, TOK), BF), shape((64, TOK), F32), shape((64, TOK), F32)],
        [],
        1,
        scal, got1,
    )
    got2 = exchange(send2, "seq", YS)
    glob = exchange(jnp.broadcast_to(got2[0, 144:208][None], (8, 64, TOK)), "seq", ZS)

    [out] = call(
        attend_kernel,
        [shape((8, TOK, DH), BF)],
        [pltpu.VMEM((DOCS, 8, TOK, 2 * DH), BF), pltpu.VMEM((DOCS, 2, TOK, DH), BF)],
        2,
        scal, pat, kv_own, q_own, kvq_mate, zps, zpx, zms, zmx, tws, twx, glob, got2, inner, outer,
        state0, steps, wft, norm_gain.reshape(HALF_HEADS, 1, DH),
    )
    mixed = exchange(out, ("seq", "fsdp"), XC)
    return mixed.transpose(1, 0, 2).reshape(1, TOK, HD)


def solution(mesh):
    placed = (
        P("fsdp", "seq", None),
        P(None, None, "fsdp"),
        P(),
        P(),
        P("fsdp", None, "seq"),
        P("fsdp", "seq", None),
    )
    return jax.shard_map(
        per_device, mesh=mesh, in_specs=placed, out_specs=P("fsdp", "seq", None), check_vma=False
    )
```

```python
import jax
import jax.numpy as jnp
from jax import lax
from jax.experimental import pallas as pl
from jax.experimental.pallas import tpu as pltpu
from jax.sharding import PartitionSpec as P

HALF_HEADS = 8
DH = 128
F = 16
HD = 1024
D = 2048
BS = 64
R = 3
TOK = 128
NB = 2
DOCS = 4
EPS = 1e-06
MASKED = -1e30
CHIPS = 64
ROWS = 208
BF = jnp.bfloat16
F32 = jnp.float32
HIGH = lax.Precision.HIGHEST


def nt(a, b):
    return lax.dot_general(a, b, (((1,), (1,)), ((), ())), preferred_element_type=F32)


def mm(a, b, precision=None):
    return jnp.dot(a, b, preferred_element_type=F32, precision=precision)


def softmax0(logits):
    top = jnp.max(logits, axis=0, keepdims=True)
    e = jnp.exp(logits - top)
    return e / jnp.sum(e, axis=0, keepdims=True)


def split2(a):
    hi = a.astype(BF)
    return hi, (a - hi.astype(F32)).astype(BF)


def split3(a):
    hi, rest = a.astype(BF), None
    rest = a - hi.astype(F32)
    mid = rest.astype(BF)
    return hi, mid, (rest - mid.astype(F32)).astype(BF)


def cumulative_of(steps):
    row = lax.broadcasted_iota(jnp.int32, (TOK, TOK), 0)
    col = lax.broadcasted_iota(jnp.int32, (TOK, TOK), 1)
    return mm(steps, jnp.where(row <= col, 1.0, 0.0).astype(F32), HIGH)


def project_kernel(
    scal, t0, at, ab, bt, bb, dt, db, ext, w, kv_own, kv_other, kvq_other, q_own, ext_own, rows, wv, sems
):
    c, x = scal[0], scal[1]
    places = [(t0, 0, 128), (at, 128, 64), (ab, 192, 64), (bt, 384, 64), (bb, 448, 64), (ext, 512, 32), (dt, 256, 64), (db, 320, 64)]
    copies = [pltpu.make_async_copy(w.at[0], wv.at[0], sems.at[8])]
    copies += [
        pltpu.make_async_copy(ref, rows.at[pl.ds(start, size)], sems.at[i])
        for i, (ref, start, size) in enumerate(places)
    ]
    copies += [pltpu.make_async_copy(w.at[k], wv.at[k], sems.at[8 + k]) for k in (1, 2)]
    for copy in copies:
        copy.start()
    first = c == 0
    for copy in copies[:9]:
        copy.wait()
    for k in range(3):
        if k:
            copies[8 + k].wait()
        part = mm(rows[...], wv[k]).astype(BF)
        for r in range(DOCS):
            n = lax.rem(x - r + DOCS, DOCS)
            lo = part[r * TOK : (r + 1) * TOK, :DH]
            hi = part[r * TOK : (r + 1) * TOK, DH:]
            own = jnp.where(first, lo, hi)
            other = jnp.where(first, hi, lo)
            if k == 0:
                q_own[n] = own
                kvq_other[n, :, 2 * DH :] = other
            else:
                here = slice((k - 1) * DH, k * DH)
                kv_own[n, :, here] = own
                kv_other[n, :, here] = other
                kvq_other[n, :, here] = other
        if k:
            ext_own[(k - 1) * 32 : k * 32] = jnp.where(first, part[512:, :DH], part[512:, DH:])


def states_kernel(scal, kv_own, kvq_mate, ext_own, steps, wft, out, state0):
    c, h = scal[0], scal[5]
    first = c == 0
    cum = cumulative_of(steps[...])
    feature = wft[h]
    states, decays = [], []
    for n in range(DOCS):
        own = kv_own[n]
        mate = kvq_mate[n, :, : 2 * DH]
        segs = (jnp.where(first, own, mate), jnp.where(first, mate, own))
        local = []
        for s in range(2):
            phi = softmax0(nt(feature, segs[s][:, :DH])).astype(BF).astype(F32)
            line = cum[2 * n + s : 2 * n + s + 1]
            final = line[:, TOK - 1 :]
            weighted = (jnp.exp(final - line) * phi).astype(BF)
            local.append(mm(weighted, segs[s][:, DH:]))
        last0 = jnp.broadcast_to(cum[2 * n : 2 * n + 1, TOK - 1 :], (1, TOK))
        last1 = jnp.broadcast_to(cum[2 * n + 1 : 2 * n + 2, TOK - 1 :], (1, TOK))
        state0[n] = local[0]
        states.append(jnp.exp(last1) * local[0] + local[1])
        decays.append(last0 + last1)
    put_states(out, jnp.concatenate(states, axis=0), decays)
    for peer in range(8):
        out[peer, 144:208] = ext_own[...]


def put_states(out, state, decays):
    hi, lo = split2(state)
    three = split3(jnp.concatenate(decays, axis=0))
    tail = jnp.concatenate(
        [p.astype(F32) for p in three] + [jnp.zeros((4, TOK), F32)], axis=0
    ).astype(BF)
    for peer in range(8):
        out[peer, 0:64] = hi
        out[peer, 64:128] = lo
        out[peer, 128:144] = tail


def get_states(got, peer):
    state = got[peer, 0:64].astype(F32) + got[peer, 64:128].astype(F32)
    tail = got[peer, 128:144].astype(F32)
    decay = (tail[0:4] + tail[4:8]) + tail[8:12]
    wide = jnp.concatenate(
        [jnp.broadcast_to(decay[n : n + 1], (F, TOK)) for n in range(DOCS)], axis=0
    )
    return state, decay, wide


def row_kernel(scal, got, h0, h1, h2, h3, h4, h5, out, inner, outer):
    z = scal[3]
    total = jnp.zeros((64, TOK), F32)
    before = jnp.zeros((64, TOK), F32)
    decays = jnp.zeros((4, TOK), F32)
    reach = jnp.zeros((64, TOK), F32)
    for peer in range(8):
        state, decay, wide = get_states(got, peer)
        grow = jnp.exp(wide)
        use = peer < z
        before = jnp.where(use, before * grow + state, before)
        reach = jnp.where(use, reach + wide, reach)
        total = total * grow + state
        decays = decays + decay
    inner[...] = before
    outer[...] = jnp.exp(reach)
    put_states(out, total, [decays])
    for peer in range(8):
        out[peer, 144:208] = got[0, 144:208]


def attend_kernel(
    scal, pat, kv_own, q_own, kvq_mate, zps, zpx, zms, zmx, tws, twx, got, inner, outer,
    state0, steps, wft, gain, out, win, qs,
):
    c, q, y, h = scal[0], scal[2], scal[4], scal[5]
    mate = 1 - c
    for n in range(DOCS):
        win[n, 3 + c] = kv_own[n]
        win[n, 3 + mate] = kvq_mate[n, :, : 2 * DH]
        win[n, 1 + c] = zps[n]
        win[n, 1 + mate] = zpx[n]
        win[n, 5 + c] = zms[n]
        win[n, 5 + mate] = zmx[n]
        win[n, 7 * mate] = tws[n]
        win[n, 7 * c] = twx[n]
        qs[n, c] = q_own[n]
        qs[n, mate] = kvq_mate[n, :, 2 * DH :]

    before = jnp.zeros((64, TOK), F32)
    for peer in range(8):
        state, _, wide = get_states(got, peer)
        before = jnp.where(peer < y, before * jnp.exp(wide) + state, before)
    entering = inner[...] + outer[...] * before

    cum = cumulative_of(steps[...])
    cum_t = cum.T
    feature = wft[h]
    row = lax.broadcasted_iota(jnp.int32, (TOK, TOK), 0)
    col = lax.broadcasted_iota(jnp.int32, (TOK, TOK), 1)
    causal = row >= col
    gains = gain[h]
    lane = lax.broadcasted_iota(jnp.int32, (1, 7 * BS), 1)
    scale = DH ** (-0.5)
    for n in range(DOCS):
        carried = entering[F * n : F * n + F]
        glob = [
            jnp.concatenate(
                [got[peer, at : at + 32].astype(F32)[8 * n : 8 * n + 8] for peer in range(8)], axis=0
            ).astype(BF)
            for at in (144, 176)
        ]
        for s in range(2):
            line = cum[2 * n + s : 2 * n + s + 1]
            column = cum_t[:, 2 * n + s : 2 * n + s + 1]
            queries = qs[n, s]
            keys = win[n, 3 + s, :, :DH]
            values = win[n, 3 + s, :, DH:]
            phi_q = softmax0(nt(feature, queries)).astype(BF).astype(F32).T
            phi_k = softmax0(nt(feature, keys)).astype(BF)
            decay = jnp.where(causal, jnp.exp(jnp.minimum(column - line, 0.0)), 0.0)
            mixing = (mm(phi_q.astype(BF), phi_k) * decay).astype(BF)
            linear = mm(mixing, values) + mm(phi_q, carried, HIGH) * jnp.exp(column)
            carried = jnp.exp(line[:, TOK - 1 :]) * carried + state0[n]
            square = jnp.mean(linear * linear, axis=1, keepdims=True)
            normed = linear * lax.rsqrt(square + EPS) * gains
            for half in range(2):
                j = 2 * s + half
                block = 4 * q + j
                picks = [win[n, 3 + (j + d) // 2 if j + d >= 0 else 2, pl.ds(BS * ((j + d) % 2), BS)] for d in (-1, 0, 1)]
                for k in range(R):
                    place = pat[12 * n + 3 * j + k]
                    picks.append(
                        win[n, lax.div(place, 2), pl.ds(pl.multiple_of(BS * lax.rem(place, 2), BS), BS)]
                    )
                near = jnp.concatenate(picks, axis=0)
                all_k = jnp.concatenate([near[:, :DH], glob[0]], axis=0)
                all_v = jnp.concatenate([near[:, DH:], glob[1]], axis=0)
                scores = nt(queries[half * BS : half * BS + BS], all_k) * scale
                bad = (
                    ((lane < BS) & (block < 2))
                    | ((lane >= BS) & (lane < 2 * BS) & (block < 1))
                    | ((lane >= 2 * BS) & (lane < 3 * BS) & (block > 4 * CHIPS - 2))
                )
                scores = jnp.where(bad, MASKED, scores)
                top = jnp.max(scores, axis=1, keepdims=True)
                e = jnp.exp(scores - top)
                soft = (e / jnp.sum(e, axis=1, keepdims=True)).astype(BF)
                sparse = mm(soft, all_v)
                out[2 * n + s, half * BS : half * BS + BS] = (
                    normed[half * BS : half * BS + BS] + sparse
                ).astype(BF)


def call(kernel, outs, scratch, spaces, *args):
    kinds = {"s": pltpu.SMEM, "v": pltpu.VMEM, "a": pl.ANY}
    return pl.pallas_call(
        kernel,
        out_shape=outs,
        in_specs=[pl.BlockSpec(memory_space=kinds[k]) for k in spaces],
        out_specs=[pl.BlockSpec(memory_space=pltpu.VMEM)] * len(outs),
        scratch_shapes=scratch,
        compiler_params=pltpu.CompilerParams(vmem_limit_bytes=28 * 2**20),
    )(*args)


def shape(dims, dtype):
    return jax.ShapeDtypeStruct(dims, dtype)


def pairs(move):
    found = []
    for q in range(CHIPS):
        for c in range(2):
            to, core = move(q, c)
            if 0 <= to < CHIPS:
                found.append((2 * q + c, 2 * to + core))
    return found


XC = [[(2 * q + c) * 4 + x for x in range(4) for c in range(2)] for q in range(CHIPS)]
ZS = [[(8 * y + z) * 2 + c for z in range(8)] for y in range(8) for c in range(2)]
YS = [[(8 * y + z) * 2 + c for y in range(8)] for z in range(8) for c in range(2)]
YC = [[(8 * y + z) * 2 + c for y in range(8) for c in range(2)] for z in range(8)]


def exchange(a, axis, groups):
    return lax.all_to_all(a, axis, 0, 0, tiled=True, axis_index_groups=groups)


def per_device(tokens, w_qkv, w_feature, norm_gain, log_decay, pattern):
    x = lax.axis_index("fsdp")
    s = lax.axis_index("seq")
    c, q = s % 2, s // 2
    z, y = q % 8, q // 8
    h = 2 * x + c
    scal = jnp.stack([c, x, q, z, y, h]).astype(jnp.int32)
    t0 = tokens[0]
    up = [(i, (i + 1) % 4) for i in range(4)]
    down = [(i, (i - 1) % 4) for i in range(4)]
    top, bottom = t0[:64], t0[64:]
    at = lax.ppermute(top, "fsdp", up)
    bb = lax.ppermute(bottom, "fsdp", down)
    ab = lax.ppermute(bottom, "fsdp", up)
    bt = lax.ppermute(top, "fsdp", down)
    dt = lax.ppermute(at, "fsdp", up)
    db = lax.ppermute(bb, "fsdp", down)

    scattered = exchange(top.reshape(16, 64, TOK), "seq", YC)[0]
    three = split3(log_decay[0])
    wanted = jnp.broadcast_to(
        jnp.pad(pattern.reshape(1, 6).astype(BF), ((0, 0), (0, TOK - 6))), (8, TOK)
    )
    small = jnp.stack([*three, wanted] + [jnp.zeros((8, TOK), BF)] * 12, axis=1)
    small = jnp.concatenate([small, jnp.broadcast_to(scattered[None], (8, 64, TOK))], axis=1)
    got0 = exchange(small, ("seq", "fsdp"), XC)
    steps = (got0[:, 0].astype(F32) + got0[:, 1].astype(F32)) + got0[:, 2].astype(F32)
    pat = got0[:, 3, :6].astype(jnp.int32).reshape(48) - (4 * q - 6)
    pat = jnp.clip(pat, 0, 15).astype(jnp.int32)
    ext = got0[:, 16:].reshape(32, D)

    w3 = w_qkv.transpose(1, 0, 2)
    wft = w_feature.transpose(0, 2, 1)
    kv_own, kv_other, kvq_other, q_own, ext_own = call(
        project_kernel,
        [
            shape((DOCS, TOK, 2 * DH), BF),
            shape((DOCS, TOK, 2 * DH), BF),
            shape((DOCS, TOK, 3 * DH), BF),
            shape((DOCS, TOK, DH), BF),
            shape((64, DH), BF),
        ],
        [
            pltpu.VMEM((4 * TOK + 32, D), BF),
            pltpu.VMEM((3, D, 2 * DH), BF),
            pltpu.SemaphoreType.DMA((11,)),
        ],
        "saaaaaaaaa",
        scal, t0, at, ab, bt, bb, dt, db, ext, w3,
    )
    kvq_mate = lax.ppermute(kvq_other, "seq", pairs(lambda q, c: (q, 1 - c)))
    zps = lax.ppermute(kv_own, "seq", pairs(lambda q, c: (q + 1, c)))
    zms = lax.ppermute(kv_own, "seq", pairs(lambda q, c: (q - 1, c)))
    zpx = lax.ppermute(kv_other, "seq", pairs(lambda q, c: (q + 1, 1 - c)))
    zmx = lax.ppermute(kv_other, "seq", pairs(lambda q, c: (q - 1, 1 - c)))
    tws = lax.ppermute(kv_own, "seq", pairs(lambda q, c: (q + 2, 1) if c else (q - 2, 0)))
    twx = lax.ppermute(kv_other, "seq", pairs(lambda q, c: (q + 2, 0) if c else (q - 2, 1)))
    halo = (zps, zpx, zms, zmx, tws, twx)

    send1, state0 = call(
        states_kernel,
        [shape((8, ROWS, TOK), BF), shape((DOCS, F, DH), F32)],
        [],
        "svvvvv",
        scal, kv_own, kvq_mate, ext_own, steps, wft,
    )
    got1 = exchange(send1, "seq", ZS)
    send2, inner, outer = call(
        row_kernel,
        [shape((8, ROWS, TOK), BF), shape((64, TOK), F32), shape((64, TOK), F32)],
        [],
        "sv" + "a" * 6,
        scal, got1, *halo,
    )
    got2 = exchange(send2, "seq", YS)

    [out] = call(
        attend_kernel,
        [shape((8, TOK, DH), BF)],
        [pltpu.VMEM((DOCS, 8, TOK, 2 * DH), BF), pltpu.VMEM((DOCS, 2, TOK, DH), BF)],
        "ss" + "v" * 16,
        scal, pat, kv_own, q_own, kvq_mate, *halo, got2, inner, outer,
        state0, steps, wft, norm_gain.reshape(HALF_HEADS, 1, DH),
    )
    mixed = exchange(out, ("seq", "fsdp"), XC)
    return mixed.transpose(1, 0, 2).reshape(1, TOK, HD)


def solution(mesh):
    placed = (
        P("fsdp", "seq", None),
        P(None, None, "fsdp"),
        P(),
        P(),
        P("fsdp", None, "seq"),
        P("fsdp", "seq", None),
    )
    return jax.shard_map(
        per_device, mesh=mesh, in_specs=placed, out_specs=P("fsdp", "seq", None), check_vma=False
    )
```

```python
import jax
import jax.numpy as jnp
from jax import lax
from jax.experimental import pallas as pl
from jax.experimental.pallas import tpu as pltpu
from jax.sharding import PartitionSpec as P

HALF_HEADS = 8
DH = 128
F = 16
HD = 1024
D = 2048
BS = 64
R = 3
TOK = 128
NB = 2
DOCS = 4
EPS = 1e-06
MASKED = -1e30
CHIPS = 64
ROWS = 208
BF = jnp.bfloat16
F32 = jnp.float32
HIGH = lax.Precision.HIGHEST


def nt(a, b):
    return lax.dot_general(a, b, (((1,), (1,)), ((), ())), preferred_element_type=F32)


def mm(a, b, precision=None):
    return jnp.dot(a, b, preferred_element_type=F32, precision=precision)


def softmax0(logits):
    top = jnp.max(logits, axis=0, keepdims=True)
    e = jnp.exp(logits - top)
    return e / jnp.sum(e, axis=0, keepdims=True)


def split2(a):
    hi = a.astype(BF)
    return hi, (a - hi.astype(F32)).astype(BF)


def split3(a):
    hi, rest = a.astype(BF), None
    rest = a - hi.astype(F32)
    mid = rest.astype(BF)
    return hi, mid, (rest - mid.astype(F32)).astype(BF)


def cumulative_of(steps):
    row = lax.broadcasted_iota(jnp.int32, (TOK, TOK), 0)
    col = lax.broadcasted_iota(jnp.int32, (TOK, TOK), 1)
    return mm(steps, jnp.where(row <= col, 1.0, 0.0).astype(F32), HIGH)


def top_kernel(tokens, out):
    out[...] = tokens[0]


def pack_kernel(pat, rows, steps, out):
    part = rows[...].astype(F32)[:8]
    body = [
        jnp.concatenate([part[:, 256 * k : 256 * k + 128], part[:, 256 * k + 128 : 256 * k + 256]], axis=0).astype(BF)
        for k in range(8)
    ]
    lane = lax.broadcasted_iota(jnp.int32, (1, TOK), 1)
    row = lax.broadcasted_iota(jnp.int32, (16, TOK), 0)
    wanted = jnp.zeros((1, TOK), jnp.int32)
    for i in range(6):
        wanted = jnp.where(lane == i, pat[0, i // 3, i % 3], wanted)
    wanted = wanted.astype(F32)
    hi, mid, lo = (p.astype(F32) for p in split3(steps[0]))
    for peer in range(8):
        for k in range(8):
            out[peer, 16 * k : 16 * k + 16] = body[k]
        here = slice(peer, peer + 1)
        tail = jnp.where(row == 0, hi[here], jnp.where(row == 1, mid[here], jnp.where(row == 2, lo[here], wanted)))
        out[peer, 128:144] = tail.astype(BF)


def project_kernel(
    scal, t0, ta, tb, dt, db, got, w, kv_own, kv_other, kvq_other, q_own, ext_own, steps, rows, wv, sems
):
    c, x = scal[0], scal[1]
    places = [(t0.at[0], 0, 128), (ta, 128, 128), (tb, 384, 128), (dt, 256, 64), (db, 320, 64)]
    copies = [
        pltpu.make_async_copy(ref, rows.at[pl.ds(start, size)], sems.at[i])
        for i, (ref, start, size) in enumerate(places)
    ]
    copies += [pltpu.make_async_copy(w.at[k], wv.at[k], sems.at[5 + k]) for k in range(3)]
    for copy in copies:
        copy.start()
    for pair in range(2):
        two = [got[4 * pair + 2 * i, 0:128].astype(F32) for i in range(2)]
        for l in range(16):
            rows[512 + 16 * pair : 528 + 16 * pair, 128 * l : 128 * l + 128] = jnp.concatenate(
                [p[8 * l : 8 * l + 8] for p in two], axis=0
            ).astype(BF)
    for i in range(8):
        tail = got[i, 128:144].astype(F32)
        steps[i : i + 1] = (tail[0:1] + tail[1:2]) + tail[2:3]
    first = c == 0
    for copy in copies[:5]:
        copy.wait()
    for k in range(3):
        copies[5 + k].wait()
        part = mm(rows[...], wv[k]).astype(BF)
        for r in range(DOCS):
            n = lax.rem(x - r + DOCS, DOCS)
            lo = part[r * TOK : (r + 1) * TOK, :DH]
            hi = part[r * TOK : (r + 1) * TOK, DH:]
            own = jnp.where(first, lo, hi)
            other = jnp.where(first, hi, lo)
            if k == 0:
                q_own[n] = own
                kvq_other[n, :, 2 * DH :] = other
            else:
                here = slice((k - 1) * DH, k * DH)
                kv_own[n, :, here] = own
                kv_other[n, :, here] = other
                kvq_other[n, :, here] = other
        if k:
            ext_own[(k - 1) * 32 : k * 32] = jnp.where(first, part[512:, :DH], part[512:, DH:])


def states_kernel(scal, kv_own, kvq_mate, ext_own, steps, wft, out, state0):
    c, h = scal[0], scal[5]
    first = c == 0
    cum = cumulative_of(steps[...])
    feature = wft[h]
    states, decays = [], []
    for n in range(DOCS):
        own = kv_own[n]
        mate = kvq_mate[n, :, : 2 * DH]
        segs = (jnp.where(first, own, mate), jnp.where(first, mate, own))
        local = []
        for s in range(2):
            phi = softmax0(nt(feature, segs[s][:, :DH])).astype(BF).astype(F32)
            line = cum[2 * n + s : 2 * n + s + 1]
            final = line[:, TOK - 1 :]
            weighted = (jnp.exp(final - line) * phi).astype(BF)
            local.append(mm(weighted, segs[s][:, DH:]))
        last0 = jnp.broadcast_to(cum[2 * n : 2 * n + 1, TOK - 1 :], (1, TOK))
        last1 = jnp.broadcast_to(cum[2 * n + 1 : 2 * n + 2, TOK - 1 :], (1, TOK))
        state0[n] = local[0]
        states.append(jnp.exp(last1) * local[0] + local[1])
        decays.append(last0 + last1)
    put_states(out, jnp.concatenate(states, axis=0), decays)
    for peer in range(8):
        out[peer, 144:208] = ext_own[...]


def put_states(out, state, decays):
    hi, lo = split2(state)
    three = split3(jnp.concatenate(decays, axis=0))
    tail = jnp.concatenate(
        [p.astype(F32) for p in three] + [jnp.zeros((4, TOK), F32)], axis=0
    ).astype(BF)
    for peer in range(8):
        out[peer, 0:64] = hi
        out[peer, 64:128] = lo
        out[peer, 128:144] = tail


def get_states(got, peer):
    state = got[peer, 0:64].astype(F32) + got[peer, 64:128].astype(F32)
    tail = got[peer, 128:144].astype(F32)
    decay = (tail[0:4] + tail[4:8]) + tail[8:12]
    wide = jnp.concatenate(
        [jnp.broadcast_to(decay[n : n + 1], (F, TOK)) for n in range(DOCS)], axis=0
    )
    return state, decay, wide


def row_kernel(scal, got, out, inner, outer):
    z = scal[3]
    total = jnp.zeros((64, TOK), F32)
    before = jnp.zeros((64, TOK), F32)
    decays = jnp.zeros((4, TOK), F32)
    reach = jnp.zeros((64, TOK), F32)
    for peer in range(8):
        state, decay, wide = get_states(got, peer)
        grow = jnp.exp(wide)
        use = peer < z
        before = jnp.where(use, before * grow + state, before)
        reach = jnp.where(use, reach + wide, reach)
        total = total * grow + state
        decays = decays + decay
    inner[...] = before
    outer[...] = jnp.exp(reach)
    put_states(out, total, [decays])
    for peer in range(8):
        out[peer, 144:208] = got[0, 144:208]


def attend_kernel(
    scal, pat, kv_own, q_own, kvq_mate, zps, zpx, zms, zmx, tws, twx, steps, wft,
    sparse, stats, local, phis, queried, win, qs,
):
    c, q, h = scal[0], scal[2], scal[5]
    mate = 1 - c
    for n in range(DOCS):
        win[n, 3 + c] = kv_own[n]
        win[n, 3 + mate] = kvq_mate[n, :, : 2 * DH]
        win[n, 1 + c] = zps[n]
        win[n, 1 + mate] = zpx[n]
        win[n, 5 + c] = zms[n]
        win[n, 5 + mate] = zmx[n]
        win[n, 7 * mate] = tws[n]
        win[n, 7 * c] = twx[n]
        qs[n, c] = q_own[n]
        qs[n, mate] = kvq_mate[n, :, 2 * DH :]

    cum = cumulative_of(steps[...])
    cum_t = cum.T
    feature = wft[h]
    row = lax.broadcasted_iota(jnp.int32, (TOK, TOK), 0)
    col = lax.broadcasted_iota(jnp.int32, (TOK, TOK), 1)
    causal = row >= col
    lane = lax.broadcasted_iota(jnp.int32, (1, 6 * BS), 1)
    first = lax.broadcasted_iota(jnp.int32, (BS, DH), 1) == 0
    scale = DH ** (-0.5)
    for n in range(DOCS):
        for s in range(2):
            line = cum[2 * n + s : 2 * n + s + 1]
            column = cum_t[:, 2 * n + s : 2 * n + s + 1]
            queries = qs[n, s]
            queried[2 * n + s] = queries
            keys = win[n, 3 + s, :, :DH]
            values = win[n, 3 + s, :, DH:]
            phi_q = softmax0(nt(feature, queries)).astype(BF).astype(F32)
            phis[2 * n + s] = phi_q
            phi_k = softmax0(nt(feature, keys)).astype(BF)
            decay = jnp.where(causal, jnp.exp(jnp.minimum(column - line, 0.0)), 0.0)
            mixing = (mm(phi_q.T.astype(BF), phi_k) * decay).astype(BF)
            local[2 * n + s] = mm(mixing, values)
            for half in range(2):
                j = 2 * s + half
                block = 4 * q + j
                picks = [
                    win[n, 3 + (j + d) // 2, pl.ds(BS * ((j + d) % 2), BS)] for d in (-1, 0, 1)
                ]
                for k in range(R):
                    place = pat[12 * n + 3 * j + k]
                    picks.append(
                        win[n, lax.div(place, 2), pl.ds(pl.multiple_of(BS * lax.rem(place, 2), BS), BS)]
                    )
                near = jnp.concatenate(picks, axis=0)
                scores = nt(queries[half * BS : half * BS + BS], near[:, :DH]) * scale
                bad = (
                    ((lane < BS) & (block < 2))
                    | ((lane >= BS) & (lane < 2 * BS) & (block < 1))
                    | ((lane >= 2 * BS) & (lane < 3 * BS) & (block > 4 * CHIPS - 2))
                )
                scores = jnp.where(bad, MASKED, scores)
                top = jnp.max(scores, axis=1, keepdims=True)
                e = jnp.exp(scores - top)
                here = slice(half * BS, half * BS + BS)
                sparse[2 * n + s, here] = mm(e.astype(BF), near[:, DH:])
                stats[2 * n + s, here] = jnp.where(first, top, jnp.sum(e, axis=1, keepdims=True))


def finish_kernel(scal, got, inner, outer, state0, steps, gain, sparse, stats, local, phis, queried, out):
    y, h = scal[4], scal[5]
    before = jnp.zeros((64, TOK), F32)
    for peer in range(8):
        state, _, wide = get_states(got, peer)
        before = jnp.where(peer < y, before * jnp.exp(wide) + state, before)
    entering = inner[...] + outer[...] * before
    cum = cumulative_of(steps[...])
    gains = gain[h]
    scale = DH ** (-0.5)
    for n in range(DOCS):
        carried = entering[F * n : F * n + F]
        glob = [
            jnp.concatenate(
                [got[peer, at : at + 32].astype(F32)[8 * n : 8 * n + 8] for peer in range(8)], axis=0
            ).astype(BF)
            for at in (144, 176)
        ]
        for s in range(2):
            i = 2 * n + s
            scores = nt(queried[i], glob[0]) * scale
            stat = stats[i]
            top, total = stat[:, 0:1], stat[:, 1:2]
            peak = jnp.maximum(top, jnp.max(scores, axis=1, keepdims=True))
            shrink = jnp.exp(top - peak)
            e = jnp.exp(scores - peak)
            total = total * shrink + jnp.sum(e, axis=1, keepdims=True)
            attended = (sparse[i] * shrink + mm(e.astype(BF), glob[1])) / total
            line = cum[i : i + 1]
            weighted = (phis[i] * jnp.exp(line)).T
            linear = local[i] + mm(weighted, carried, HIGH)
            carried = jnp.exp(line[:, TOK - 1 :]) * carried + state0[n]
            square = jnp.mean(linear * linear, axis=1, keepdims=True)
            normed = linear * lax.rsqrt(square + EPS) * gains
            out[i] = (normed + attended).astype(BF)


def call(kernel, outs, scratch, spaces, micros, room, *args):
    kinds = {"s": pltpu.SMEM, "v": pltpu.VMEM, "a": pl.ANY, "h": pltpu.HBM}
    return pl.pallas_call(
        kernel,
        out_shape=outs,
        in_specs=[pl.BlockSpec(memory_space=kinds[k]) for k in spaces],
        out_specs=[pl.BlockSpec(memory_space=pltpu.VMEM)] * len(outs),
        scratch_shapes=scratch,
        compiler_params=pltpu.CompilerParams(vmem_limit_bytes=room * 2**20),
        cost_estimate=pl.CostEstimate(
            flops=int(micros * 1e9), bytes_accessed=int(micros * 3e6), transcendentals=0
        ),
    )(*args)


def shape(dims, dtype):
    return jax.ShapeDtypeStruct(dims, dtype)


def pairs(move):
    found = []
    for q in range(CHIPS):
        for c in range(2):
            to, core = move(q, c)
            if 0 <= to < CHIPS:
                found.append((2 * q + c, 2 * to + core))
    return found


XC = [[(2 * q + c) * 4 + x for x in range(4) for c in range(2)] for q in range(CHIPS)]
ZS = [[(8 * y + z) * 2 + c for z in range(8)] for y in range(8) for c in range(2)]
YS = [[(8 * y + z) * 2 + c for y in range(8)] for z in range(8) for c in range(2)]
YC = [[(8 * y + z) * 2 + c for y in range(8) for c in range(2)] for z in range(8)]


def exchange(a, axis, groups):
    return lax.all_to_all(a, axis, 0, 0, tiled=True, axis_index_groups=groups)


def per_device(tokens, w_qkv, w_feature, norm_gain, log_decay, pattern):
    x = lax.axis_index("fsdp")
    s = lax.axis_index("seq")
    c, q = s % 2, s // 2
    z, y = q % 8, q // 8
    h = 2 * x + c
    scal = jnp.stack([c, x, q, z, y, h]).astype(jnp.int32)
    t0 = tokens[0]
    up = [(i, (i + 1) % 4) for i in range(4)]
    down = [(i, (i - 1) % 4) for i in range(4)]
    ta = lax.ppermute(t0, "fsdp", up)
    tb = lax.ppermute(t0, "fsdp", down)
    dt = lax.ppermute(ta[:64], "fsdp", up)
    db = lax.ppermute(tb[64:], "fsdp", down)

    top = pl.pallas_call(
        top_kernel,
        grid=(1,),
        out_shape=shape((64, D), BF),
        in_specs=[pl.BlockSpec((1, 64, D), lambda i: (0, 0, 0))],
        out_specs=pl.BlockSpec((64, D), lambda i: (0, 0)),
        cost_estimate=pl.CostEstimate(flops=10**10, bytes_accessed=3 * 10**7, transcendentals=0),
    )(tokens)
    scattered = exchange(top, "seq", YS)
    packed = pl.pallas_call(
        pack_kernel,
        grid=(1,),
        out_shape=shape((8, 144, TOK), BF),
        in_specs=[
            pl.BlockSpec(memory_space=pltpu.SMEM),
            pl.BlockSpec((16, D), lambda i: (0, 0)),
            pl.BlockSpec((1, 8, TOK), lambda i: (0, 0, 0)),
        ],
        out_specs=pl.BlockSpec((8, 144, TOK), lambda i: (0, 0, 0)),
        cost_estimate=pl.CostEstimate(flops=10**10, bytes_accessed=3 * 10**7, transcendentals=0),
    )(pattern, scattered, log_decay)
    got0 = exchange(packed, ("seq", "fsdp"), XC)
    pat = got0[:, 131, :6].astype(jnp.int32).reshape(48) - (4 * q - 6)
    pat = jnp.clip(pat, 0, 15).astype(jnp.int32)

    w3 = w_qkv.transpose(1, 0, 2)
    wft = w_feature.transpose(0, 2, 1)
    kv_own, kv_other, kvq_other, q_own, ext_own, steps = call(
        project_kernel,
        [
            shape((DOCS, TOK, 2 * DH), BF),
            shape((DOCS, TOK, 2 * DH), BF),
            shape((DOCS, TOK, 3 * DH), BF),
            shape((DOCS, TOK, DH), BF),
            shape((64, DH), BF),
            shape((8, TOK), F32),
        ],
        [
            pltpu.VMEM((4 * TOK + 32, D), BF),
            pltpu.VMEM((3, D, 2 * DH), BF),
            pltpu.SemaphoreType.DMA((8,)),
        ],
        "shhhhhvh",
        3,
        16,
        scal, tokens, ta, tb, dt, db, got0, w3,
    )
    kvq_mate = lax.ppermute(kvq_other, "seq", pairs(lambda q, c: (q, 1 - c)))
    zps = lax.ppermute(kv_own, "seq", pairs(lambda q, c: (q + 1, c)))
    zms = lax.ppermute(kv_own, "seq", pairs(lambda q, c: (q - 1, c)))
    zpx = lax.ppermute(kv_other, "seq", pairs(lambda q, c: (q + 1, 1 - c)))
    zmx = lax.ppermute(kv_other, "seq", pairs(lambda q, c: (q - 1, 1 - c)))
    tws = lax.ppermute(kv_own, "seq", pairs(lambda q, c: (q + 2, 1) if c else (q - 2, 0)))
    twx = lax.ppermute(kv_other, "seq", pairs(lambda q, c: (q + 2, 0) if c else (q - 2, 1)))
    halo = (zps, zpx, zms, zmx, tws, twx)

    send1, state0 = call(
        states_kernel,
        [shape((8, ROWS, TOK), BF), shape((DOCS, F, DH), F32)],
        [],
        "svvvvv",
        30,
        6,
        scal, kv_own, kvq_mate, ext_own, steps, wft,
    )
    got1 = exchange(send1, "seq", ZS)
    send2, inner, outer = call(
        row_kernel,
        [shape((8, ROWS, TOK), BF), shape((64, TOK), F32), shape((64, TOK), F32)],
        [],
        "sv",
        1,
        4,
        scal, got1,
    )
    got2 = exchange(send2, "seq", YS)
    sparse, stats, local, phis, queried = call(
        attend_kernel,
        [
            shape((8, TOK, DH), F32),
            shape((8, TOK, DH), F32),
            shape((8, TOK, DH), F32),
            shape((8, F, TOK), F32),
            shape((8, TOK, DH), BF),
        ],
        [pltpu.VMEM((DOCS, 8, TOK, 2 * DH), BF), pltpu.VMEM((DOCS, 2, TOK, DH), BF)],
        "ss" + "v" * 11,
        8,
        14,
        scal, pat, kv_own, q_own, kvq_mate, *halo, steps, wft,
    )
    [out] = call(
        finish_kernel,
        [shape((8, TOK, DH), BF)],
        [],
        "s" + "v" * 11,
        2,
        10,
        scal, got2, inner, outer, state0, steps, norm_gain.reshape(HALF_HEADS, 1, DH),
        sparse, stats, local, phis, queried,
    )
    mixed = exchange(out, ("seq", "fsdp"), XC)
    return mixed.transpose(1, 0, 2).reshape(1, TOK, HD)


def solution(mesh):
    placed = (
        P("fsdp", "seq", None),
        P(None, None, "fsdp"),
        P(),
        P(),
        P("fsdp", None, "seq"),
        P("fsdp", "seq", None),
    )
    return jax.shard_map(
        per_device, mesh=mesh, in_specs=placed, out_specs=P("fsdp", "seq", None), check_vma=False
    )
```

```python
import jax
import jax.numpy as jnp
from jax import lax
from jax.experimental import pallas as pl
from jax.experimental.pallas import tpu as pltpu
from jax.sharding import PartitionSpec as P

HALF_HEADS = 8
DH = 128
F = 16
HD = 1024
D = 2048
BS = 64
R = 3
TOK = 128
NB = 2
DOCS = 4
EPS = 1e-06
MASKED = -1e30
CHIPS = 64
ROWS = 208
BF = jnp.bfloat16
F32 = jnp.float32
HIGH = lax.Precision.HIGHEST


def nt(a, b):
    return lax.dot_general(a, b, (((1,), (1,)), ((), ())), preferred_element_type=F32)


def mm(a, b, precision=None):
    return jnp.dot(a, b, preferred_element_type=F32, precision=precision)


def softmax0(logits):
    top = jnp.max(logits, axis=0, keepdims=True)
    e = jnp.exp(logits - top)
    return e / jnp.sum(e, axis=0, keepdims=True)


def split2(a):
    hi = a.astype(BF)
    return hi, (a - hi.astype(F32)).astype(BF)


def split3(a):
    hi, rest = a.astype(BF), None
    rest = a - hi.astype(F32)
    mid = rest.astype(BF)
    return hi, mid, (rest - mid.astype(F32)).astype(BF)


def cumulative_of(steps):
    row = lax.broadcasted_iota(jnp.int32, (TOK, TOK), 0)
    col = lax.broadcasted_iota(jnp.int32, (TOK, TOK), 1)
    return mm(steps, jnp.where(row <= col, 1.0, 0.0).astype(F32), HIGH)


def pack_kernel(pat, steps, packed):
    lane = lax.broadcasted_iota(jnp.int32, (8, TOK), 1)
    row = lax.broadcasted_iota(jnp.int32, (8, TOK), 0)
    wanted = jnp.zeros((8, TOK), jnp.int32)
    for i in range(6):
        wanted = jnp.where(lane == i, pat[0, i // 3, i % 3], wanted)
    wanted = wanted.astype(F32)
    for head in range(8):
        packed[head] = jnp.where(row == 0, steps[0, head : head + 1], wanted)


def halves_kernel(ta, tb, got, da, db):
    da[...] = ta[...]
    db[...] = tb[...]


def early_kernel(t0, got, w, own):
    for k in range(3):
        own[k] = mm(t0[0], w[k]).astype(BF)


def project_kernel(
    scal, early, ta, tb, td1, td2, got, w, kv_own, kv_other, kvq_other, q_own, steps, rows
):
    c, x = scal[0], scal[1]
    rows[0:128] = ta[...]
    rows[128:192] = td1[...]
    rows[192:256] = td2[...]
    rows[256:384] = tb[...]
    for i in range(8):
        steps[i : i + 1] = got[i, 0:1]
    first = c == 0
    for k in range(3):
        part = jnp.concatenate([early[k], mm(rows[...], w[k]).astype(BF)], axis=0)
        for r in range(DOCS):
            n = lax.rem(x - r + DOCS, DOCS)
            lo = part[r * TOK : (r + 1) * TOK, :DH]
            hi = part[r * TOK : (r + 1) * TOK, DH:]
            own = jnp.where(first, lo, hi)
            other = jnp.where(first, hi, lo)
            if k == 0:
                q_own[n] = own
                kvq_other[n, :, 2 * DH :] = other
            else:
                here = slice((k - 1) * DH, k * DH)
                kv_own[n, :, here] = own
                kv_other[n, :, here] = other
                kvq_other[n, :, here] = other


def states_kernel(scal, kv_own, kvq_mate, steps, wft, out, state0):
    c, h = scal[0], scal[5]
    first = c == 0
    cum = cumulative_of(steps[...])
    feature = wft[h]
    states, decays = [], []
    for n in range(DOCS):
        own = kv_own[n]
        mate = kvq_mate[n, :, : 2 * DH]
        segs = (jnp.where(first, own, mate), jnp.where(first, mate, own))
        local = []
        for s in range(2):
            phi = softmax0(nt(feature, segs[s][:, :DH])).astype(BF).astype(F32)
            line = cum[2 * n + s : 2 * n + s + 1]
            final = line[:, TOK - 1 :]
            weighted = (jnp.exp(final - line) * phi).astype(BF)
            local.append(mm(weighted, segs[s][:, DH:]))
        last0 = jnp.broadcast_to(cum[2 * n : 2 * n + 1, TOK - 1 :], (1, TOK))
        last1 = jnp.broadcast_to(cum[2 * n + 1 : 2 * n + 2, TOK - 1 :], (1, TOK))
        state0[n] = local[0]
        states.append(jnp.exp(last1) * local[0] + local[1])
        decays.append(last0 + last1)
        for half in range(2):
            out[2 * n + half, 144:176] = segs[0][32 * half : 32 * half + 32, :DH]
            out[2 * n + half, 176:208] = segs[0][32 * half : 32 * half + 32, DH:]
    put_states(out, jnp.concatenate(states, axis=0), decays)


def put_states(out, state, decays):
    hi, lo = split2(state)
    three = split3(jnp.concatenate(decays, axis=0))
    tail = jnp.concatenate(
        [p.astype(F32) for p in three] + [jnp.zeros((4, TOK), F32)], axis=0
    ).astype(BF)
    for peer in range(8):
        out[peer, 0:64] = hi
        out[peer, 64:128] = lo
        out[peer, 128:144] = tail


def get_states(got, peer):
    state = got[peer, 0:64].astype(F32) + got[peer, 64:128].astype(F32)
    tail = got[peer, 128:144].astype(F32)
    decay = (tail[0:4] + tail[4:8]) + tail[8:12]
    wide = jnp.concatenate(
        [jnp.broadcast_to(decay[n : n + 1], (F, TOK)) for n in range(DOCS)], axis=0
    )
    return state, decay, wide


def row_kernel(scal, got, out, inner, outer):
    z = scal[3]
    total = jnp.zeros((64, TOK), F32)
    before = jnp.zeros((64, TOK), F32)
    decays = jnp.zeros((4, TOK), F32)
    reach = jnp.zeros((64, TOK), F32)
    for peer in range(8):
        state, decay, wide = get_states(got, peer)
        grow = jnp.exp(wide)
        use = peer < z
        before = jnp.where(use, before * grow + state, before)
        reach = jnp.where(use, reach + wide, reach)
        total = total * grow + state
        decays = decays + decay
    inner[...] = before
    outer[...] = jnp.exp(reach)
    put_states(out, total, [decays])
    for peer in range(8):
        out[peer, 144:208] = got[0, 144:208]


def attend_kernel(
    scal, pat, kv_own, q_own, kvq_mate, zps, zpx, zms, zmx, tws, twx, glob, got, inner, outer,
    state0, steps, wft, gain, out, win, qs,
):
    c, q, y, h = scal[0], scal[2], scal[4], scal[5]
    mate = 1 - c
    for n in range(DOCS):
        win[n, 3 + c] = kv_own[n]
        win[n, 3 + mate] = kvq_mate[n, :, : 2 * DH]
        win[n, 1 + c] = zps[n]
        win[n, 1 + mate] = zpx[n]
        win[n, 5 + c] = zms[n]
        win[n, 5 + mate] = zmx[n]
        win[n, 7 * mate] = tws[n]
        win[n, 7 * c] = twx[n]
        qs[n, c] = q_own[n]
        qs[n, mate] = kvq_mate[n, :, 2 * DH :]

    before = jnp.zeros((64, TOK), F32)
    for peer in range(8):
        state, _, wide = get_states(got, peer)
        before = jnp.where(peer < y, before * jnp.exp(wide) + state, before)
    entering = inner[...] + outer[...] * before

    cum = cumulative_of(steps[...])
    cum_t = cum.T
    feature = wft[h]
    row = lax.broadcasted_iota(jnp.int32, (TOK, TOK), 0)
    col = lax.broadcasted_iota(jnp.int32, (TOK, TOK), 1)
    causal = row >= col
    gains = gain[h]
    lane = lax.broadcasted_iota(jnp.int32, (1, 7 * BS), 1)
    scale = DH ** (-0.5)
    for n in range(DOCS):
        carried = entering[F * n : F * n + F]
        for s in range(2):
            line = cum[2 * n + s : 2 * n + s + 1]
            column = cum_t[:, 2 * n + s : 2 * n + s + 1]
            queries = qs[n, s]
            keys = win[n, 3 + s, :, :DH]
            values = win[n, 3 + s, :, DH:]
            phi_q = softmax0(nt(feature, queries)).astype(BF).astype(F32).T
            phi_k = softmax0(nt(feature, keys)).astype(BF)
            decay = jnp.where(causal, jnp.exp(jnp.minimum(column - line, 0.0)), 0.0)
            mixing = (mm(phi_q.astype(BF), phi_k) * decay).astype(BF)
            linear = mm(mixing, values) + mm(phi_q, carried, HIGH) * jnp.exp(column)
            carried = jnp.exp(line[:, TOK - 1 :]) * carried + state0[n]
            square = jnp.mean(linear * linear, axis=1, keepdims=True)
            normed = linear * lax.rsqrt(square + EPS) * gains
            for half in range(2):
                j = 2 * s + half
                block = 4 * q + j
                picks = [win[n, 3 + (j + d) // 2 if j + d >= 0 else 2, pl.ds(BS * ((j + d) % 2), BS)] for d in (-1, 0, 1)]
                for k in range(R):
                    place = pat[12 * n + 3 * j + k]
                    picks.append(
                        win[n, lax.div(place, 2), pl.ds(pl.multiple_of(BS * lax.rem(place, 2), BS), BS)]
                    )
                near = jnp.concatenate(picks, axis=0)
                gk = jnp.concatenate([glob[2 * n, 0:32], glob[2 * n + 1, 0:32]], axis=0)
                gv = jnp.concatenate([glob[2 * n, 32:64], glob[2 * n + 1, 32:64]], axis=0)
                all_k = jnp.concatenate([near[:, :DH], gk], axis=0)
                all_v = jnp.concatenate([near[:, DH:], gv], axis=0)
                scores = nt(queries[half * BS : half * BS + BS], all_k) * scale
                bad = (
                    ((lane < BS) & (block < 2))
                    | ((lane >= BS) & (lane < 2 * BS) & (block < 1))
                    | ((lane >= 2 * BS) & (lane < 3 * BS) & (block > 4 * CHIPS - 2))
                )
                scores = jnp.where(bad, MASKED, scores)
                top = jnp.max(scores, axis=1, keepdims=True)
                e = jnp.exp(scores - top)
                soft = (e / jnp.sum(e, axis=1, keepdims=True)).astype(BF)
                sparse = mm(soft, all_v)
                out[2 * n + s, half * BS : half * BS + BS] = (
                    normed[half * BS : half * BS + BS] + sparse
                ).astype(BF)


def call(kernel, outs, scratch, spaces, micros, room, *args):
    kinds = {"s": pltpu.SMEM, "v": pltpu.VMEM, "a": pl.ANY}
    return pl.pallas_call(
        kernel,
        out_shape=outs,
        in_specs=[pl.BlockSpec(memory_space=kinds[k]) for k in spaces],
        out_specs=[pl.BlockSpec(memory_space=pltpu.VMEM)] * len(outs),
        scratch_shapes=scratch,
        compiler_params=pltpu.CompilerParams(vmem_limit_bytes=room * 2**20),
        cost_estimate=pl.CostEstimate(
            flops=int(micros * 1e9), bytes_accessed=int(micros * 3e6), transcendentals=0
        ),
    )(*args)


def shape(dims, dtype):
    return jax.ShapeDtypeStruct(dims, dtype)


def pairs(move):
    found = []
    for q in range(CHIPS):
        for c in range(2):
            to, core = move(q, c)
            if 0 <= to < CHIPS:
                found.append((2 * q + c, 2 * to + core))
    return found


XC = [[(2 * q + c) * 4 + x for x in range(4) for c in range(2)] for q in range(CHIPS)]
ZS = [[(8 * y + z) * 2 + c for z in range(8)] for y in range(8) for c in range(2)]
YS = [[(8 * y + z) * 2 + c for y in range(8)] for z in range(8) for c in range(2)]


def exchange(a, axis, groups):
    return lax.all_to_all(a, axis, 0, 0, tiled=True, axis_index_groups=groups)


def per_device(tokens, w_qkv, w_feature, norm_gain, log_decay, pattern):
    x = lax.axis_index("fsdp")
    s = lax.axis_index("seq")
    c, q = s % 2, s // 2
    z, y = q % 8, q // 8
    h = 2 * x + c
    scal = jnp.stack([c, x, q, z, y, h]).astype(jnp.int32)
    t0 = tokens[0]
    up = [(i, (i + 1) % 4) for i in range(4)]
    down = [(i, (i - 1) % 4) for i in range(4)]
    ta = lax.ppermute(t0, "fsdp", up)
    tb = lax.ppermute(t0, "fsdp", down)

    w3 = w_qkv.transpose(1, 0, 2)
    wft = w_feature.transpose(0, 2, 1)
    [packed] = call(pack_kernel, [shape((8, 8, TOK), F32)], [], "sv", 1, 4, pattern, log_decay)
    got0 = exchange(packed, ("seq", "fsdp"), XC)
    da, db = pl.pallas_call(
        halves_kernel,
        grid=(1,),
        out_shape=[shape((64, D), BF)] * 2,
        in_specs=[
            pl.BlockSpec((64, D), lambda i: (0, 0)),
            pl.BlockSpec((64, D), lambda i: (1, 0)),
            pl.BlockSpec(memory_space=pl.ANY),
        ],
        out_specs=[pl.BlockSpec((64, D), lambda i: (0, 0))] * 2,
    )(ta, tb, got0)
    td1 = lax.ppermute(da, "fsdp", up)
    td2 = lax.ppermute(db, "fsdp", down)
    [early] = call(
        early_kernel, [shape((3, TOK, 2 * DH), BF)], [], "vav", 6, 12, tokens, got0, w3
    )
    pat = got0[:, 1, :6].astype(jnp.int32).reshape(48) - (4 * q - 6)
    pat = jnp.clip(pat, 0, 15).astype(jnp.int32)

    kv_own, kv_other, kvq_other, q_own, steps = call(
        project_kernel,
        [
            shape((DOCS, TOK, 2 * DH), BF),
            shape((DOCS, TOK, 2 * DH), BF),
            shape((DOCS, TOK, 3 * DH), BF),
            shape((DOCS, TOK, DH), BF),
            shape((8, TOK), F32),
        ],
        [pltpu.VMEM((3 * TOK, D), BF)],
        "s" + "v" * 7,
        3,
        16,
        scal, early, ta, tb, td1, td2, got0, w3,
    )
    kvq_mate = lax.ppermute(kvq_other, "seq", pairs(lambda q, c: (q, 1 - c)))
    zps = lax.ppermute(kv_own, "seq", pairs(lambda q, c: (q + 1, c)))
    zms = lax.ppermute(kv_own, "seq", pairs(lambda q, c: (q - 1, c)))
    zpx = lax.ppermute(kv_other, "seq", pairs(lambda q, c: (q + 1, 1 - c)))
    zmx = lax.ppermute(kv_other, "seq", pairs(lambda q, c: (q - 1, 1 - c)))
    tws = lax.ppermute(kv_own, "seq", pairs(lambda q, c: (q + 2, 1) if c else (q - 2, 0)))
    twx = lax.ppermute(kv_other, "seq", pairs(lambda q, c: (q + 2, 0) if c else (q - 2, 1)))

    send1, state0 = call(
        states_kernel,
        [shape((8, ROWS, TOK), BF), shape((DOCS, F, DH), F32)],
        [],
        "svvvv",
        2,
        6,
        scal, kv_own, kvq_mate, steps, wft,
    )
    got1 = exchange(send1, "seq", ZS)
    send2, inner, outer = call(
        row_kernel,
        [shape((8, ROWS, TOK), BF), shape((64, TOK), F32), shape((64, TOK), F32)],
        [],
        "sv",
        40,
        4,
        scal, got1,
    )
    got2 = exchange(send2, "seq", YS)
    glob = exchange(jnp.broadcast_to(got2[0, 144:208][None], (8, 64, TOK)), "seq", ZS)

    [out] = call(
        attend_kernel,
        [shape((8, TOK, DH), BF)],
        [pltpu.VMEM((DOCS, 8, TOK, 2 * DH), BF), pltpu.VMEM((DOCS, 2, TOK, DH), BF)],
        "ss" + "v" * 17,
        8,
        16,
        scal, pat, kv_own, q_own, kvq_mate, zps, zpx, zms, zmx, tws, twx, glob, got2, inner, outer,
        state0, steps, wft, norm_gain.reshape(HALF_HEADS, 1, DH),
    )
    mixed = exchange(out, ("seq", "fsdp"), XC)
    return mixed.transpose(1, 0, 2).reshape(1, TOK, HD)


def solution(mesh):
    placed = (
        P("fsdp", "seq", None),
        P(None, None, "fsdp"),
        P(),
        P(),
        P("fsdp", None, "seq"),
        P("fsdp", "seq", None),
    )
    return jax.shard_map(
        per_device, mesh=mesh, in_specs=placed, out_specs=P("fsdp", "seq", None), check_vma=False
    )
```

```python
import jax
import jax.numpy as jnp
from jax import lax
from jax.experimental import pallas as pl
from jax.experimental.pallas import tpu as pltpu
from jax.sharding import PartitionSpec as P

HALF_HEADS = 8
DH = 128
F = 16
HD = 1024
D = 2048
BS = 64
R = 3
TOK = 128
NB = 2
DOCS = 4
EPS = 1e-06
MASKED = -1e30
CHIPS = 64
ROWS = 208
BF = jnp.bfloat16
F32 = jnp.float32
HIGH = lax.Precision.HIGHEST


def nt(a, b):
    return lax.dot_general(a, b, (((1,), (1,)), ((), ())), preferred_element_type=F32)


def mm(a, b, precision=None):
    return jnp.dot(a, b, preferred_element_type=F32, precision=precision)


def softmax0(logits):
    top = jnp.max(logits, axis=0, keepdims=True)
    e = jnp.exp(logits - top)
    return e / jnp.sum(e, axis=0, keepdims=True)


def split2(a):
    hi = a.astype(BF)
    return hi, (a - hi.astype(F32)).astype(BF)


def split3(a):
    hi, rest = a.astype(BF), None
    rest = a - hi.astype(F32)
    mid = rest.astype(BF)
    return hi, mid, (rest - mid.astype(F32)).astype(BF)


def cumulative_of(steps):
    row = lax.broadcasted_iota(jnp.int32, (TOK, TOK), 0)
    col = lax.broadcasted_iota(jnp.int32, (TOK, TOK), 1)
    return mm(steps, jnp.where(row <= col, 1.0, 0.0).astype(F32), HIGH)


def pack_kernel(pat, steps, packed):
    lane = lax.broadcasted_iota(jnp.int32, (8, TOK), 1)
    row = lax.broadcasted_iota(jnp.int32, (8, TOK), 0)
    wanted = jnp.zeros((8, TOK), jnp.int32)
    for i in range(6):
        wanted = jnp.where(lane == i, pat[0, i // 3, i % 3], wanted)
    wanted = wanted.astype(F32)
    for head in range(8):
        packed[head] = jnp.where(row == 0, steps[0, head : head + 1], wanted)


def early_kernel(t0, got, w, own):
    for k in range(3):
        own[k] = mm(t0[0], w[k]).astype(BF)


def project_kernel(
    scal, early, ta, tb, td1, td2, got, w, kv_own, kv_other, kvq_other, q_own, steps, rows
):
    c, x = scal[0], scal[1]
    rows[0:128] = ta[...]
    rows[128:192] = td1[...]
    rows[192:256] = td2[...]
    rows[256:384] = tb[...]
    for i in range(8):
        steps[i : i + 1] = got[i, 0:1]
    first = c == 0
    for k in range(3):
        part = jnp.concatenate([early[k], mm(rows[...], w[k]).astype(BF)], axis=0)
        for r in range(DOCS):
            n = lax.rem(x - r + DOCS, DOCS)
            lo = part[r * TOK : (r + 1) * TOK, :DH]
            hi = part[r * TOK : (r + 1) * TOK, DH:]
            own = jnp.where(first, lo, hi)
            other = jnp.where(first, hi, lo)
            if k == 0:
                q_own[n] = own
                kvq_other[n, :, 2 * DH :] = other
            else:
                here = slice((k - 1) * DH, k * DH)
                kv_own[n, :, here] = own
                kv_other[n, :, here] = other
                kvq_other[n, :, here] = other


def states_kernel(scal, kv_own, kvq_mate, steps, wft, out, state0):
    c, h = scal[0], scal[5]
    first = c == 0
    cum = cumulative_of(steps[...])
    feature = wft[h]
    states, decays = [], []
    for n in range(DOCS):
        own = kv_own[n]
        mate = kvq_mate[n, :, : 2 * DH]
        segs = (jnp.where(first, own, mate), jnp.where(first, mate, own))
        local = []
        for s in range(2):
            phi = softmax0(nt(feature, segs[s][:, :DH])).astype(BF).astype(F32)
            line = cum[2 * n + s : 2 * n + s + 1]
            final = line[:, TOK - 1 :]
            weighted = (jnp.exp(final - line) * phi).astype(BF)
            local.append(mm(weighted, segs[s][:, DH:]))
        last0 = jnp.broadcast_to(cum[2 * n : 2 * n + 1, TOK - 1 :], (1, TOK))
        last1 = jnp.broadcast_to(cum[2 * n + 1 : 2 * n + 2, TOK - 1 :], (1, TOK))
        state0[n] = local[0]
        states.append(jnp.exp(last1) * local[0] + local[1])
        decays.append(last0 + last1)
        for half in range(2):
            out[2 * n + half, 144:176] = segs[0][32 * half : 32 * half + 32, :DH]
            out[2 * n + half, 176:208] = segs[0][32 * half : 32 * half + 32, DH:]
    put_states(out, jnp.concatenate(states, axis=0), decays)


def put_states(out, state, decays):
    hi, lo = split2(state)
    three = split3(jnp.concatenate(decays, axis=0))
    tail = jnp.concatenate(
        [p.astype(F32) for p in three] + [jnp.zeros((4, TOK), F32)], axis=0
    ).astype(BF)
    for peer in range(8):
        out[peer, 0:64] = hi
        out[peer, 64:128] = lo
        out[peer, 128:144] = tail


def get_states(got, peer):
    state = got[peer, 0:64].astype(F32) + got[peer, 64:128].astype(F32)
    tail = got[peer, 128:144].astype(F32)
    decay = (tail[0:4] + tail[4:8]) + tail[8:12]
    wide = jnp.concatenate(
        [jnp.broadcast_to(decay[n : n + 1], (F, TOK)) for n in range(DOCS)], axis=0
    )
    return state, decay, wide


def row_kernel(scal, got, out, inner, outer):
    z = scal[3]
    total = jnp.zeros((64, TOK), F32)
    before = jnp.zeros((64, TOK), F32)
    decays = jnp.zeros((4, TOK), F32)
    reach = jnp.zeros((64, TOK), F32)
    for peer in range(8):
        state, decay, wide = get_states(got, peer)
        grow = jnp.exp(wide)
        use = peer < z
        before = jnp.where(use, before * grow + state, before)
        reach = jnp.where(use, reach + wide, reach)
        total = total * grow + state
        decays = decays + decay
    inner[...] = before
    outer[...] = jnp.exp(reach)
    put_states(out, total, [decays])
    for peer in range(8):
        out[peer, 144:208] = got[0, 144:208]


def attend_kernel(
    scal, pat, kv_own, q_own, kvq_mate, zps, zpx, zms, zmx, tws, twx, glob, got, inner, outer,
    state0, steps, wft, gain, out, win, qs,
):
    c, q, y, h = scal[0], scal[2], scal[4], scal[5]
    mate = 1 - c
    for n in range(DOCS):
        win[n, 3 + c] = kv_own[n]
        win[n, 3 + mate] = kvq_mate[n, :, : 2 * DH]
        win[n, 1 + c] = zps[n]
        win[n, 1 + mate] = zpx[n]
        win[n, 5 + c] = zms[n]
        win[n, 5 + mate] = zmx[n]
        win[n, 7 * mate] = tws[n]
        win[n, 7 * c] = twx[n]
        qs[n, c] = q_own[n]
        qs[n, mate] = kvq_mate[n, :, 2 * DH :]

    before = jnp.zeros((64, TOK), F32)
    for peer in range(8):
        state, _, wide = get_states(got, peer)
        before = jnp.where(peer < y, before * jnp.exp(wide) + state, before)
    entering = inner[...] + outer[...] * before

    cum = cumulative_of(steps[...])
    cum_t = cum.T
    feature = wft[h]
    row = lax.broadcasted_iota(jnp.int32, (TOK, TOK), 0)
    col = lax.broadcasted_iota(jnp.int32, (TOK, TOK), 1)
    causal = row >= col
    gains = gain[h]
    lane = lax.broadcasted_iota(jnp.int32, (1, 7 * BS), 1)
    scale = DH ** (-0.5)
    for n in range(DOCS):
        carried = entering[F * n : F * n + F]
        for s in range(2):
            line = cum[2 * n + s : 2 * n + s + 1]
            column = cum_t[:, 2 * n + s : 2 * n + s + 1]
            queries = qs[n, s]
            keys = win[n, 3 + s, :, :DH]
            values = win[n, 3 + s, :, DH:]
            phi_q = softmax0(nt(feature, queries)).astype(BF).astype(F32).T
            phi_k = softmax0(nt(feature, keys)).astype(BF)
            decay = jnp.where(causal, jnp.exp(jnp.minimum(column - line, 0.0)), 0.0)
            mixing = (mm(phi_q.astype(BF), phi_k) * decay).astype(BF)
            linear = mm(mixing, values) + mm(phi_q, carried, HIGH) * jnp.exp(column)
            carried = jnp.exp(line[:, TOK - 1 :]) * carried + state0[n]
            square = jnp.mean(linear * linear, axis=1, keepdims=True)
            normed = linear * lax.rsqrt(square + EPS) * gains
            for half in range(2):
                j = 2 * s + half
                block = 4 * q + j
                picks = [win[n, 3 + (j + d) // 2 if j + d >= 0 else 2, pl.ds(BS * ((j + d) % 2), BS)] for d in (-1, 0, 1)]
                for k in range(R):
                    place = pat[12 * n + 3 * j + k]
                    picks.append(
                        win[n, lax.div(place, 2), pl.ds(pl.multiple_of(BS * lax.rem(place, 2), BS), BS)]
                    )
                near = jnp.concatenate(picks, axis=0)
                gk = jnp.concatenate([glob[2 * n, 0:32], glob[2 * n + 1, 0:32]], axis=0)
                gv = jnp.concatenate([glob[2 * n, 32:64], glob[2 * n + 1, 32:64]], axis=0)
                all_k = jnp.concatenate([near[:, :DH], gk], axis=0)
                all_v = jnp.concatenate([near[:, DH:], gv], axis=0)
                scores = nt(queries[half * BS : half * BS + BS], all_k) * scale
                bad = (
                    ((lane < BS) & (block < 2))
                    | ((lane >= BS) & (lane < 2 * BS) & (block < 1))
                    | ((lane >= 2 * BS) & (lane < 3 * BS) & (block > 4 * CHIPS - 2))
                )
                scores = jnp.where(bad, MASKED, scores)
                top = jnp.max(scores, axis=1, keepdims=True)
                e = jnp.exp(scores - top)
                soft = (e / jnp.sum(e, axis=1, keepdims=True)).astype(BF)
                sparse = mm(soft, all_v)
                out[2 * n + s, half * BS : half * BS + BS] = (
                    normed[half * BS : half * BS + BS] + sparse
                ).astype(BF)


def call(kernel, outs, scratch, spaces, micros, room, *args):
    kinds = {"s": pltpu.SMEM, "v": pltpu.VMEM, "a": pl.ANY}
    return pl.pallas_call(
        kernel,
        out_shape=outs,
        in_specs=[pl.BlockSpec(memory_space=kinds[k]) for k in spaces],
        out_specs=[pl.BlockSpec(memory_space=pltpu.VMEM)] * len(outs),
        scratch_shapes=scratch,
        compiler_params=pltpu.CompilerParams(vmem_limit_bytes=room * 2**20),
        cost_estimate=pl.CostEstimate(
            flops=int(micros * 1e9), bytes_accessed=int(micros * 3e6), transcendentals=0
        ),
    )(*args)


def shape(dims, dtype):
    return jax.ShapeDtypeStruct(dims, dtype)


def pairs(move):
    found = []
    for q in range(CHIPS):
        for c in range(2):
            to, core = move(q, c)
            if 0 <= to < CHIPS:
                found.append((2 * q + c, 2 * to + core))
    return found


XC = [[(2 * q + c) * 4 + x for x in range(4) for c in range(2)] for q in range(CHIPS)]
ZS = [[(8 * y + z) * 2 + c for z in range(8)] for y in range(8) for c in range(2)]
YS = [[(8 * y + z) * 2 + c for y in range(8)] for z in range(8) for c in range(2)]


def exchange(a, axis, groups):
    return lax.all_to_all(a, axis, 0, 0, tiled=True, axis_index_groups=groups)


def per_device(tokens, w_qkv, w_feature, norm_gain, log_decay, pattern):
    x = lax.axis_index("fsdp")
    s = lax.axis_index("seq")
    c, q = s % 2, s // 2
    z, y = q % 8, q // 8
    h = 2 * x + c
    scal = jnp.stack([c, x, q, z, y, h]).astype(jnp.int32)
    t0 = tokens[0]
    up = [(i, (i + 1) % 4) for i in range(4)]
    down = [(i, (i - 1) % 4) for i in range(4)]
    ta = lax.ppermute(t0, "fsdp", up)
    tb = lax.ppermute(t0, "fsdp", down)

    w3 = w_qkv.transpose(1, 0, 2)
    wft = w_feature.transpose(0, 2, 1)
    [packed] = call(pack_kernel, [shape((8, 8, TOK), F32)], [], "sv", 1, 4, pattern, log_decay)
    got0 = exchange(packed, ("seq", "fsdp"), XC)
    td1 = lax.ppermute(ta[:64], "fsdp", up)
    td2 = lax.ppermute(tb[64:], "fsdp", down)
    [early] = call(
        early_kernel, [shape((3, TOK, 2 * DH), BF)], [], "vav", 6, 12, tokens, got0, w3
    )
    pat = got0[:, 1, :6].astype(jnp.int32).reshape(48) - (4 * q - 6)
    pat = jnp.clip(pat, 0, 15).astype(jnp.int32)

    kv_own, kv_other, kvq_other, q_own, steps = call(
        project_kernel,
        [
            shape((DOCS, TOK, 2 * DH), BF),
            shape((DOCS, TOK, 2 * DH), BF),
            shape((DOCS, TOK, 3 * DH), BF),
            shape((DOCS, TOK, DH), BF),
            shape((8, TOK), F32),
        ],
        [pltpu.VMEM((3 * TOK, D), BF)],
        "s" + "v" * 7,
        3,
        16,
        scal, early, ta, tb, td1, td2, got0, w3,
    )
    def behind(a, done):
        return lax.optimization_barrier((a, done))[0]

    kvq_mate = lax.ppermute(kvq_other, "seq", pairs(lambda q, c: (q, 1 - c)))
    tws = lax.ppermute(kv_own, "seq", pairs(lambda q, c: (q + 2, 1) if c else (q - 2, 0)))
    twx = lax.ppermute(kv_other, "seq", pairs(lambda q, c: (q + 2, 0) if c else (q - 2, 1)))
    zps = lax.ppermute(kv_own, "seq", pairs(lambda q, c: (q + 1, c)))
    zpx = lax.ppermute(kv_other, "seq", pairs(lambda q, c: (q + 1, 1 - c)))
    zms = lax.ppermute(behind(kv_own, kvq_mate), "seq", pairs(lambda q, c: (q - 1, c)))
    zmx = lax.ppermute(behind(kv_other, zps), "seq", pairs(lambda q, c: (q - 1, 1 - c)))

    def chain(kv_own, kvq_mate, steps):
        send1, state0 = call(
            states_kernel,
            [shape((8, ROWS, TOK), BF), shape((DOCS, F, DH), F32)],
            [],
            "svvvv",
            2,
            6,
            scal, kv_own, kvq_mate, steps, wft,
        )
        got1 = exchange(send1, "seq", ZS)
        send2, inner, outer = call(
            row_kernel,
            [shape((8, ROWS, TOK), BF), shape((64, TOK), F32), shape((64, TOK), F32)],
            [],
            "sv",
            3,
            4,
            scal, got1,
        )
        got2 = exchange(send2, "seq", YS)
        glob = exchange(jnp.broadcast_to(got2[0, 144:208][None], (8, 64, TOK)), "seq", ZS)
        return got2, glob, inner, outer, state0

    def idle(*_):
        return (
            jnp.zeros((8, ROWS, TOK), BF),
            jnp.zeros((8, 64, TOK), BF),
            jnp.zeros((64, TOK), F32),
            jnp.zeros((64, TOK), F32),
            jnp.zeros((DOCS, F, DH), F32),
        )

    got2, glob, inner, outer, state0 = lax.cond(s < 1000, chain, idle, kv_own, kvq_mate, steps)

    [out] = call(
        attend_kernel,
        [shape((8, TOK, DH), BF)],
        [pltpu.VMEM((DOCS, 8, TOK, 2 * DH), BF), pltpu.VMEM((DOCS, 2, TOK, DH), BF)],
        "ss" + "v" * 17,
        8,
        16,
        scal, pat, kv_own, q_own, kvq_mate, zps, zpx, zms, zmx, tws, twx, glob, got2, inner, outer,
        state0, steps, wft, norm_gain.reshape(HALF_HEADS, 1, DH),
    )
    mixed = exchange(out, ("seq", "fsdp"), XC)
    return mixed.transpose(1, 0, 2).reshape(1, TOK, HD)


def solution(mesh):
    placed = (
        P("fsdp", "seq", None),
        P(None, None, "fsdp"),
        P(),
        P(),
        P("fsdp", None, "seq"),
        P("fsdp", "seq", None),
    )
    return jax.shard_map(
        per_device, mesh=mesh, in_specs=placed, out_specs=P("fsdp", "seq", None), check_vma=False
    )
```

```python
import jax
import jax.numpy as jnp
from jax import lax
from jax.experimental import pallas as pl
from jax.experimental.pallas import tpu as pltpu
from jax.sharding import PartitionSpec as P

HALF_HEADS = 8
DH = 128
F = 16
HD = 1024
D = 2048
BS = 64
R = 3
TOK = 128
NB = 2
DOCS = 4
EPS = 1e-06
MASKED = -1e30
CHIPS = 64
ROWS = 96
BF = jnp.bfloat16
F32 = jnp.float32
HIGH = lax.Precision.HIGHEST


def nt(a, b):
    return lax.dot_general(a, b, (((1,), (1,)), ((), ())), preferred_element_type=F32)


def mm(a, b, precision=None):
    return jnp.dot(a, b, preferred_element_type=F32, precision=precision)


def softmax0(logits):
    top = jnp.max(logits, axis=0, keepdims=True)
    e = jnp.exp(logits - top)
    return e / jnp.sum(e, axis=0, keepdims=True)


def split2(a):
    hi = a.astype(BF)
    return hi, (a - hi.astype(F32)).astype(BF)


def split3(a):
    hi, rest = a.astype(BF), None
    rest = a - hi.astype(F32)
    mid = rest.astype(BF)
    return hi, mid, (rest - mid.astype(F32)).astype(BF)


def cumulative_of(steps):
    row = lax.broadcasted_iota(jnp.int32, (TOK, TOK), 0)
    col = lax.broadcasted_iota(jnp.int32, (TOK, TOK), 1)
    return mm(steps, jnp.where(row <= col, 1.0, 0.0).astype(F32), HIGH)


def pack_kernel(pat, steps, packed):
    lane = lax.broadcasted_iota(jnp.int32, (8, TOK), 1)
    row = lax.broadcasted_iota(jnp.int32, (8, TOK), 0)
    wanted = jnp.zeros((8, TOK), jnp.int32)
    for i in range(6):
        wanted = jnp.where(lane == i, pat[0, i // 3, i % 3], wanted)
    wanted = wanted.astype(F32)
    for head in range(8):
        packed[head] = jnp.where(row == 0, steps[0, head : head + 1], wanted)


def early_kernel(t0, got, w, own):
    for k in range(3):
        own[k] = mm(t0[0], w[k]).astype(BF)


def project_kernel(
    scal, early, ta, tb, td1, td2, got, w, kv_own, kvq_other, q_own, steps, rows
):
    c, x = scal[0], scal[1]
    rows[0:128] = ta[...]
    rows[128:192] = td1[...]
    rows[192:256] = td2[...]
    rows[256:384] = tb[...]
    for i in range(8):
        steps[i : i + 1] = got[i, 0:1]
    first = c == 0
    for k in range(3):
        part = jnp.concatenate([early[k], mm(rows[...], w[k]).astype(BF)], axis=0)
        for r in range(DOCS):
            n = lax.rem(x - r + DOCS, DOCS)
            lo = part[r * TOK : (r + 1) * TOK, :DH]
            hi = part[r * TOK : (r + 1) * TOK, DH:]
            own = jnp.where(first, lo, hi)
            other = jnp.where(first, hi, lo)
            if k == 0:
                q_own[n] = own
                kvq_other[n, :, 2 * DH :] = other
            else:
                here = slice((k - 1) * DH, k * DH)
                kv_own[n, :, here] = own
                kvq_other[n, :, here] = other


def states_kernel(scal, kv_own, q_own, kvq_mate, steps, wft, out, state0, kv2, q2):
    c, h = scal[0], scal[5]
    first = c == 0
    cum = cumulative_of(steps[...])
    feature = wft[h]
    row = lax.broadcasted_iota(jnp.int32, (16, TOK), 0)
    for n in range(DOCS):
        own = kv_own[n]
        mate = kvq_mate[n, :, : 2 * DH]
        segs = (jnp.where(first, own, mate), jnp.where(first, mate, own))
        q2[c, n] = q_own[n]
        q2[1 - c, n] = kvq_mate[n, :, 2 * DH :]
        local = []
        for s in range(2):
            kv2[s, n] = segs[s]
            phi = softmax0(nt(feature, segs[s][:, :DH])).astype(BF).astype(F32)
            line = cum[2 * n + s : 2 * n + s + 1]
            final = line[:, TOK - 1 :]
            weighted = (jnp.exp(final - line) * phi).astype(BF)
            local.append(mm(weighted, segs[s][:, DH:]))
        last0 = jnp.broadcast_to(cum[2 * n : 2 * n + 1, TOK - 1 :], (1, TOK))
        last1 = jnp.broadcast_to(cum[2 * n + 1 : 2 * n + 2, TOK - 1 :], (1, TOK))
        state0[n] = local[0]
        state = jnp.exp(last1) * local[0] + local[1]
        tail = decay_rows(row, last0 + last1)
        for half in range(2):
            p = 2 * n + half
            out[p, 0:16] = state_rows(state[8 * half : 8 * half + 8])
            out[p, 16:32] = tail
            out[p, 32:64] = segs[0][32 * half : 32 * half + 32, :DH]
            out[p, 64:96] = segs[0][32 * half : 32 * half + 32, DH:]


def state_rows(state):
    hi, lo = split2(state)
    return jnp.concatenate([hi.astype(F32), lo.astype(F32)], axis=0).astype(BF)


def decay_rows(row, decay):
    hi, mid, lo = (p.astype(F32) for p in split3(decay))
    return jnp.where(row == 0, hi, jnp.where(row == 1, mid, jnp.where(row == 2, lo, 0.0))).astype(BF)


def read_state(got, peer):
    both = got[peer, 0:16].astype(F32)
    return both[0:8] + both[8:16]


def read_decay(got, peer):
    tail = got[peer, 16:32].astype(F32)
    return (tail[0:1] + tail[1:2]) + tail[2:3]


def row_kernel(got, out, inner, outer):
    row = lax.broadcasted_iota(jnp.int32, (16, TOK), 0)
    total = jnp.zeros((8, TOK), F32)
    reach = jnp.zeros((1, TOK), F32)
    for peer in range(8):
        inner[peer] = total
        outer[peer] = jnp.broadcast_to(jnp.exp(reach), (8, TOK))
        decay = read_decay(got, peer)
        total = total * jnp.exp(decay) + read_state(got, peer)
        reach = reach + decay
    state, tail = state_rows(total), decay_rows(row, reach)
    for peer in range(8):
        out[peer, 0:16] = state
        out[peer, 16:32] = tail
        out[peer, 32:96] = got[0, 32:96]


def back_kernel(scal, got, inner, outer, out):
    y = scal[4]
    before = jnp.zeros((8, TOK), F32)
    for peer in range(8):
        longer = before * jnp.exp(read_decay(got, peer)) + read_state(got, peer)
        before = jnp.where(peer < y, longer, before)
    for peer in range(8):
        out[peer, 0:16] = state_rows(inner[peer] + outer[peer] * before)
        out[peer, 16:80] = got[0, 32:96]


def attend_kernel(scal, pat, kv2, q2, zp, zm, tp, tm, got, state0, steps, wft, gain, out, win):
    q, h = scal[2], scal[5]
    for n in range(DOCS):
        win[n, 0] = tp[n]
        win[n, 7] = tm[n]
        for s in range(2):
            win[n, 1 + s] = zp[s, n]
            win[n, 3 + s] = kv2[s, n]
            win[n, 5 + s] = zm[s, n]

    cum = cumulative_of(steps[...])
    cum_t = cum.T
    feature = wft[h]
    row = lax.broadcasted_iota(jnp.int32, (TOK, TOK), 0)
    col = lax.broadcasted_iota(jnp.int32, (TOK, TOK), 1)
    causal = row >= col
    gains = gain[h]
    lane = lax.broadcasted_iota(jnp.int32, (1, 7 * BS), 1)
    scale = DH ** (-0.5)
    for n in range(DOCS):
        carried = jnp.concatenate([read_state(got, 2 * n), read_state(got, 2 * n + 1)], axis=0)
        gk = jnp.concatenate([got[2 * n, 16:48], got[2 * n + 1, 16:48]], axis=0)
        gv = jnp.concatenate([got[2 * n, 48:80], got[2 * n + 1, 48:80]], axis=0)
        for s in range(2):
            line = cum[2 * n + s : 2 * n + s + 1]
            column = cum_t[:, 2 * n + s : 2 * n + s + 1]
            queries = q2[s, n]
            keys = kv2[s, n, :, :DH]
            values = kv2[s, n, :, DH:]
            phi_q = softmax0(nt(feature, queries)).astype(BF).astype(F32).T
            phi_k = softmax0(nt(feature, keys)).astype(BF)
            decay = jnp.where(causal, jnp.exp(jnp.minimum(column - line, 0.0)), 0.0)
            mixing = (mm(phi_q.astype(BF), phi_k) * decay).astype(BF)
            linear = mm(mixing, values) + mm(phi_q, carried, HIGH) * jnp.exp(column)
            carried = jnp.exp(line[:, TOK - 1 :]) * carried + state0[n]
            square = jnp.mean(linear * linear, axis=1, keepdims=True)
            normed = linear * lax.rsqrt(square + EPS) * gains
            for half in range(2):
                j = 2 * s + half
                block = 4 * q + j
                picks = [win[n, 3 + (j + d) // 2, pl.ds(BS * ((j + d) % 2), BS)] for d in (-1, 0, 1)]
                for k in range(R):
                    place = pat[12 * n + 3 * j + k]
                    picks.append(
                        win[n, lax.div(place, 2), pl.ds(pl.multiple_of(BS * lax.rem(place, 2), BS), BS)]
                    )
                near = jnp.concatenate(picks, axis=0)
                all_k = jnp.concatenate([near[:, :DH], gk], axis=0)
                all_v = jnp.concatenate([near[:, DH:], gv], axis=0)
                scores = nt(queries[half * BS : half * BS + BS], all_k) * scale
                bad = (
                    ((lane < BS) & (block < 2))
                    | ((lane >= BS) & (lane < 2 * BS) & (block < 1))
                    | ((lane >= 2 * BS) & (lane < 3 * BS) & (block > 4 * CHIPS - 2))
                )
                scores = jnp.where(bad, MASKED, scores)
                top = jnp.max(scores, axis=1, keepdims=True)
                e = jnp.exp(scores - top)
                soft = (e / jnp.sum(e, axis=1, keepdims=True)).astype(BF)
                sparse = mm(soft, all_v)
                out[2 * n + s, half * BS : half * BS + BS] = (
                    normed[half * BS : half * BS + BS] + sparse
                ).astype(BF)


def call(kernel, outs, scratch, spaces, micros, room, *args):
    kinds = {"s": pltpu.SMEM, "v": pltpu.VMEM, "a": pl.ANY}
    return pl.pallas_call(
        kernel,
        out_shape=outs,
        in_specs=[pl.BlockSpec(memory_space=kinds[k]) for k in spaces],
        out_specs=[pl.BlockSpec(memory_space=pltpu.VMEM)] * len(outs),
        scratch_shapes=scratch,
        compiler_params=pltpu.CompilerParams(vmem_limit_bytes=room * 2**20),
        cost_estimate=pl.CostEstimate(
            flops=int(micros * 1e9), bytes_accessed=int(micros * 3e6), transcendentals=0
        ),
    )(*args)


def shape(dims, dtype):
    return jax.ShapeDtypeStruct(dims, dtype)


def pairs(move):
    found = []
    for q in range(CHIPS):
        for c in range(2):
            to, core = move(q, c)
            if 0 <= to < CHIPS:
                found.append((2 * q + c, 2 * to + core))
    return found


XC = [[(2 * q + c) * 4 + x for x in range(4) for c in range(2)] for q in range(CHIPS)]
ZS = [[(8 * y + z) * 2 + c for z in range(8)] for y in range(8) for c in range(2)]
YS = [[(8 * y + z) * 2 + c for y in range(8)] for z in range(8) for c in range(2)]


def exchange(a, axis, groups):
    return lax.all_to_all(a, axis, 0, 0, tiled=True, axis_index_groups=groups)


def per_device(tokens, w_qkv, w_feature, norm_gain, log_decay, pattern):
    x = lax.axis_index("fsdp")
    s = lax.axis_index("seq")
    c, q = s % 2, s // 2
    z, y = q % 8, q // 8
    h = 2 * x + c
    scal = jnp.stack([c, x, q, z, y, h]).astype(jnp.int32)
    t0 = tokens[0]
    up = [(i, (i + 1) % 4) for i in range(4)]
    down = [(i, (i - 1) % 4) for i in range(4)]
    ta = lax.ppermute(t0, "fsdp", up)
    tb = lax.ppermute(t0, "fsdp", down)

    w3 = w_qkv.transpose(1, 0, 2)
    wft = w_feature.transpose(0, 2, 1)
    [packed] = call(pack_kernel, [shape((8, 8, TOK), F32)], [], "sv", 1, 4, pattern, log_decay)
    got0 = exchange(packed, ("seq", "fsdp"), XC)
    td1 = lax.ppermute(ta[:64], "fsdp", up)
    td2 = lax.ppermute(tb[64:], "fsdp", down)
    [early] = call(
        early_kernel, [shape((3, TOK, 2 * DH), BF)], [], "vav", 6, 12, tokens, got0, w3
    )
    pat = got0[:, 1, :6].astype(jnp.int32).reshape(48) - (4 * q - 6)
    pat = jnp.clip(pat, 0, 15).astype(jnp.int32)

    kv_own, kvq_other, q_own, steps = call(
        project_kernel,
        [
            shape((DOCS, TOK, 2 * DH), BF),
            shape((DOCS, TOK, 3 * DH), BF),
            shape((DOCS, TOK, DH), BF),
            shape((8, TOK), F32),
        ],
        [pltpu.VMEM((3 * TOK, D), BF)],
        "s" + "v" * 7,
        3,
        16,
        scal, early, ta, tb, td1, td2, got0, w3,
    )
    kvq_mate = lax.ppermute(kvq_other, "seq", pairs(lambda q, c: (q, 1 - c)))
    send1, state0, kv2, q2 = call(
        states_kernel,
        [
            shape((8, ROWS, TOK), BF),
            shape((DOCS, F, DH), F32),
            shape((2, DOCS, TOK, 2 * DH), BF),
            shape((2, DOCS, TOK, DH), BF),
        ],
        [],
        "svvvvv",
        2,
        8,
        scal, kv_own, q_own, kvq_mate, steps, wft,
    )
    got1 = exchange(send1, "seq", ZS)
    zp = lax.ppermute(kv2, "seq", pairs(lambda q, c: (q + 1, c)))
    zm = lax.ppermute(kv2, "seq", pairs(lambda q, c: (q - 1, c)))
    tp = lax.ppermute(kv2[1], "seq", pairs(lambda q, c: (q + 2, c)))
    tm = lax.ppermute(kv2[0], "seq", pairs(lambda q, c: (q - 2, c)))

    def chain(got1):
        send2, inner, outer = call(
            row_kernel,
            [shape((8, ROWS, TOK), BF), shape((8, 8, TOK), F32), shape((8, 8, TOK), F32)],
            [],
            "v",
            1,
            4,
            got1,
        )
        got2 = exchange(send2, "seq", YS)
        [send3] = call(
            back_kernel, [shape((8, 80, TOK), BF)], [], "svvv", 1, 4, scal, got2, inner, outer
        )
        return exchange(send3, "seq", ZS)

    got3 = lax.cond(s < 1000, chain, lambda _: jnp.zeros((8, 80, TOK), BF), got1)

    [out] = call(
        attend_kernel,
        [shape((8, TOK, DH), BF)],
        [pltpu.VMEM((DOCS, 8, TOK, 2 * DH), BF)],
        "ss" + "v" * 11,
        8,
        16,
        scal, pat, kv2, q2, zp, zm, tp, tm, got3, state0, steps, wft,
        norm_gain.reshape(HALF_HEADS, 1, DH),
    )
    mixed = exchange(out, ("seq", "fsdp"), XC)
    return mixed.transpose(1, 0, 2).reshape(1, TOK, HD)


def solution(mesh):
    placed = (
        P("fsdp", "seq", None),
        P(None, None, "fsdp"),
        P(),
        P(),
        P("fsdp", None, "seq"),
        P("fsdp", "seq", None),
    )
    return jax.shard_map(
        per_device, mesh=mesh, in_specs=placed, out_specs=P("fsdp", "seq", None), check_vma=False
    )
```

```python
import jax
import jax.numpy as jnp
from jax import lax
from jax.experimental import pallas as pl
from jax.experimental.pallas import tpu as pltpu
from jax.sharding import PartitionSpec as P

HALF_HEADS = 8
DH = 128
F = 16
HD = 1024
D = 2048
BS = 64
R = 3
TOK = 128
NB = 2
DOCS = 4
EPS = 1e-06
LOG2E = 1.4426950408889634
MASKED = -1e30
CHIPS = 64
ROWS = 96
BF = jnp.bfloat16
F32 = jnp.float32
HIGH = lax.Precision.HIGHEST


def nt(a, b):
    return lax.dot_general(a, b, (((1,), (1,)), ((), ())), preferred_element_type=F32)


def mm(a, b, precision=None):
    return jnp.dot(a, b, preferred_element_type=F32, precision=precision)


def softmax0(logits):
    top = jnp.max(logits, axis=0, keepdims=True)
    e = jnp.exp(logits - top)
    return e / jnp.sum(e, axis=0, keepdims=True)


def split2(a):
    hi = a.astype(BF)
    return hi, (a - hi.astype(F32)).astype(BF)


def split3(a):
    hi, rest = a.astype(BF), None
    rest = a - hi.astype(F32)
    mid = rest.astype(BF)
    return hi, mid, (rest - mid.astype(F32)).astype(BF)


def cumulative_of(steps):
    row = lax.broadcasted_iota(jnp.int32, (TOK, TOK), 0)
    col = lax.broadcasted_iota(jnp.int32, (TOK, TOK), 1)
    return mm(steps, jnp.where(row <= col, 1.0, 0.0).astype(F32), HIGH)


def pack_kernel(pat, steps, packed):
    lane = lax.broadcasted_iota(jnp.int32, (8, TOK), 1)
    row = lax.broadcasted_iota(jnp.int32, (8, TOK), 0)
    wanted = jnp.zeros((8, TOK), jnp.int32)
    for i in range(6):
        wanted = jnp.where(lane == i, pat[0, i // 3, i % 3], wanted)
    wanted = wanted.astype(F32)
    for head in range(8):
        packed[head] = jnp.where(row == 0, steps[0, head : head + 1], wanted)


def early_kernel(t0, got, w, own):
    for k in range(3):
        own[k] = mm(t0[0], w[k]).astype(BF)


def project_kernel(
    scal, early, ta, tb, td1, td2, got, w, kv_own, kvq_other, q_own, steps, rows
):
    c, x = scal[0], scal[1]
    rows[0:128] = ta[...]
    rows[128:192] = td1[...]
    rows[192:256] = td2[...]
    rows[256:384] = tb[...]
    for i in range(8):
        steps[i : i + 1] = got[i, 0:1]
    first = c == 0
    for k in range(3):
        part = jnp.concatenate([early[k], mm(rows[...], w[k]).astype(BF)], axis=0)
        for r in range(DOCS):
            n = lax.rem(x - r + DOCS, DOCS)
            lo = part[r * TOK : (r + 1) * TOK, :DH]
            hi = part[r * TOK : (r + 1) * TOK, DH:]
            own = jnp.where(first, lo, hi)
            other = jnp.where(first, hi, lo)
            if k == 0:
                q_own[n] = own
                kvq_other[n, :, 2 * DH :] = other
            else:
                here = slice((k - 1) * DH, k * DH)
                kv_own[n, :, here] = own
                kvq_other[n, :, here] = other


def states_kernel(scal, kv_own, kvq_mate, steps, wft, out, state0):
    c, h = scal[0], scal[5]
    first = c == 0
    cum = cumulative_of(steps[...])
    feature = wft[h]
    row = lax.broadcasted_iota(jnp.int32, (16, TOK), 0)
    for n in range(DOCS):
        own = kv_own[n]
        mate = kvq_mate[n, :, : 2 * DH]
        segs = (jnp.where(first, own, mate), jnp.where(first, mate, own))
        local = []
        for s in range(2):
            phi = softmax0(nt(feature, segs[s][:, :DH])).astype(BF).astype(F32)
            line = cum[2 * n + s : 2 * n + s + 1]
            final = line[:, TOK - 1 :]
            weighted = (jnp.exp(final - line) * phi).astype(BF)
            local.append(mm(weighted, segs[s][:, DH:]))
        last0 = jnp.broadcast_to(cum[2 * n : 2 * n + 1, TOK - 1 :], (1, TOK))
        last1 = jnp.broadcast_to(cum[2 * n + 1 : 2 * n + 2, TOK - 1 :], (1, TOK))
        state0[n] = local[0]
        state = jnp.exp(last1) * local[0] + local[1]
        tail = decay_rows(row, last0 + last1)
        for half in range(2):
            p = 2 * n + half
            out[p, 0:16] = state_rows(state[8 * half : 8 * half + 8])
            out[p, 16:32] = tail
            out[p, 32:64] = segs[0][32 * half : 32 * half + 32, :DH]
            out[p, 64:96] = segs[0][32 * half : 32 * half + 32, DH:]


def join_kernel(scal, kv_own, q_own, kvq_mate, send1, kv2, q2, seg0, seg1):
    c = scal[0]
    first = c == 0
    for n in range(DOCS):
        own = kv_own[n]
        mate = kvq_mate[n, :, : 2 * DH]
        early, later = jnp.where(first, own, mate), jnp.where(first, mate, own)
        kv2[0, n] = early
        seg0[n] = early
        kv2[1, n] = later
        seg1[n] = later
        q2[c, n] = q_own[n]
        q2[1 - c, n] = kvq_mate[n, :, 2 * DH :]


def state_rows(state):
    hi, lo = split2(state)
    return jnp.concatenate([hi.astype(F32), lo.astype(F32)], axis=0).astype(BF)


def decay_rows(row, decay):
    hi, mid, lo = (p.astype(F32) for p in split3(decay))
    return jnp.where(row == 0, hi, jnp.where(row == 1, mid, jnp.where(row == 2, lo, 0.0))).astype(BF)


def read_state(got, peer):
    both = got[peer, 0:16].astype(F32)
    return both[0:8] + both[8:16]


def read_decay(got, peer):
    tail = got[peer, 16:32].astype(F32)
    return (tail[0:1] + tail[1:2]) + tail[2:3]


def row_kernel(got, out, inner, outer):
    row = lax.broadcasted_iota(jnp.int32, (16, TOK), 0)
    total = jnp.zeros((8, TOK), F32)
    reach = jnp.zeros((1, TOK), F32)
    for peer in range(8):
        inner[peer] = total
        outer[peer] = jnp.broadcast_to(jnp.exp(reach), (8, TOK))
        decay = read_decay(got, peer)
        total = total * jnp.exp(decay) + read_state(got, peer)
        reach = reach + decay
    state, tail = state_rows(total), decay_rows(row, reach)
    for peer in range(8):
        out[peer, 0:16] = state
        out[peer, 16:32] = tail
        out[peer, 32:96] = got[0, 32:96]


def back_kernel(scal, got, inner, outer, out):
    y = scal[4]
    before = jnp.zeros((8, TOK), F32)
    for peer in range(8):
        longer = before * jnp.exp(read_decay(got, peer)) + read_state(got, peer)
        before = jnp.where(peer < y, longer, before)
    for peer in range(8):
        out[peer, 0:16] = state_rows(inner[peer] + outer[peer] * before)
        out[peer, 16:80] = got[0, 32:96]


def attend_kernel(scal, pat, kv2, q2, zp, zm, tp, tm, got, state0, steps, wft, gain, out, win):
    q, h = scal[2], scal[5]
    for n in range(DOCS):
        win[n, 0] = tp[n]
        win[n, 7] = tm[n]
        for s in range(2):
            win[n, 1 + s] = zp[s, n]
            win[n, 3 + s] = kv2[s, n]
            win[n, 5 + s] = zm[s, n]

    cum = cumulative_of(steps[...])
    cum_t = cum.T
    feature = wft[h]
    row = lax.broadcasted_iota(jnp.int32, (TOK, TOK), 0)
    col = lax.broadcasted_iota(jnp.int32, (TOK, TOK), 1)
    causal = row >= col
    gains = gain[h]
    lane = lax.broadcasted_iota(jnp.int32, (1, 7 * BS), 1)
    scale = DH ** (-0.5) * LOG2E
    for n in range(DOCS):
        carried = jnp.concatenate([read_state(got, 2 * n), read_state(got, 2 * n + 1)], axis=0)
        gk = jnp.concatenate([got[2 * n, 16:48], got[2 * n + 1, 16:48]], axis=0)
        gv = jnp.concatenate([got[2 * n, 48:80], got[2 * n + 1, 48:80]], axis=0)
        for s in range(2):
            line = cum[2 * n + s : 2 * n + s + 1]
            column = cum_t[:, 2 * n + s : 2 * n + s + 1]
            queries = q2[s, n]
            keys = kv2[s, n, :, :DH]
            values = kv2[s, n, :, DH:]
            phi_q = softmax0(nt(feature, queries)).astype(BF).astype(F32).T
            phi_k = softmax0(nt(feature, keys)).astype(BF)
            decay = jnp.where(causal, jnp.exp(jnp.minimum(column - line, 0.0)), 0.0)
            mixing = (mm(phi_q.astype(BF), phi_k) * decay).astype(BF)
            linear = mm(mixing, values) + mm(phi_q, carried, HIGH) * jnp.exp(column)
            carried = jnp.exp(line[:, TOK - 1 :]) * carried + state0[n]
            square = jnp.mean(linear * linear, axis=1, keepdims=True)
            normed = linear * lax.rsqrt(square + EPS) * gains
            for half in range(2):
                j = 2 * s + half
                block = 4 * q + j
                picks = [win[n, 3 + (j + d) // 2, pl.ds(BS * ((j + d) % 2), BS)] for d in (-1, 0, 1)]
                for k in range(R):
                    place = pat[12 * n + 3 * j + k]
                    picks.append(
                        win[n, lax.div(place, 2), pl.ds(pl.multiple_of(BS * lax.rem(place, 2), BS), BS)]
                    )
                near = jnp.concatenate(picks, axis=0)
                all_k = jnp.concatenate([near[:, :DH], gk], axis=0)
                all_v = jnp.concatenate([near[:, DH:], gv], axis=0)
                scores = nt(queries[half * BS : half * BS + BS], all_k)
                bad = (
                    ((lane < BS) & (block < 2))
                    | ((lane >= BS) & (lane < 2 * BS) & (block < 1))
                    | ((lane >= 2 * BS) & (lane < 3 * BS) & (block > 4 * CHIPS - 2))
                )
                scores = jnp.where(bad, MASKED, scores)
                top = jnp.max(scores, axis=1, keepdims=True)
                e = jnp.exp2((scores - top) * scale)
                share = 1.0 / jnp.sum(e, axis=1, keepdims=True)
                sparse = mm(e.astype(BF), all_v) * share
                out[2 * n + s, half * BS : half * BS + BS] = (
                    normed[half * BS : half * BS + BS] + sparse
                ).astype(BF)


def call(kernel, outs, scratch, spaces, micros, room, *args):
    kinds = {"s": pltpu.SMEM, "v": pltpu.VMEM, "a": pl.ANY}
    return pl.pallas_call(
        kernel,
        out_shape=outs,
        in_specs=[pl.BlockSpec(memory_space=kinds[k]) for k in spaces],
        out_specs=[pl.BlockSpec(memory_space=pltpu.VMEM)] * len(outs),
        scratch_shapes=scratch,
        compiler_params=pltpu.CompilerParams(vmem_limit_bytes=room * 2**20),
        cost_estimate=pl.CostEstimate(
            flops=int(micros * 1e9), bytes_accessed=int(micros * 3e6), transcendentals=0
        ),
    )(*args)


def shape(dims, dtype):
    return jax.ShapeDtypeStruct(dims, dtype)


def pairs(move):
    found = []
    for q in range(CHIPS):
        for c in range(2):
            to, core = move(q, c)
            if 0 <= to < CHIPS:
                found.append((2 * q + c, 2 * to + core))
    return found


XC = [[(2 * q + c) * 4 + x for x in range(4) for c in range(2)] for q in range(CHIPS)]
ZS = [[(8 * y + z) * 2 + c for z in range(8)] for y in range(8) for c in range(2)]
YS = [[(8 * y + z) * 2 + c for y in range(8)] for z in range(8) for c in range(2)]


def exchange(a, axis, groups):
    return lax.all_to_all(a, axis, 0, 0, tiled=True, axis_index_groups=groups)


def per_device(tokens, w_qkv, w_feature, norm_gain, log_decay, pattern):
    x = lax.axis_index("fsdp")
    s = lax.axis_index("seq")
    c, q = s % 2, s // 2
    z, y = q % 8, q // 8
    h = 2 * x + c
    scal = jnp.stack([c, x, q, z, y, h]).astype(jnp.int32)
    t0 = tokens[0]
    up = [(i, (i + 1) % 4) for i in range(4)]
    down = [(i, (i - 1) % 4) for i in range(4)]
    ta = lax.ppermute(t0, "fsdp", up)
    tb = lax.ppermute(t0, "fsdp", down)

    w3 = w_qkv.transpose(1, 0, 2)
    wft = w_feature.transpose(0, 2, 1)
    [packed] = call(pack_kernel, [shape((8, 8, TOK), F32)], [], "sv", 1, 4, pattern, log_decay)
    got0 = exchange(packed, ("seq", "fsdp"), XC)
    td1 = lax.ppermute(ta[:64], "fsdp", up)
    td2 = lax.ppermute(tb[64:], "fsdp", down)
    [early] = call(
        early_kernel, [shape((3, TOK, 2 * DH), BF)], [], "vav", 6, 12, tokens, got0, w3
    )
    pat = got0[:, 1, :6].astype(jnp.int32).reshape(48) - (4 * q - 6)
    pat = jnp.clip(pat, 0, 15).astype(jnp.int32)

    kv_own, kvq_other, q_own, steps = call(
        project_kernel,
        [
            shape((DOCS, TOK, 2 * DH), BF),
            shape((DOCS, TOK, 3 * DH), BF),
            shape((DOCS, TOK, DH), BF),
            shape((8, TOK), F32),
        ],
        [pltpu.VMEM((3 * TOK, D), BF)],
        "s" + "v" * 7,
        3,
        16,
        scal, early, ta, tb, td1, td2, got0, w3,
    )
    kvq_mate = lax.ppermute(kvq_other, "seq", pairs(lambda q, c: (q, 1 - c)))
    send1, state0 = call(
        states_kernel,
        [shape((8, ROWS, TOK), BF), shape((DOCS, F, DH), F32)],
        [],
        "svvvv",
        2,
        8,
        scal, kv_own, kvq_mate, steps, wft,
    )
    got1 = exchange(send1, "seq", ZS)
    kv2, q2, seg0, seg1 = call(
        join_kernel,
        [
            shape((2, DOCS, TOK, 2 * DH), BF),
            shape((2, DOCS, TOK, DH), BF),
            shape((DOCS, TOK, 2 * DH), BF),
            shape((DOCS, TOK, 2 * DH), BF),
        ],
        [],
        "svvva",
        1,
        8,
        scal, kv_own, q_own, kvq_mate, send1,
    )
    kv2, seg0, seg1, got1 = lax.optimization_barrier((kv2, seg0, seg1, got1))
    zp = lax.ppermute(kv2, "seq", pairs(lambda q, c: (q + 1, c)))
    zm = lax.ppermute(kv2, "seq", pairs(lambda q, c: (q - 1, c)))
    tp = lax.ppermute(seg1, "seq", pairs(lambda q, c: (q + 2, c)))
    tm = lax.ppermute(seg0, "seq", pairs(lambda q, c: (q - 2, c)))

    def chain(got1):
        send2, inner, outer = call(
            row_kernel,
            [shape((8, ROWS, TOK), BF), shape((8, 8, TOK), F32), shape((8, 8, TOK), F32)],
            [],
            "v",
            1,
            4,
            got1,
        )
        got2 = exchange(send2, "seq", YS)
        [send3] = call(
            back_kernel, [shape((8, 80, TOK), BF)], [], "svvv", 1, 4, scal, got2, inner, outer
        )
        return exchange(send3, "seq", ZS)

    got3 = lax.cond(s < 1000, chain, lambda _: jnp.zeros((8, 80, TOK), BF), got1)

    [out] = call(
        attend_kernel,
        [shape((8, TOK, DH), BF)],
        [pltpu.VMEM((DOCS, 8, TOK, 2 * DH), BF)],
        "ss" + "v" * 11,
        8,
        16,
        scal, pat, kv2, q2, zp, zm, tp, tm, got3, state0, steps, wft,
        norm_gain.reshape(HALF_HEADS, 1, DH),
    )
    mixed = exchange(out, ("seq", "fsdp"), XC)
    return mixed.transpose(1, 0, 2).reshape(1, TOK, HD)


def solution(mesh):
    placed = (
        P("fsdp", "seq", None),
        P(None, None, "fsdp"),
        P(),
        P(),
        P("fsdp", None, "seq"),
        P("fsdp", "seq", None),
    )
    return jax.shard_map(
        per_device, mesh=mesh, in_specs=placed, out_specs=P("fsdp", "seq", None), check_vma=False
    )
```

```python
import jax
import jax.numpy as jnp
from jax import lax
from jax.experimental import pallas as pl
from jax.experimental.pallas import tpu as pltpu
from jax.sharding import PartitionSpec as P

HALF_HEADS = 8
DH = 128
F = 16
HD = 1024
D = 2048
BS = 64
R = 3
TOK = 128
NB = 2
DOCS = 4
EPS = 1e-06
LOG2E = 1.4426950408889634
MASKED = -1e30
CHIPS = 64
ROWS = 96
BF = jnp.bfloat16
F32 = jnp.float32
HIGH = lax.Precision.HIGHEST


def nt(a, b):
    return lax.dot_general(a, b, (((1,), (1,)), ((), ())), preferred_element_type=F32)


def mm(a, b, precision=None):
    return jnp.dot(a, b, preferred_element_type=F32, precision=precision)


def softmax0(logits):
    top = jnp.max(logits, axis=0, keepdims=True)
    e = jnp.exp(logits - top)
    return e / jnp.sum(e, axis=0, keepdims=True)


def split2(a):
    hi = a.astype(BF)
    return hi, (a - hi.astype(F32)).astype(BF)


def split3(a):
    hi, rest = a.astype(BF), None
    rest = a - hi.astype(F32)
    mid = rest.astype(BF)
    return hi, mid, (rest - mid.astype(F32)).astype(BF)


def cumulative_of(steps):
    row = lax.broadcasted_iota(jnp.int32, (TOK, TOK), 0)
    col = lax.broadcasted_iota(jnp.int32, (TOK, TOK), 1)
    return mm(steps, jnp.where(row <= col, 1.0, 0.0).astype(F32), HIGH)


def pack_kernel(pat, steps, packed):
    lane = lax.broadcasted_iota(jnp.int32, (8, TOK), 1)
    row = lax.broadcasted_iota(jnp.int32, (8, TOK), 0)
    wanted = jnp.zeros((8, TOK), jnp.int32)
    for i in range(6):
        wanted = jnp.where(lane == i, pat[0, i // 3, i % 3], wanted)
    wanted = wanted.astype(F32)
    for head in range(8):
        packed[head] = jnp.where(row == 0, steps[0, head : head + 1], wanted)


def early_kernel(t0, got, w, own):
    for k in range(3):
        own[k] = mm(t0[0], w[k]).astype(BF)


def project_kernel(
    scal, early, ta, tb, td1, td2, got, w, kv_own, kvq_other, q_own, steps, rows
):
    c, x = scal[0], scal[1]
    rows[0:128] = ta[...]
    rows[128:192] = td1[...]
    rows[192:256] = td2[...]
    rows[256:384] = tb[...]
    for i in range(8):
        steps[i : i + 1] = got[i, 0:1]
    first = c == 0
    for k in range(3):
        part = jnp.concatenate([early[k], mm(rows[...], w[k]).astype(BF)], axis=0)
        for r in range(DOCS):
            n = lax.rem(x - r + DOCS, DOCS)
            lo = part[r * TOK : (r + 1) * TOK, :DH]
            hi = part[r * TOK : (r + 1) * TOK, DH:]
            own = jnp.where(first, lo, hi)
            other = jnp.where(first, hi, lo)
            if k == 0:
                q_own[n] = own
                kvq_other[n, :, 2 * DH :] = other
            else:
                here = slice((k - 1) * DH, k * DH)
                kv_own[n, :, here] = own
                kvq_other[n, :, here] = other


def states_kernel(scal, kv_own, kvq_mate, steps, wft, out, state0):
    c, h = scal[0], scal[5]
    first = c == 0
    cum = cumulative_of(steps[...])
    feature = wft[h]
    row = lax.broadcasted_iota(jnp.int32, (16, TOK), 0)
    for n in range(DOCS):
        own = kv_own[n]
        mate = kvq_mate[n, :, : 2 * DH]
        segs = (jnp.where(first, own, mate), jnp.where(first, mate, own))
        local = []
        for s in range(2):
            phi = softmax0(nt(feature, segs[s][:, :DH])).astype(BF).astype(F32)
            line = cum[2 * n + s : 2 * n + s + 1]
            final = line[:, TOK - 1 :]
            weighted = (jnp.exp(final - line) * phi).astype(BF)
            local.append(mm(weighted, segs[s][:, DH:]))
        last0 = jnp.broadcast_to(cum[2 * n : 2 * n + 1, TOK - 1 :], (1, TOK))
        last1 = jnp.broadcast_to(cum[2 * n + 1 : 2 * n + 2, TOK - 1 :], (1, TOK))
        state0[n] = local[0]
        state = jnp.exp(last1) * local[0] + local[1]
        tail = decay_rows(row, last0 + last1)
        for half in range(2):
            p = 2 * n + half
            out[p, 0:16] = state_rows(state[8 * half : 8 * half + 8])
            out[p, 16:32] = tail
            out[p, 32:64] = segs[0][32 * half : 32 * half + 32, :DH]
            out[p, 64:96] = segs[0][32 * half : 32 * half + 32, DH:]


def join_kernel(scal, kv_own, q_own, kvq_mate, kv2, q2):
    c = scal[0]
    first = c == 0
    for n in range(DOCS):
        own = kv_own[n]
        mate = kvq_mate[n, :, : 2 * DH]
        early, later = jnp.where(first, own, mate), jnp.where(first, mate, own)
        kv2[0, n] = early
        kv2[1, n] = later
        q2[c, n] = q_own[n]
        q2[1 - c, n] = kvq_mate[n, :, 2 * DH :]


def state_rows(state):
    hi, lo = split2(state)
    return jnp.concatenate([hi.astype(F32), lo.astype(F32)], axis=0).astype(BF)


def decay_rows(row, decay):
    hi, mid, lo = (p.astype(F32) for p in split3(decay))
    return jnp.where(row == 0, hi, jnp.where(row == 1, mid, jnp.where(row == 2, lo, 0.0))).astype(BF)


def read_state(got, peer):
    both = got[peer, 0:16].astype(F32)
    return both[0:8] + both[8:16]


def read_decay(got, peer):
    tail = got[peer, 16:32].astype(F32)
    return (tail[0:1] + tail[1:2]) + tail[2:3]


def row_kernel(got, out, inner, outer):
    row = lax.broadcasted_iota(jnp.int32, (16, TOK), 0)
    total = jnp.zeros((8, TOK), F32)
    reach = jnp.zeros((1, TOK), F32)
    for peer in range(8):
        inner[peer] = total
        outer[peer] = jnp.broadcast_to(jnp.exp(reach), (8, TOK))
        decay = read_decay(got, peer)
        total = total * jnp.exp(decay) + read_state(got, peer)
        reach = reach + decay
    state, tail = state_rows(total), decay_rows(row, reach)
    for peer in range(8):
        out[peer, 0:16] = state
        out[peer, 16:32] = tail
        out[peer, 32:96] = got[0, 32:96]


def back_kernel(scal, got, inner, outer, out):
    y = scal[4]
    before = jnp.zeros((8, TOK), F32)
    for peer in range(8):
        longer = before * jnp.exp(read_decay(got, peer)) + read_state(got, peer)
        before = jnp.where(peer < y, longer, before)
    for peer in range(8):
        out[peer, 0:16] = state_rows(inner[peer] + outer[peer] * before)
        out[peer, 16:80] = got[0, 32:96]


def attend_kernel(scal, pat, kv2, q2, zp, zm, tp, tm, got, state0, steps, wft, gain, out, win):
    q, h = scal[2], scal[5]
    for n in range(DOCS):
        win[n, 0] = tp[n]
        win[n, 7] = tm[n]
        for s in range(2):
            win[n, 1 + s] = zp[s, n]
            win[n, 3 + s] = kv2[s, n]
            win[n, 5 + s] = zm[s, n]

    cum = cumulative_of(steps[...])
    cum_t = cum.T
    feature = wft[h]
    row = lax.broadcasted_iota(jnp.int32, (TOK, TOK), 0)
    col = lax.broadcasted_iota(jnp.int32, (TOK, TOK), 1)
    causal = row >= col
    gains = gain[h]
    lane = lax.broadcasted_iota(jnp.int32, (1, 7 * BS), 1)
    scale = DH ** (-0.5) * LOG2E
    for n in range(DOCS):
        carried = jnp.concatenate([read_state(got, 2 * n), read_state(got, 2 * n + 1)], axis=0)
        gk = jnp.concatenate([got[2 * n, 16:48], got[2 * n + 1, 16:48]], axis=0)
        gv = jnp.concatenate([got[2 * n, 48:80], got[2 * n + 1, 48:80]], axis=0)
        for s in range(2):
            line = cum[2 * n + s : 2 * n + s + 1]
            column = cum_t[:, 2 * n + s : 2 * n + s + 1]
            queries = q2[s, n]
            keys = kv2[s, n, :, :DH]
            values = kv2[s, n, :, DH:]
            phi_q = softmax0(nt(feature, queries)).astype(BF).astype(F32).T
            phi_k = softmax0(nt(feature, keys)).astype(BF)
            decay = jnp.where(causal, jnp.exp(jnp.minimum(column - line, 0.0)), 0.0)
            mixing = (mm(phi_q.astype(BF), phi_k) * decay).astype(BF)
            linear = mm(mixing, values) + mm(phi_q, carried, HIGH) * jnp.exp(column)
            carried = jnp.exp(line[:, TOK - 1 :]) * carried + state0[n]
            square = jnp.mean(linear * linear, axis=1, keepdims=True)
            normed = linear * lax.rsqrt(square + EPS) * gains
            for half in range(2):
                j = 2 * s + half
                block = 4 * q + j
                picks = [win[n, 3 + (j + d) // 2, pl.ds(BS * ((j + d) % 2), BS)] for d in (-1, 0, 1)]
                for k in range(R):
                    place = pat[12 * n + 3 * j + k]
                    picks.append(
                        win[n, lax.div(place, 2), pl.ds(pl.multiple_of(BS * lax.rem(place, 2), BS), BS)]
                    )
                near = jnp.concatenate(picks, axis=0)
                all_k = jnp.concatenate([near[:, :DH], gk], axis=0)
                all_v = jnp.concatenate([near[:, DH:], gv], axis=0)
                scores = nt(queries[half * BS : half * BS + BS], all_k)
                bad = (
                    ((lane < BS) & (block < 2))
                    | ((lane >= BS) & (lane < 2 * BS) & (block < 1))
                    | ((lane >= 2 * BS) & (lane < 3 * BS) & (block > 4 * CHIPS - 2))
                )
                scores = jnp.where(bad, MASKED, scores)
                top = jnp.max(scores, axis=1, keepdims=True)
                e = jnp.exp2((scores - top) * scale)
                share = 1.0 / jnp.sum(e, axis=1, keepdims=True)
                sparse = mm(e.astype(BF), all_v) * share
                out[2 * n + s, half * BS : half * BS + BS] = (
                    normed[half * BS : half * BS + BS] + sparse
                ).astype(BF)


def call(kernel, outs, scratch, spaces, micros, room, *args):
    kinds = {"s": pltpu.SMEM, "v": pltpu.VMEM, "a": pl.ANY}
    return pl.pallas_call(
        kernel,
        out_shape=outs,
        in_specs=[pl.BlockSpec(memory_space=kinds[k]) for k in spaces],
        out_specs=[pl.BlockSpec(memory_space=pltpu.VMEM)] * len(outs),
        scratch_shapes=scratch,
        compiler_params=pltpu.CompilerParams(vmem_limit_bytes=room * 2**20),
        cost_estimate=pl.CostEstimate(
            flops=int(micros * 1e9), bytes_accessed=int(micros * 3e6), transcendentals=0
        ),
    )(*args)


def shape(dims, dtype):
    return jax.ShapeDtypeStruct(dims, dtype)


def pairs(move):
    found = []
    for q in range(CHIPS):
        for c in range(2):
            to, core = move(q, c)
            if 0 <= to < CHIPS:
                found.append((2 * q + c, 2 * to + core))
    return found


XC = [[(2 * q + c) * 4 + x for x in range(4) for c in range(2)] for q in range(CHIPS)]
ZS = [[(8 * y + z) * 2 + c for z in range(8)] for y in range(8) for c in range(2)]
YS = [[(8 * y + z) * 2 + c for y in range(8)] for z in range(8) for c in range(2)]


def exchange(a, axis, groups):
    return lax.all_to_all(a, axis, 0, 0, tiled=True, axis_index_groups=groups)


def per_device(tokens, w_qkv, w_feature, norm_gain, log_decay, pattern):
    x = lax.axis_index("fsdp")
    s = lax.axis_index("seq")
    c, q = s % 2, s // 2
    z, y = q % 8, q // 8
    h = 2 * x + c
    scal = jnp.stack([c, x, q, z, y, h]).astype(jnp.int32)
    t0 = tokens[0]
    up = [(i, (i + 1) % 4) for i in range(4)]
    down = [(i, (i - 1) % 4) for i in range(4)]
    ta = lax.ppermute(t0, "fsdp", up)
    tb = lax.ppermute(t0, "fsdp", down)

    w3 = w_qkv.transpose(1, 0, 2)
    wft = w_feature.transpose(0, 2, 1)
    [packed] = call(pack_kernel, [shape((8, 8, TOK), F32)], [], "sv", 1, 4, pattern, log_decay)
    got0 = exchange(packed, ("seq", "fsdp"), XC)
    td1 = lax.ppermute(ta[:64], "fsdp", up)
    td2 = lax.ppermute(tb[64:], "fsdp", down)
    [early] = call(
        early_kernel, [shape((3, TOK, 2 * DH), BF)], [], "vav", 6, 12, tokens, got0, w3
    )
    pat = got0[:, 1, :6].astype(jnp.int32).reshape(48) - (4 * q - 6)
    pat = jnp.clip(pat, 0, 15).astype(jnp.int32)

    kv_own, kvq_other, q_own, steps = call(
        project_kernel,
        [
            shape((DOCS, TOK, 2 * DH), BF),
            shape((DOCS, TOK, 3 * DH), BF),
            shape((DOCS, TOK, DH), BF),
            shape((8, TOK), F32),
        ],
        [pltpu.VMEM((3 * TOK, D), BF)],
        "s" + "v" * 7,
        3,
        16,
        scal, early, ta, tb, td1, td2, got0, w3,
    )
    kvq_mate = lax.ppermute(kvq_other, "seq", pairs(lambda q, c: (q, 1 - c)))
    kv2, q2 = call(
        join_kernel,
        [shape((2, DOCS, TOK, 2 * DH), BF), shape((2, DOCS, TOK, DH), BF)],
        [],
        "svvv",
        20,
        8,
        scal, kv_own, q_own, kvq_mate,
    )
    zp = lax.ppermute(kv2, "seq", pairs(lambda q, c: (q + 1, c)))
    zm = lax.ppermute(kv2, "seq", pairs(lambda q, c: (q - 1, c)))
    send1, state0 = call(
        states_kernel,
        [shape((8, ROWS, TOK), BF), shape((DOCS, F, DH), F32)],
        [],
        "svvvv",
        2,
        8,
        scal, kv_own, kvq_mate, steps, wft,
    )
    got1 = exchange(send1, "seq", ZS)
    near_p, near_m, got1 = lax.optimization_barrier((zp[1], zm[0], got1))
    tp = lax.ppermute(near_p, "seq", pairs(lambda q, c: (q + 1, c)))
    tm = lax.ppermute(near_m, "seq", pairs(lambda q, c: (q - 1, c)))

    def chain(got1):
        send2, inner, outer = call(
            row_kernel,
            [shape((8, ROWS, TOK), BF), shape((8, 8, TOK), F32), shape((8, 8, TOK), F32)],
            [],
            "v",
            1,
            4,
            got1,
        )
        got2 = exchange(send2, "seq", YS)
        [send3] = call(
            back_kernel, [shape((8, 80, TOK), BF)], [], "svvv", 1, 4, scal, got2, inner, outer
        )
        return exchange(send3, "seq", ZS)

    got3 = lax.cond(s < 1000, chain, lambda _: jnp.zeros((8, 80, TOK), BF), got1)

    [out] = call(
        attend_kernel,
        [shape((8, TOK, DH), BF)],
        [pltpu.VMEM((DOCS, 8, TOK, 2 * DH), BF)],
        "ss" + "v" * 11,
        8,
        16,
        scal, pat, kv2, q2, zp, zm, tp, tm, got3, state0, steps, wft,
        norm_gain.reshape(HALF_HEADS, 1, DH),
    )
    mixed = exchange(out, ("seq", "fsdp"), XC)
    return mixed.transpose(1, 0, 2).reshape(1, TOK, HD)


def solution(mesh):
    placed = (
        P("fsdp", "seq", None),
        P(None, None, "fsdp"),
        P(),
        P(),
        P("fsdp", None, "seq"),
        P("fsdp", "seq", None),
    )
    return jax.shard_map(
        per_device, mesh=mesh, in_specs=placed, out_specs=P("fsdp", "seq", None), check_vma=False
    )
```

```python
import jax
import jax.numpy as jnp
from jax import lax
from jax.experimental import pallas as pl
from jax.experimental.pallas import tpu as pltpu
from jax.sharding import PartitionSpec as P

HALF_HEADS = 8
DH = 128
F = 16
HD = 1024
D = 2048
BS = 64
R = 3
TOK = 128
NB = 2
DOCS = 4
EPS = 1e-06
LOG2E = 1.4426950408889634
MASKED = -1e30
CHIPS = 64
ROWS = 96
BF = jnp.bfloat16
F32 = jnp.float32
HIGH = lax.Precision.HIGHEST


def nt(a, b):
    return lax.dot_general(a, b, (((1,), (1,)), ((), ())), preferred_element_type=F32)


def mm(a, b, precision=None):
    return jnp.dot(a, b, preferred_element_type=F32, precision=precision)


def softmax0(logits):
    top = jnp.max(logits, axis=0, keepdims=True)
    e = jnp.exp(logits - top)
    return e / jnp.sum(e, axis=0, keepdims=True)


def split2(a):
    hi = a.astype(BF)
    return hi, (a - hi.astype(F32)).astype(BF)


def split3(a):
    hi, rest = a.astype(BF), None
    rest = a - hi.astype(F32)
    mid = rest.astype(BF)
    return hi, mid, (rest - mid.astype(F32)).astype(BF)


def cumulative_of(steps):
    row = lax.broadcasted_iota(jnp.int32, (TOK, TOK), 0)
    col = lax.broadcasted_iota(jnp.int32, (TOK, TOK), 1)
    return mm(steps, jnp.where(row <= col, 1.0, 0.0).astype(F32), HIGH)


def pack_kernel(pat, steps, packed):
    lane = lax.broadcasted_iota(jnp.int32, (8, TOK), 1)
    row = lax.broadcasted_iota(jnp.int32, (8, TOK), 0)
    wanted = jnp.zeros((8, TOK), jnp.int32)
    for i in range(6):
        wanted = jnp.where(lane == i, pat[0, i // 3, i % 3], wanted)
    wanted = wanted.astype(F32)
    for head in range(8):
        packed[head] = jnp.where(row == 0, steps[0, head : head + 1], wanted)


def early_kernel(t0, got, w, own):
    for k in range(3):
        own[k] = mm(t0[0], w[k]).astype(BF)


def project_kernel(
    scal, early, ta, tb, td1, td2, got, w, kv_own, kvq_other, q_own, steps, rows
):
    c, x = scal[0], scal[1]
    rows[0:128] = ta[...]
    rows[128:192] = td1[...]
    rows[192:256] = td2[...]
    rows[256:384] = tb[...]
    for i in range(8):
        steps[i : i + 1] = got[i, 0:1]
    first = c == 0
    for k in range(3):
        part = jnp.concatenate([early[k], mm(rows[...], w[k]).astype(BF)], axis=0)
        for r in range(DOCS):
            n = lax.rem(x - r + DOCS, DOCS)
            lo = part[r * TOK : (r + 1) * TOK, :DH]
            hi = part[r * TOK : (r + 1) * TOK, DH:]
            own = jnp.where(first, lo, hi)
            other = jnp.where(first, hi, lo)
            if k == 0:
                q_own[n] = own
                kvq_other[n, :, 2 * DH :] = other
            else:
                here = slice((k - 1) * DH, k * DH)
                kv_own[n, :, here] = own
                kvq_other[n, :, here] = other


def states_kernel(scal, kv_own, kvq_mate, steps, wft, out, state0):
    c, h = scal[0], scal[5]
    first = c == 0
    cum = cumulative_of(steps[...])
    feature = wft[h]
    row = lax.broadcasted_iota(jnp.int32, (16, TOK), 0)
    segs = []
    for n in range(DOCS):
        own = kv_own[n]
        mate = kvq_mate[n, :, : 2 * DH]
        segs += [jnp.where(first, own, mate), jnp.where(first, mate, own)]
    keys = jnp.concatenate([a[:, :DH] for a in segs], axis=0)
    phi = softmax0(nt(feature, keys)).astype(BF).astype(F32)
    lines = [cum[i : i + 1] for i in range(8)]
    finals = [a[:, TOK - 1 :] for a in lines]
    weighted = [
        (jnp.exp(finals[i] - lines[i]) * phi[:, TOK * i : TOK * i + TOK]).astype(BF) for i in range(8)
    ]
    local = [mm(weighted[i], segs[i][:, DH:]) for i in range(8)]
    for n in range(DOCS):
        last0 = jnp.broadcast_to(finals[2 * n], (1, TOK))
        last1 = jnp.broadcast_to(finals[2 * n + 1], (1, TOK))
        state0[n] = local[2 * n]
        state = jnp.exp(last1) * local[2 * n] + local[2 * n + 1]
        tail = decay_rows(row, last0 + last1)
        for half in range(2):
            p = 2 * n + half
            out[p, 0:16] = state_rows(state[8 * half : 8 * half + 8])
            out[p, 16:32] = tail
            out[p, 32:64] = segs[2 * n][32 * half : 32 * half + 32, :DH]
            out[p, 64:96] = segs[2 * n][32 * half : 32 * half + 32, DH:]


def join_kernel(scal, kv_own, q_own, kvq_mate, kv2, q2):
    c = scal[0]
    first = c == 0
    for n in range(DOCS):
        own = kv_own[n]
        mate = kvq_mate[n, :, : 2 * DH]
        early, later = jnp.where(first, own, mate), jnp.where(first, mate, own)
        kv2[0, n] = early
        kv2[1, n] = later
        q2[c, n] = q_own[n]
        q2[1 - c, n] = kvq_mate[n, :, 2 * DH :]


def state_rows(state):
    hi, lo = split2(state)
    return jnp.concatenate([hi.astype(F32), lo.astype(F32)], axis=0).astype(BF)


def decay_rows(row, decay):
    hi, mid, lo = (p.astype(F32) for p in split3(decay))
    return jnp.where(row == 0, hi, jnp.where(row == 1, mid, jnp.where(row == 2, lo, 0.0))).astype(BF)


def read_state(got, peer):
    both = got[peer, 0:16].astype(F32)
    return both[0:8] + both[8:16]


def read_decay(got, peer):
    tail = got[peer, 16:32].astype(F32)
    return (tail[0:1] + tail[1:2]) + tail[2:3]


def row_kernel(got, out, inner, outer):
    row = lax.broadcasted_iota(jnp.int32, (16, TOK), 0)
    total = jnp.zeros((8, TOK), F32)
    reach = jnp.zeros((1, TOK), F32)
    for peer in range(8):
        inner[peer] = total
        outer[peer] = jnp.broadcast_to(jnp.exp(reach), (8, TOK))
        decay = read_decay(got, peer)
        total = total * jnp.exp(decay) + read_state(got, peer)
        reach = reach + decay
    state, tail = state_rows(total), decay_rows(row, reach)
    for peer in range(8):
        out[peer, 0:16] = state
        out[peer, 16:32] = tail
        out[peer, 32:96] = got[0, 32:96]


def back_kernel(scal, got, inner, outer, out):
    y = scal[4]
    before = jnp.zeros((8, TOK), F32)
    for peer in range(8):
        longer = before * jnp.exp(read_decay(got, peer)) + read_state(got, peer)
        before = jnp.where(peer < y, longer, before)
    for peer in range(8):
        out[peer, 0:16] = state_rows(inner[peer] + outer[peer] * before)
        out[peer, 16:80] = got[0, 32:96]


def attend_kernel(scal, pat, kv2, q2, zp, zm, tp, tm, got, state0, steps, wft, gain, out, win):
    q, h = scal[2], scal[5]
    for n in range(DOCS):
        win[n, 0] = tp[n]
        win[n, 7] = tm[n]
        for s in range(2):
            win[n, 1 + s] = zp[s, n]
            win[n, 3 + s] = kv2[s, n]
            win[n, 5 + s] = zm[s, n]

    cum = cumulative_of(steps[...])
    cum_t = cum.T
    feature = wft[h]
    row = lax.broadcasted_iota(jnp.int32, (TOK, TOK), 0)
    col = lax.broadcasted_iota(jnp.int32, (TOK, TOK), 1)
    causal = row >= col
    gains = gain[h]
    units = [(n, s) for n in range(DOCS) for s in range(2)]
    lines = [cum[i : i + 1] for i in range(8)]
    columns = [cum_t[:, i : i + 1] for i in range(8)]
    both = jnp.concatenate([q2[s, n] for n, s in units] + [kv2[s, n, :, :DH] for n, s in units], axis=0)
    phi = softmax0(nt(feature, both)).astype(BF)
    phi_q = phi[:, : 8 * TOK].astype(F32).T
    phi_b = phi_q.astype(BF)
    alike = [mm(phi_b[TOK * i : TOK * i + TOK], phi[:, TOK * (8 + i) : TOK * (9 + i)]) for i in range(8)]
    entering = []
    for n in range(DOCS):
        carried = jnp.concatenate([read_state(got, 2 * n), read_state(got, 2 * n + 1)], axis=0)
        entering += [carried, jnp.exp(lines[2 * n][:, TOK - 1 :]) * carried + state0[n]]
    brought = [mm(phi_q[TOK * i : TOK * i + TOK], entering[i], HIGH) for i in range(8)]
    decays = [jnp.where(causal, jnp.exp(jnp.minimum(columns[i] - lines[i], 0.0)), 0.0) for i in range(8)]
    mixing = [(alike[i] * decays[i]).astype(BF) for i in range(8)]
    inside = [mm(mixing[i], kv2[s, n, :, DH:]) for i, (n, s) in enumerate(units)]
    linear = [inside[i] + brought[i] * jnp.exp(columns[i]) for i in range(8)]
    roots = [lax.rsqrt(jnp.mean(a * a, axis=1, keepdims=True) + EPS) for a in linear]
    normed = [linear[i] * roots[i] * gains for i in range(8)]

    lane = lax.broadcasted_iota(jnp.int32, (1, 7 * BS), 1)
    scale = DH ** (-0.5) * LOG2E
    for n in range(DOCS):
        gk = jnp.concatenate([got[2 * n, 16:48], got[2 * n + 1, 16:48]], axis=0)
        gv = jnp.concatenate([got[2 * n, 48:80], got[2 * n + 1, 48:80]], axis=0)
        picked = []
        for j in range(4):
            picks = [win[n, 3 + (j + d) // 2, pl.ds(BS * ((j + d) % 2), BS)] for d in (-1, 0, 1)]
            for k in range(R):
                place = pat[12 * n + 3 * j + k]
                picks.append(
                    win[n, lax.div(place, 2), pl.ds(pl.multiple_of(BS * lax.rem(place, 2), BS), BS)]
                )
            picked.append(jnp.concatenate(picks, axis=0))
        scores = [
            nt(q2[j // 2, n, BS * (j % 2) : BS * (j % 2) + BS], jnp.concatenate([picked[j][:, :DH], gk], axis=0))
            for j in range(4)
        ]
        for j in range(4):
            block = 4 * q + j
            bad = (
                ((lane < BS) & (block < 2))
                | ((lane >= BS) & (lane < 2 * BS) & (block < 1))
                | ((lane >= 2 * BS) & (lane < 3 * BS) & (block > 4 * CHIPS - 2))
            )
            scores[j] = jnp.where(bad, MASKED, scores[j])
        tops = [jnp.max(a, axis=1, keepdims=True) for a in scores]
        es = [jnp.exp2((a - top) * scale) for a, top in zip(scores, tops)]
        shares = [1.0 / jnp.sum(e, axis=1, keepdims=True) for e in es]
        sparse = [
            mm(es[j].astype(BF), jnp.concatenate([picked[j][:, DH:], gv], axis=0)) * shares[j] for j in range(4)
        ]
        for j in range(4):
            half = slice(BS * (j % 2), BS * (j % 2) + BS)
            out[2 * n + j // 2, half] = (normed[2 * n + j // 2][half] + sparse[j]).astype(BF)


def call(kernel, outs, scratch, spaces, micros, room, *args):
    kinds = {"s": pltpu.SMEM, "v": pltpu.VMEM, "a": pl.ANY}
    return pl.pallas_call(
        kernel,
        out_shape=outs,
        in_specs=[pl.BlockSpec(memory_space=kinds[k]) for k in spaces],
        out_specs=[pl.BlockSpec(memory_space=pltpu.VMEM)] * len(outs),
        scratch_shapes=scratch,
        compiler_params=pltpu.CompilerParams(vmem_limit_bytes=room * 2**20),
        cost_estimate=pl.CostEstimate(
            flops=int(micros * 1e9), bytes_accessed=int(micros * 3e6), transcendentals=0
        ),
    )(*args)


def shape(dims, dtype):
    return jax.ShapeDtypeStruct(dims, dtype)


def pairs(move):
    found = []
    for q in range(CHIPS):
        for c in range(2):
            to, core = move(q, c)
            if 0 <= to < CHIPS:
                found.append((2 * q + c, 2 * to + core))
    return found


XC = [[(2 * q + c) * 4 + x for x in range(4) for c in range(2)] for q in range(CHIPS)]
ZS = [[(8 * y + z) * 2 + c for z in range(8)] for y in range(8) for c in range(2)]
YS = [[(8 * y + z) * 2 + c for y in range(8)] for z in range(8) for c in range(2)]


def exchange(a, axis, groups):
    return lax.all_to_all(a, axis, 0, 0, tiled=True, axis_index_groups=groups)


def per_device(tokens, w_qkv, w_feature, norm_gain, log_decay, pattern):
    x = lax.axis_index("fsdp")
    s = lax.axis_index("seq")
    c, q = s % 2, s // 2
    z, y = q % 8, q // 8
    h = 2 * x + c
    scal = jnp.stack([c, x, q, z, y, h]).astype(jnp.int32)
    t0 = tokens[0]
    up = [(i, (i + 1) % 4) for i in range(4)]
    down = [(i, (i - 1) % 4) for i in range(4)]
    ta = lax.ppermute(t0, "fsdp", up)
    tb = lax.ppermute(t0, "fsdp", down)

    w3 = w_qkv.transpose(1, 0, 2)
    wft = w_feature.transpose(0, 2, 1)
    [packed] = call(pack_kernel, [shape((8, 8, TOK), F32)], [], "sv", 1, 4, pattern, log_decay)
    got0 = exchange(packed, ("seq", "fsdp"), XC)
    td1 = lax.ppermute(ta[:64], "fsdp", up)
    td2 = lax.ppermute(tb[64:], "fsdp", down)
    [early] = call(
        early_kernel, [shape((3, TOK, 2 * DH), BF)], [], "vav", 6, 12, tokens, got0, w3
    )
    pat = got0[:, 1, :6].astype(jnp.int32).reshape(48) - (4 * q - 6)
    pat = jnp.clip(pat, 0, 15).astype(jnp.int32)

    kv_own, kvq_other, q_own, steps = call(
        project_kernel,
        [
            shape((DOCS, TOK, 2 * DH), BF),
            shape((DOCS, TOK, 3 * DH), BF),
            shape((DOCS, TOK, DH), BF),
            shape((8, TOK), F32),
        ],
        [pltpu.VMEM((3 * TOK, D), BF)],
        "s" + "v" * 7,
        3,
        16,
        scal, early, ta, tb, td1, td2, got0, w3,
    )
    kvq_mate = lax.ppermute(kvq_other, "seq", pairs(lambda q, c: (q, 1 - c)))
    kv2, q2 = call(
        join_kernel,
        [shape((2, DOCS, TOK, 2 * DH), BF), shape((2, DOCS, TOK, DH), BF)],
        [],
        "svvv",
        20,
        8,
        scal, kv_own, q_own, kvq_mate,
    )
    zp = lax.ppermute(kv2, "seq", pairs(lambda q, c: (q + 1, c)))
    zm = lax.ppermute(kv2, "seq", pairs(lambda q, c: (q - 1, c)))
    send1, state0 = call(
        states_kernel,
        [shape((8, ROWS, TOK), BF), shape((DOCS, F, DH), F32)],
        [],
        "svvvv",
        2,
        8,
        scal, kv_own, kvq_mate, steps, wft,
    )
    got1 = exchange(send1, "seq", ZS)
    def chain(got1, near_p, near_m):
        send2, inner, outer = call(
            row_kernel,
            [shape((8, ROWS, TOK), BF), shape((8, 8, TOK), F32), shape((8, 8, TOK), F32)],
            [],
            "v",
            1,
            4,
            got1,
        )
        got2 = exchange(send2, "seq", YS)
        [send3] = call(
            back_kernel, [shape((8, 80, TOK), BF)], [], "svvv", 1, 4, scal, got2, inner, outer
        )
        tp = lax.ppermute(near_p, "seq", pairs(lambda q, c: (q + 1, c)))
        tm = lax.ppermute(near_m, "seq", pairs(lambda q, c: (q - 1, c)))
        return exchange(send3, "seq", ZS), tp, tm

    got3, tp, tm = chain(got1, zp[1], zm[0])

    [out] = call(
        attend_kernel,
        [shape((8, TOK, DH), BF)],
        [pltpu.VMEM((DOCS, 8, TOK, 2 * DH), BF)],
        "ss" + "v" * 11,
        8,
        16,
        scal, pat, kv2, q2, zp, zm, tp, tm, got3, state0, steps, wft,
        norm_gain.reshape(HALF_HEADS, 1, DH),
    )
    mixed = exchange(out, ("seq", "fsdp"), XC)
    return mixed.transpose(1, 0, 2).reshape(1, TOK, HD)


def solution(mesh):
    placed = (
        P("fsdp", "seq", None),
        P(None, None, "fsdp"),
        P(),
        P(),
        P("fsdp", None, "seq"),
        P("fsdp", "seq", None),
    )
    return jax.shard_map(
        per_device, mesh=mesh, in_specs=placed, out_specs=P("fsdp", "seq", None), check_vma=False
    )
```

```python
import jax
import jax.numpy as jnp
from jax import lax
from jax.experimental import pallas as pl
from jax.experimental.pallas import tpu as pltpu
from jax.sharding import PartitionSpec as P

HALF_HEADS = 8
DH = 128
F = 16
HD = 1024
D = 2048
BS = 64
R = 3
TOK = 128
NB = 2
DOCS = 4
EPS = 1e-06
LOG2E = 1.4426950408889634
MASKED = -1e30
CHIPS = 64
ROWS = 96
BF = jnp.bfloat16
F32 = jnp.float32
HIGH = lax.Precision.HIGHEST


def nt(a, b):
    return lax.dot_general(a, b, (((1,), (1,)), ((), ())), preferred_element_type=F32)


def mm(a, b, precision=None):
    return jnp.dot(a, b, preferred_element_type=F32, precision=precision)


def softmax0(logits):
    top = jnp.max(logits, axis=0, keepdims=True)
    e = jnp.exp(logits - top)
    return e / jnp.sum(e, axis=0, keepdims=True)


def split2(a):
    hi = a.astype(BF)
    return hi, (a - hi.astype(F32)).astype(BF)


def split3(a):
    hi, rest = a.astype(BF), None
    rest = a - hi.astype(F32)
    mid = rest.astype(BF)
    return hi, mid, (rest - mid.astype(F32)).astype(BF)


def cumulative_of(steps):
    row = lax.broadcasted_iota(jnp.int32, (TOK, TOK), 0)
    col = lax.broadcasted_iota(jnp.int32, (TOK, TOK), 1)
    return mm(steps, jnp.where(row <= col, 1.0, 0.0).astype(F32), HIGH)


def split_kernel(pat, tokens, steps, upper, lower):
    for b in range(4):
        upper[64 * b : 64 * b + 64] = tokens[0, :64, 512 * b : 512 * b + 512]
    lower[...] = tokens[0, 64:]
    lane = lax.broadcasted_iota(jnp.int32, (8, TOK), 1)
    wanted = jnp.zeros((8, TOK), jnp.int32)
    for i in range(6):
        wanted = jnp.where(lane == i, pat[0, i // 3, i % 3], wanted)
    parts = [p.astype(F32) for p in split3(steps[0])] + [wanted.astype(F32)]
    body = jnp.concatenate(parts, axis=1)
    upper[256:272] = jnp.concatenate([body, jnp.zeros((8, 4 * TOK), F32)], axis=0).astype(BF)


def early_kernel(t0, w, ta1, own):
    for k in range(3):
        own[k] = mm(t0[0], w[k]).astype(BF)


def project_kernel(
    scal, early, upper, ta1, td1, tb1, ta2, td2, tb2, w,
    kv_own, kvq_other, q_own, steps_own, wanted_own, rows,
):
    c, x, h = scal[0], scal[1], scal[5]
    for r, part in enumerate((ta1, td1, tb1)):
        for b in range(4):
            rows[128 * r : 128 * r + 64, 512 * b : 512 * b + 512] = part[64 * b : 64 * b + 64]
    for r, part in enumerate((ta2, td2, tb2)):
        rows[128 * r + 64 : 128 * r + 128] = part[...]
    first = c == 0
    head = lax.broadcasted_iota(jnp.int32, (8, 4 * TOK), 0)
    row = lax.broadcasted_iota(jnp.int32, (16, 3 * TOK), 0)
    other_head = h + 1 - 2 * c
    for r, part in enumerate((upper, ta1, td1, tb1)):
        n = lax.rem(x - r + DOCS, DOCS)
        body = part[256:272].astype(F32)[0:8]
        mine = jnp.sum(jnp.where(head == h, body, 0.0), axis=0, keepdims=True)
        theirs = jnp.sum(jnp.where(head == other_head, body, 0.0), axis=0, keepdims=True)
        decay = (mine[:, :TOK] + mine[:, TOK : 2 * TOK]) + mine[:, 2 * TOK : 3 * TOK]
        wanted = mine[:, 3 * TOK :]
        steps_own[n] = jnp.broadcast_to(decay, (8, TOK))
        wanted_own[n] = jnp.broadcast_to(wanted, (8, TOK))
        line = jnp.concatenate([wanted, wanted, wanted], axis=1)
        note = jnp.where(row == 0, theirs[:, : 3 * TOK], jnp.where(row == 1, line, 0.0))
        kvq_other[n, TOK:] = note.astype(BF)
    for k in range(3):
        part = jnp.concatenate([early[k], mm(rows[...], w[k]).astype(BF)], axis=0)
        for r in range(DOCS):
            n = lax.rem(x - r + DOCS, DOCS)
            lo = part[r * TOK : (r + 1) * TOK, :DH]
            hi = part[r * TOK : (r + 1) * TOK, DH:]
            own = jnp.where(first, lo, hi)
            other = jnp.where(first, hi, lo)
            if k == 0:
                q_own[n] = own
                kvq_other[n, :TOK, 2 * DH :] = other
            else:
                here = slice((k - 1) * DH, k * DH)
                kv_own[n, :, here] = own
                kvq_other[n, :TOK, here] = other


def states_kernel(scal, kv_own, kvq_mate, steps_own, wanted_own, wft, out, state0, steps, wanted):
    c, h = scal[0], scal[5]
    first = c == 0
    place = lax.broadcasted_iota(jnp.int32, (8, TOK), 0)
    decays, blocks = jnp.zeros((8, TOK), F32), jnp.zeros((8, TOK), F32)
    for n in range(DOCS):
        note = kvq_mate[n, TOK:].astype(F32)
        theirs = (note[0:1, :TOK] + note[0:1, TOK : 2 * TOK]) + note[0:1, 2 * TOK :]
        here = place == 2 * n + c
        there = place == 2 * n + 1 - c
        decays = jnp.where(here, steps_own[n], jnp.where(there, theirs, decays))
        blocks = jnp.where(here, wanted_own[n], jnp.where(there, note[1:2, :TOK], blocks))
    steps[...] = decays
    wanted[...] = blocks
    cum = cumulative_of(decays)
    feature = wft[h]
    row = lax.broadcasted_iota(jnp.int32, (16, TOK), 0)
    segs = []
    for n in range(DOCS):
        own = kv_own[n]
        mate = kvq_mate[n, :TOK, : 2 * DH]
        segs += [jnp.where(first, own, mate), jnp.where(first, mate, own)]
    keys = jnp.concatenate([a[:, :DH] for a in segs], axis=0)
    phi = softmax0(nt(feature, keys)).astype(BF).astype(F32)
    lines = [cum[i : i + 1] for i in range(8)]
    finals = [a[:, TOK - 1 :] for a in lines]
    weighted = [
        (jnp.exp(finals[i] - lines[i]) * phi[:, TOK * i : TOK * i + TOK]).astype(BF) for i in range(8)
    ]
    local = [mm(weighted[i], segs[i][:, DH:]) for i in range(8)]
    for n in range(DOCS):
        last0 = jnp.broadcast_to(finals[2 * n], (1, TOK))
        last1 = jnp.broadcast_to(finals[2 * n + 1], (1, TOK))
        state0[n] = local[2 * n]
        state = jnp.exp(last1) * local[2 * n] + local[2 * n + 1]
        tail = decay_rows(row, last0 + last1)
        for half in range(2):
            p = 2 * n + half
            out[p, 0:16] = state_rows(state[8 * half : 8 * half + 8])
            out[p, 16:32] = tail
            out[p, 32:64] = segs[2 * n][32 * half : 32 * half + 32, :DH]
            out[p, 64:96] = segs[2 * n][32 * half : 32 * half + 32, DH:]


def join_kernel(scal, kv_own, q_own, kvq_mate, kv2, q2):
    c = scal[0]
    first = c == 0
    for n in range(DOCS):
        own = kv_own[n]
        mate = kvq_mate[n, :TOK, : 2 * DH]
        early, later = jnp.where(first, own, mate), jnp.where(first, mate, own)
        kv2[0, n] = early
        kv2[1, n] = later
        q2[c, n] = q_own[n]
        q2[1 - c, n] = kvq_mate[n, :TOK, 2 * DH :]


def state_rows(state):
    hi, lo = split2(state)
    return jnp.concatenate([hi.astype(F32), lo.astype(F32)], axis=0).astype(BF)


def decay_rows(row, decay):
    hi, mid, lo = (p.astype(F32) for p in split3(decay))
    return jnp.where(row == 0, hi, jnp.where(row == 1, mid, jnp.where(row == 2, lo, 0.0))).astype(BF)


def read_state(got, peer):
    both = got[peer, 0:16].astype(F32)
    return both[0:8] + both[8:16]


def read_decay(got, peer):
    tail = got[peer, 16:32].astype(F32)
    return (tail[0:1] + tail[1:2]) + tail[2:3]


def row_kernel(got, out, inner, outer):
    row = lax.broadcasted_iota(jnp.int32, (16, TOK), 0)
    total = jnp.zeros((8, TOK), F32)
    reach = jnp.zeros((1, TOK), F32)
    for peer in range(8):
        inner[peer] = total
        outer[peer] = jnp.broadcast_to(jnp.exp(reach), (8, TOK))
        decay = read_decay(got, peer)
        total = total * jnp.exp(decay) + read_state(got, peer)
        reach = reach + decay
    state, tail = state_rows(total), decay_rows(row, reach)
    for peer in range(8):
        out[peer, 0:16] = state
        out[peer, 16:32] = tail
        out[peer, 32:96] = got[0, 32:96]


def back_kernel(scal, got, inner, outer, out):
    y = scal[4]
    before = jnp.zeros((8, TOK), F32)
    for peer in range(8):
        longer = before * jnp.exp(read_decay(got, peer)) + read_state(got, peer)
        before = jnp.where(peer < y, longer, before)
    for peer in range(8):
        out[peer, 0:16] = state_rows(inner[peer] + outer[peer] * before)
        out[peer, 16:80] = got[0, 32:96]


def attend_kernel(scal, pat, kv2, q2, zp, zm, tp, tm, got, state0, steps, wft, gain, out, win):
    q, h = scal[2], scal[5]
    for n in range(DOCS):
        win[n, 0] = tp[n]
        win[n, 7] = tm[n]
        for s in range(2):
            win[n, 1 + s] = zp[s, n]
            win[n, 3 + s] = kv2[s, n]
            win[n, 5 + s] = zm[s, n]

    cum = cumulative_of(steps[...])
    cum_t = cum.T
    feature = wft[h]
    row = lax.broadcasted_iota(jnp.int32, (TOK, TOK), 0)
    col = lax.broadcasted_iota(jnp.int32, (TOK, TOK), 1)
    causal = row >= col
    gains = gain[h]
    units = [(n, s) for n in range(DOCS) for s in range(2)]
    lines = [cum[i : i + 1] for i in range(8)]
    columns = [cum_t[:, i : i + 1] for i in range(8)]
    both = jnp.concatenate([q2[s, n] for n, s in units] + [kv2[s, n, :, :DH] for n, s in units], axis=0)
    phi = softmax0(nt(feature, both)).astype(BF)
    phi_q = phi[:, : 8 * TOK].astype(F32).T
    phi_b = phi_q.astype(BF)
    alike = [mm(phi_b[TOK * i : TOK * i + TOK], phi[:, TOK * (8 + i) : TOK * (9 + i)]) for i in range(8)]
    entering = []
    for n in range(DOCS):
        carried = jnp.concatenate([read_state(got, 2 * n), read_state(got, 2 * n + 1)], axis=0)
        entering += [carried, jnp.exp(lines[2 * n][:, TOK - 1 :]) * carried + state0[n]]
    brought = [mm(phi_q[TOK * i : TOK * i + TOK], entering[i], HIGH) for i in range(8)]
    decays = [jnp.where(causal, jnp.exp(jnp.minimum(columns[i] - lines[i], 0.0)), 0.0) for i in range(8)]
    mixing = [(alike[i] * decays[i]).astype(BF) for i in range(8)]
    inside = [mm(mixing[i], kv2[s, n, :, DH:]) for i, (n, s) in enumerate(units)]
    linear = [inside[i] + brought[i] * jnp.exp(columns[i]) for i in range(8)]
    roots = [lax.rsqrt(jnp.mean(a * a, axis=1, keepdims=True) + EPS) for a in linear]
    normed = [linear[i] * roots[i] * gains for i in range(8)]

    lane = lax.broadcasted_iota(jnp.int32, (1, 7 * BS), 1)
    scale = DH ** (-0.5) * LOG2E
    for n in range(DOCS):
        gk = jnp.concatenate([got[2 * n, 16:48], got[2 * n + 1, 16:48]], axis=0)
        gv = jnp.concatenate([got[2 * n, 48:80], got[2 * n + 1, 48:80]], axis=0)
        picked = []
        for j in range(4):
            picks = [win[n, 3 + (j + d) // 2, pl.ds(BS * ((j + d) % 2), BS)] for d in (-1, 0, 1)]
            for k in range(R):
                place = pat[12 * n + 3 * j + k]
                picks.append(
                    win[n, lax.div(place, 2), pl.ds(pl.multiple_of(BS * lax.rem(place, 2), BS), BS)]
                )
            picked.append(jnp.concatenate(picks, axis=0))
        scores = [
            nt(q2[j // 2, n, BS * (j % 2) : BS * (j % 2) + BS], jnp.concatenate([picked[j][:, :DH], gk], axis=0))
            for j in range(4)
        ]
        for j in range(4):
            block = 4 * q + j
            bad = (
                ((lane < BS) & (block < 2))
                | ((lane >= BS) & (lane < 2 * BS) & (block < 1))
                | ((lane >= 2 * BS) & (lane < 3 * BS) & (block > 4 * CHIPS - 2))
            )
            scores[j] = jnp.where(bad, MASKED, scores[j])
        tops = [jnp.max(a, axis=1, keepdims=True) for a in scores]
        es = [jnp.exp2((a - top) * scale) for a, top in zip(scores, tops)]
        shares = [1.0 / jnp.sum(e, axis=1, keepdims=True) for e in es]
        sparse = [
            mm(es[j].astype(BF), jnp.concatenate([picked[j][:, DH:], gv], axis=0)) * shares[j] for j in range(4)
        ]
        for j in range(4):
            half = slice(BS * (j % 2), BS * (j % 2) + BS)
            out[2 * n + j // 2, half] = (normed[2 * n + j // 2][half] + sparse[j]).astype(BF)


def call(kernel, outs, scratch, spaces, micros, room, *args):
    kinds = {"s": pltpu.SMEM, "v": pltpu.VMEM, "a": pl.ANY}
    return pl.pallas_call(
        kernel,
        out_shape=outs,
        in_specs=[pl.BlockSpec(memory_space=kinds[k]) for k in spaces],
        out_specs=[pl.BlockSpec(memory_space=pltpu.VMEM)] * len(outs),
        scratch_shapes=scratch,
        compiler_params=pltpu.CompilerParams(vmem_limit_bytes=room * 2**20),
        cost_estimate=pl.CostEstimate(
            flops=int(micros * 1e9), bytes_accessed=int(micros * 3e6), transcendentals=0
        ),
    )(*args)


def shape(dims, dtype):
    return jax.ShapeDtypeStruct(dims, dtype)


def pairs(move):
    found = []
    for q in range(CHIPS):
        for c in range(2):
            to, core = move(q, c)
            if 0 <= to < CHIPS:
                found.append((2 * q + c, 2 * to + core))
    return found


XC = [[(2 * q + c) * 4 + x for x in range(4) for c in range(2)] for q in range(CHIPS)]
ZS = [[(8 * y + z) * 2 + c for z in range(8)] for y in range(8) for c in range(2)]
YS = [[(8 * y + z) * 2 + c for y in range(8)] for z in range(8) for c in range(2)]


def exchange(a, axis, groups):
    return lax.all_to_all(a, axis, 0, 0, tiled=True, axis_index_groups=groups)


def per_device(tokens, w_qkv, w_feature, norm_gain, log_decay, pattern):
    x = lax.axis_index("fsdp")
    s = lax.axis_index("seq")
    c, q = s % 2, s // 2
    z, y = q % 8, q // 8
    h = 2 * x + c
    scal = jnp.stack([c, x, q, z, y, h]).astype(jnp.int32)
    up = [(i, (i + 1) % 4) for i in range(4)]
    down = [(i, (i - 1) % 4) for i in range(4)]
    w3 = w_qkv.transpose(1, 0, 2)
    wft = w_feature.transpose(0, 2, 1)
    upper, lower = pl.pallas_call(
        split_kernel,
        grid=(1,),
        out_shape=[shape((272, 512), BF), shape((64, D), BF)],
        in_specs=[
            pl.BlockSpec(memory_space=pltpu.SMEM),
            pl.BlockSpec((1, TOK, D), lambda i: (0, 0, 0)),
            pl.BlockSpec((1, 8, TOK), lambda i: (0, 0, 0)),
        ],
        out_specs=[
            pl.BlockSpec((272, 512), lambda i: (0, 0)),
            pl.BlockSpec((64, D), lambda i: (0, 0)),
        ],
    )(pattern, tokens, log_decay)
    ta1 = lax.ppermute(upper, "fsdp", up)
    tb2 = lax.ppermute(lower, "fsdp", down)
    ta2 = lax.ppermute(lower, "fsdp", up)
    tb1 = lax.ppermute(upper, "fsdp", down)
    td1 = lax.ppermute(ta1, "fsdp", up)
    td2 = lax.ppermute(tb2, "fsdp", down)
    [early] = call(early_kernel, [shape((3, TOK, 2 * DH), BF)], [], "vva", 6, 12, tokens, w3, ta1)

    kv_own, kvq_other, q_own, steps_own, wanted_own = call(
        project_kernel,
        [
            shape((DOCS, TOK, 2 * DH), BF),
            shape((DOCS, TOK + 16, 3 * DH), BF),
            shape((DOCS, TOK, DH), BF),
            shape((DOCS, 8, TOK), F32),
            shape((DOCS, 8, TOK), F32),
        ],
        [pltpu.VMEM((3 * TOK, D), BF)],
        "s" + "v" * 9,
        3,
        16,
        scal, early, upper, ta1, td1, tb1, ta2, td2, tb2, w3,
    )
    kvq_mate = lax.ppermute(kvq_other, "seq", pairs(lambda q, c: (q, 1 - c)))
    kv2, q2 = call(
        join_kernel,
        [shape((2, DOCS, TOK, 2 * DH), BF), shape((2, DOCS, TOK, DH), BF)],
        [],
        "svvv",
        20,
        8,
        scal, kv_own, q_own, kvq_mate,
    )
    zp = lax.ppermute(kv2, "seq", pairs(lambda q, c: (q + 1, c)))
    zm = lax.ppermute(kv2, "seq", pairs(lambda q, c: (q - 1, c)))
    send1, state0, steps, wanted = call(
        states_kernel,
        [
            shape((8, ROWS, TOK), BF),
            shape((DOCS, F, DH), F32),
            shape((8, TOK), F32),
            shape((8, TOK), F32),
        ],
        [],
        "svvvvv",
        2,
        8,
        scal, kv_own, kvq_mate, steps_own, wanted_own, wft,
    )
    pat = wanted[:, :6].astype(jnp.int32).reshape(48) - (4 * q - 6)
    pat = jnp.clip(pat, 0, 15).astype(jnp.int32)
    got1 = exchange(send1, "seq", ZS)
    def chain(got1, near_p, near_m):
        send2, inner, outer = call(
            row_kernel,
            [shape((8, ROWS, TOK), BF), shape((8, 8, TOK), F32), shape((8, 8, TOK), F32)],
            [],
            "v",
            1,
            4,
            got1,
        )
        got2 = exchange(send2, "seq", YS)
        [send3] = call(
            back_kernel, [shape((8, 80, TOK), BF)], [], "svvv", 1, 4, scal, got2, inner, outer
        )
        tp = lax.ppermute(near_p, "seq", pairs(lambda q, c: (q + 1, c)))
        tm = lax.ppermute(near_m, "seq", pairs(lambda q, c: (q - 1, c)))
        return exchange(send3, "seq", ZS), tp, tm

    got3, tp, tm = chain(got1, zp[1], zm[0])

    [out] = call(
        attend_kernel,
        [shape((8, TOK, DH), BF)],
        [pltpu.VMEM((DOCS, 8, TOK, 2 * DH), BF)],
        "ss" + "v" * 11,
        8,
        16,
        scal, pat, kv2, q2, zp, zm, tp, tm, got3, state0, steps, wft,
        norm_gain.reshape(HALF_HEADS, 1, DH),
    )
    mixed = exchange(out, ("seq", "fsdp"), XC)
    return mixed.transpose(1, 0, 2).reshape(1, TOK, HD)


def solution(mesh):
    placed = (
        P("fsdp", "seq", None),
        P(None, None, "fsdp"),
        P(),
        P(),
        P("fsdp", None, "seq"),
        P("fsdp", "seq", None),
    )
    return jax.shard_map(
        per_device, mesh=mesh, in_specs=placed, out_specs=P("fsdp", "seq", None), check_vma=False
    )
```

```python
import jax
import jax.numpy as jnp
from jax import lax
from jax.experimental import pallas as pl
from jax.experimental.pallas import tpu as pltpu
from jax.sharding import PartitionSpec as P

HALF_HEADS = 8
DH = 128
F = 16
HD = 1024
D = 2048
BS = 64
R = 3
TOK = 128
NB = 2
DOCS = 4
EPS = 1e-06
LOG2E = 1.4426950408889634
MASKED = -1e30
CHIPS = 64
ROWS = 96
BF = jnp.bfloat16
F32 = jnp.float32
HIGH = lax.Precision.HIGHEST


def nt(a, b):
    return lax.dot_general(a, b, (((1,), (1,)), ((), ())), preferred_element_type=F32)


def mm(a, b, precision=None):
    return jnp.dot(a, b, preferred_element_type=F32, precision=precision)


def softmax0(logits):
    top = jnp.max(logits, axis=0, keepdims=True)
    e = jnp.exp(logits - top)
    return e / jnp.sum(e, axis=0, keepdims=True)


def split2(a):
    hi = a.astype(BF)
    return hi, (a - hi.astype(F32)).astype(BF)


def split3(a):
    hi, rest = a.astype(BF), None
    rest = a - hi.astype(F32)
    mid = rest.astype(BF)
    return hi, mid, (rest - mid.astype(F32)).astype(BF)


def cumulative_of(steps):
    row = lax.broadcasted_iota(jnp.int32, (TOK, TOK), 0)
    col = lax.broadcasted_iota(jnp.int32, (TOK, TOK), 1)
    return mm(steps, jnp.where(row <= col, 1.0, 0.0).astype(F32), HIGH)


def split_kernel(pat, tokens, steps, upper, lower):
    for b in range(4):
        upper[64 * b : 64 * b + 64] = tokens[0, :64, 512 * b : 512 * b + 512]
    lower[...] = tokens[0, 64:]
    lane = lax.broadcasted_iota(jnp.int32, (8, TOK), 1)
    wanted = jnp.zeros((8, TOK), jnp.int32)
    for i in range(6):
        wanted = jnp.where(lane == i, pat[0, i // 3, i % 3], wanted)
    parts = [p.astype(F32) for p in split3(steps[0])] + [wanted.astype(F32)]
    body = jnp.concatenate(parts, axis=1)
    upper[256:272] = jnp.concatenate([body, jnp.zeros((8, 4 * TOK), F32)], axis=0).astype(BF)


def early_kernel(t0, w, ta1, own):
    for k in range(3):
        own[k] = mm(t0[0], w[k]).astype(BF)


def project_kernel(
    scal, early, upper, ta1, td1, tb1, ta2, td2, tb2, w,
    kv_own, kvq_other, q_own, steps_own, wanted_own, rows,
):
    c, x, h = scal[0], scal[1], scal[5]
    for r, part in enumerate((ta1, td1, tb1)):
        for b in range(4):
            rows[128 * r : 128 * r + 64, 512 * b : 512 * b + 512] = part[64 * b : 64 * b + 64]
    for r, part in enumerate((ta2, td2, tb2)):
        rows[128 * r + 64 : 128 * r + 128] = part[...]
    first = c == 0
    head = lax.broadcasted_iota(jnp.int32, (8, 4 * TOK), 0)
    row = lax.broadcasted_iota(jnp.int32, (16, 3 * TOK), 0)
    other_head = h + 1 - 2 * c
    for r, part in enumerate((upper, ta1, td1, tb1)):
        n = lax.rem(x - r + DOCS, DOCS)
        body = part[256:272].astype(F32)[0:8]
        mine = jnp.sum(jnp.where(head == h, body, 0.0), axis=0, keepdims=True)
        theirs = jnp.sum(jnp.where(head == other_head, body, 0.0), axis=0, keepdims=True)
        decay = (mine[:, :TOK] + mine[:, TOK : 2 * TOK]) + mine[:, 2 * TOK : 3 * TOK]
        wanted = mine[:, 3 * TOK :]
        steps_own[n] = jnp.broadcast_to(decay, (8, TOK))
        wanted_own[n] = jnp.broadcast_to(wanted, (8, TOK))
        line = jnp.concatenate([wanted, wanted, wanted], axis=1)
        note = jnp.where(row == 0, theirs[:, : 3 * TOK], jnp.where(row == 1, line, 0.0))
        kvq_other[n, TOK:] = note.astype(BF)
    for k in range(3):
        part = jnp.concatenate([early[k], mm(rows[...], w[k]).astype(BF)], axis=0)
        for r in range(DOCS):
            n = lax.rem(x - r + DOCS, DOCS)
            lo = part[r * TOK : (r + 1) * TOK, :DH]
            hi = part[r * TOK : (r + 1) * TOK, DH:]
            own = jnp.where(first, lo, hi)
            other = jnp.where(first, hi, lo)
            if k == 0:
                q_own[n] = own
                kvq_other[n, :TOK, 2 * DH :] = other
            else:
                here = slice((k - 1) * DH, k * DH)
                kv_own[n, :, here] = own
                kvq_other[n, :TOK, here] = other


def states_kernel(scal, kv_own, kvq_mate, steps_own, wanted_own, wft, out, state0, steps, wanted):
    c, h = scal[0], scal[5]
    first = c == 0
    place = lax.broadcasted_iota(jnp.int32, (8, TOK), 0)
    decays, blocks = jnp.zeros((8, TOK), F32), jnp.zeros((8, TOK), F32)
    for n in range(DOCS):
        note = kvq_mate[n, TOK:].astype(F32)
        theirs = (note[0:1, :TOK] + note[0:1, TOK : 2 * TOK]) + note[0:1, 2 * TOK :]
        here = place == 2 * n + c
        there = place == 2 * n + 1 - c
        decays = jnp.where(here, steps_own[n], jnp.where(there, theirs, decays))
        blocks = jnp.where(here, wanted_own[n], jnp.where(there, note[1:2, :TOK], blocks))
    steps[...] = decays
    wanted[...] = blocks
    cum = cumulative_of(decays)
    feature = wft[h]
    row = lax.broadcasted_iota(jnp.int32, (16, TOK), 0)
    segs = []
    for n in range(DOCS):
        own = kv_own[n]
        mate = kvq_mate[n, :TOK, : 2 * DH]
        segs += [jnp.where(first, own, mate), jnp.where(first, mate, own)]
    keys = jnp.concatenate([a[:, :DH] for a in segs], axis=0)
    phi = softmax0(nt(feature, keys)).astype(BF).astype(F32)
    lines = [cum[i : i + 1] for i in range(8)]
    finals = [a[:, TOK - 1 :] for a in lines]
    weighted = [
        (jnp.exp(finals[i] - lines[i]) * phi[:, TOK * i : TOK * i + TOK]).astype(BF) for i in range(8)
    ]
    local = [mm(weighted[i], segs[i][:, DH:]) for i in range(8)]
    for n in range(DOCS):
        last0 = jnp.broadcast_to(finals[2 * n], (1, TOK))
        last1 = jnp.broadcast_to(finals[2 * n + 1], (1, TOK))
        state0[n] = local[2 * n]
        state = jnp.exp(last1) * local[2 * n] + local[2 * n + 1]
        tail = decay_rows(row, last0 + last1)
        for half in range(2):
            p = 2 * n + half
            out[p, 0:16] = state_rows(state[8 * half : 8 * half + 8])
            out[p, 16:32] = tail
            out[p, 32:64] = segs[2 * n][32 * half : 32 * half + 32, :DH]
            out[p, 64:96] = segs[2 * n][32 * half : 32 * half + 32, DH:]


def join_kernel(scal, kv_own, q_own, kvq_mate, send1, kv2, q2):
    c = scal[0]
    first = c == 0
    for n in range(DOCS):
        own = kv_own[n]
        mate = kvq_mate[n, :TOK, : 2 * DH]
        early, later = jnp.where(first, own, mate), jnp.where(first, mate, own)
        kv2[0, n] = early
        kv2[1, n] = later
        q2[c, n] = q_own[n]
        q2[1 - c, n] = kvq_mate[n, :TOK, 2 * DH :]


def state_rows(state):
    hi, lo = split2(state)
    return jnp.concatenate([hi.astype(F32), lo.astype(F32)], axis=0).astype(BF)


def decay_rows(row, decay):
    hi, mid, lo = (p.astype(F32) for p in split3(decay))
    return jnp.where(row == 0, hi, jnp.where(row == 1, mid, jnp.where(row == 2, lo, 0.0))).astype(BF)


def read_state(got, peer):
    both = got[peer, 0:16].astype(F32)
    return both[0:8] + both[8:16]


def read_decay(got, peer):
    tail = got[peer, 16:32].astype(F32)
    return (tail[0:1] + tail[1:2]) + tail[2:3]


def row_kernel(got, out, inner, outer):
    row = lax.broadcasted_iota(jnp.int32, (16, TOK), 0)
    total = jnp.zeros((8, TOK), F32)
    reach = jnp.zeros((1, TOK), F32)
    for peer in range(8):
        inner[peer] = total
        outer[peer] = jnp.broadcast_to(jnp.exp(reach), (8, TOK))
        decay = read_decay(got, peer)
        total = total * jnp.exp(decay) + read_state(got, peer)
        reach = reach + decay
    state, tail = state_rows(total), decay_rows(row, reach)
    for peer in range(8):
        out[peer, 0:16] = state
        out[peer, 16:32] = tail
        out[peer, 32:96] = got[0, 32:96]


def back_kernel(scal, got, inner, outer, *refs):
    out = refs[-1]
    y = scal[4]
    before = jnp.zeros((8, TOK), F32)
    for peer in range(8):
        longer = before * jnp.exp(read_decay(got, peer)) + read_state(got, peer)
        before = jnp.where(peer < y, longer, before)
    for peer in range(8):
        out[peer, 0:16] = state_rows(inner[peer] + outer[peer] * before)
        out[peer, 16:80] = got[0, 32:96]


def attend_kernel(scal, pat, kv2, q2, zp, zm, tp, tm, got, state0, steps, wft, gain, out, win):
    q, h = scal[2], scal[5]
    for n in range(DOCS):
        win[n, 0] = tp[n]
        win[n, 7] = tm[n]
        for s in range(2):
            win[n, 1 + s] = zp[s, n]
            win[n, 3 + s] = kv2[s, n]
            win[n, 5 + s] = zm[s, n]

    cum = cumulative_of(steps[...])
    cum_t = cum.T
    feature = wft[h]
    row = lax.broadcasted_iota(jnp.int32, (TOK, TOK), 0)
    col = lax.broadcasted_iota(jnp.int32, (TOK, TOK), 1)
    causal = row >= col
    gains = gain[h]
    units = [(n, s) for n in range(DOCS) for s in range(2)]
    lines = [cum[i : i + 1] for i in range(8)]
    columns = [cum_t[:, i : i + 1] for i in range(8)]
    both = jnp.concatenate([q2[s, n] for n, s in units] + [kv2[s, n, :, :DH] for n, s in units], axis=0)
    phi = softmax0(nt(feature, both)).astype(BF)
    phi_q = phi[:, : 8 * TOK].astype(F32).T
    phi_b = phi_q.astype(BF)
    alike = [mm(phi_b[TOK * i : TOK * i + TOK], phi[:, TOK * (8 + i) : TOK * (9 + i)]) for i in range(8)]
    entering = []
    for n in range(DOCS):
        carried = jnp.concatenate([read_state(got, 2 * n), read_state(got, 2 * n + 1)], axis=0)
        entering += [carried, jnp.exp(lines[2 * n][:, TOK - 1 :]) * carried + state0[n]]
    brought = [mm(phi_q[TOK * i : TOK * i + TOK], entering[i], HIGH) for i in range(8)]
    decays = [jnp.where(causal, jnp.exp(jnp.minimum(columns[i] - lines[i], 0.0)), 0.0) for i in range(8)]
    mixing = [(alike[i] * decays[i]).astype(BF) for i in range(8)]
    inside = [mm(mixing[i], kv2[s, n, :, DH:]) for i, (n, s) in enumerate(units)]
    linear = [inside[i] + brought[i] * jnp.exp(columns[i]) for i in range(8)]
    roots = [lax.rsqrt(jnp.mean(a * a, axis=1, keepdims=True) + EPS) for a in linear]
    normed = [linear[i] * roots[i] * gains for i in range(8)]

    lane = lax.broadcasted_iota(jnp.int32, (1, 7 * BS), 1)
    scale = DH ** (-0.5) * LOG2E
    for n in range(DOCS):
        gk = jnp.concatenate([got[2 * n, 16:48], got[2 * n + 1, 16:48]], axis=0)
        gv = jnp.concatenate([got[2 * n, 48:80], got[2 * n + 1, 48:80]], axis=0)
        picked = []
        for j in range(4):
            picks = [win[n, 3 + (j + d) // 2, pl.ds(BS * ((j + d) % 2), BS)] for d in (-1, 0, 1)]
            for k in range(R):
                place = pat[12 * n + 3 * j + k]
                picks.append(
                    win[n, lax.div(place, 2), pl.ds(pl.multiple_of(BS * lax.rem(place, 2), BS), BS)]
                )
            picked.append(jnp.concatenate(picks, axis=0))
        scores = [
            nt(q2[j // 2, n, BS * (j % 2) : BS * (j % 2) + BS], jnp.concatenate([picked[j][:, :DH], gk], axis=0))
            for j in range(4)
        ]
        for j in range(4):
            block = 4 * q + j
            bad = (
                ((lane < BS) & (block < 2))
                | ((lane >= BS) & (lane < 2 * BS) & (block < 1))
                | ((lane >= 2 * BS) & (lane < 3 * BS) & (block > 4 * CHIPS - 2))
            )
            scores[j] = jnp.where(bad, MASKED, scores[j])
        tops = [jnp.max(a, axis=1, keepdims=True) for a in scores]
        es = [jnp.exp2((a - top) * scale) for a, top in zip(scores, tops)]
        shares = [1.0 / jnp.sum(e, axis=1, keepdims=True) for e in es]
        sparse = [
            mm(es[j].astype(BF), jnp.concatenate([picked[j][:, DH:], gv], axis=0)) * shares[j] for j in range(4)
        ]
        for j in range(4):
            half = slice(BS * (j % 2), BS * (j % 2) + BS)
            out[2 * n + j // 2, half] = (normed[2 * n + j // 2][half] + sparse[j]).astype(BF)


def call(kernel, outs, scratch, spaces, micros, room, *args):
    kinds = {"s": pltpu.SMEM, "v": pltpu.VMEM, "a": pl.ANY}
    return pl.pallas_call(
        kernel,
        out_shape=outs,
        in_specs=[pl.BlockSpec(memory_space=kinds[k]) for k in spaces],
        out_specs=[pl.BlockSpec(memory_space=pltpu.VMEM)] * len(outs),
        scratch_shapes=scratch,
        compiler_params=pltpu.CompilerParams(vmem_limit_bytes=room * 2**20),
        cost_estimate=pl.CostEstimate(
            flops=int(micros * 1e9), bytes_accessed=int(micros * 3e6), transcendentals=0
        ),
    )(*args)


def shape(dims, dtype):
    return jax.ShapeDtypeStruct(dims, dtype)


def pairs(move):
    found = []
    for q in range(CHIPS):
        for c in range(2):
            to, core = move(q, c)
            if 0 <= to < CHIPS:
                found.append((2 * q + c, 2 * to + core))
    return found


XC = [[(2 * q + c) * 4 + x for x in range(4) for c in range(2)] for q in range(CHIPS)]
ZS = [[(8 * y + z) * 2 + c for z in range(8)] for y in range(8) for c in range(2)]
YS = [[(8 * y + z) * 2 + c for y in range(8)] for z in range(8) for c in range(2)]


def exchange(a, axis, groups):
    return lax.all_to_all(a, axis, 0, 0, tiled=True, axis_index_groups=groups)


def per_device(tokens, w_qkv, w_feature, norm_gain, log_decay, pattern):
    x = lax.axis_index("fsdp")
    s = lax.axis_index("seq")
    c, q = s % 2, s // 2
    z, y = q % 8, q // 8
    h = 2 * x + c
    scal = jnp.stack([c, x, q, z, y, h]).astype(jnp.int32)
    up = [(i, (i + 1) % 4) for i in range(4)]
    down = [(i, (i - 1) % 4) for i in range(4)]
    w3 = w_qkv.transpose(1, 0, 2)
    wft = w_feature.transpose(0, 2, 1)
    upper, lower = pl.pallas_call(
        split_kernel,
        grid=(1,),
        out_shape=[shape((272, 512), BF), shape((64, D), BF)],
        in_specs=[
            pl.BlockSpec(memory_space=pltpu.SMEM),
            pl.BlockSpec((1, TOK, D), lambda i: (0, 0, 0)),
            pl.BlockSpec((1, 8, TOK), lambda i: (0, 0, 0)),
        ],
        out_specs=[
            pl.BlockSpec((272, 512), lambda i: (0, 0)),
            pl.BlockSpec((64, D), lambda i: (0, 0)),
        ],
    )(pattern, tokens, log_decay)
    ta1 = lax.ppermute(upper, "fsdp", up)
    tb2 = lax.ppermute(lower, "fsdp", down)
    ta2 = lax.ppermute(lower, "fsdp", up)
    tb1 = lax.ppermute(upper, "fsdp", down)
    td1 = lax.ppermute(ta1, "fsdp", up)
    td2 = lax.ppermute(tb2, "fsdp", down)
    [early] = call(early_kernel, [shape((3, TOK, 2 * DH), BF)], [], "vva", 6, 12, tokens, w3, ta1)

    kv_own, kvq_other, q_own, steps_own, wanted_own = call(
        project_kernel,
        [
            shape((DOCS, TOK, 2 * DH), BF),
            shape((DOCS, TOK + 16, 3 * DH), BF),
            shape((DOCS, TOK, DH), BF),
            shape((DOCS, 8, TOK), F32),
            shape((DOCS, 8, TOK), F32),
        ],
        [pltpu.VMEM((3 * TOK, D), BF)],
        "s" + "v" * 9,
        3,
        16,
        scal, early, upper, ta1, td1, tb1, ta2, td2, tb2, w3,
    )
    kvq_mate = lax.ppermute(kvq_other, "seq", pairs(lambda q, c: (q, 1 - c)))
    send1, state0, steps, wanted = call(
        states_kernel,
        [
            shape((8, ROWS, TOK), BF),
            shape((DOCS, F, DH), F32),
            shape((8, TOK), F32),
            shape((8, TOK), F32),
        ],
        [],
        "svvvvv",
        2,
        8,
        scal, kv_own, kvq_mate, steps_own, wanted_own, wft,
    )
    pat = wanted[:, :6].astype(jnp.int32).reshape(48) - (4 * q - 6)
    pat = jnp.clip(pat, 0, 15).astype(jnp.int32)
    kv2, q2 = call(
        join_kernel,
        [shape((2, DOCS, TOK, 2 * DH), BF), shape((2, DOCS, TOK, DH), BF)],
        [],
        "svvva",
        20,
        8,
        scal, kv_own, q_own, kvq_mate, send1,
    )
    zp = lax.ppermute(kv2, "seq", pairs(lambda q, c: (q + 1, c)))
    zm = lax.ppermute(kv2, "seq", pairs(lambda q, c: (q - 1, c)))
    got1 = exchange(send1, "seq", ZS)
    def chain(got1, near_p, near_m):
        send2, inner, outer = call(
            row_kernel,
            [shape((8, ROWS, TOK), BF), shape((8, 8, TOK), F32), shape((8, 8, TOK), F32)],
            [],
            "v",
            1,
            4,
            got1,
        )
        tp = lax.ppermute(near_p, "seq", pairs(lambda q, c: (q + 1, c)))
        tm = lax.ppermute(near_m, "seq", pairs(lambda q, c: (q - 1, c)))
        got2 = exchange(send2, "seq", YS)
        [send3] = call(
            back_kernel, [shape((8, 80, TOK), BF)], [], "svvvaa", 1, 4, scal, got2, inner, outer, tp, tm
        )
        return exchange(send3, "seq", ZS), tp, tm

    got3, tp, tm = chain(got1, zp[1], zm[0])

    [out] = call(
        attend_kernel,
        [shape((8, TOK, DH), BF)],
        [pltpu.VMEM((DOCS, 8, TOK, 2 * DH), BF)],
        "ss" + "v" * 11,
        8,
        16,
        scal, pat, kv2, q2, zp, zm, tp, tm, got3, state0, steps, wft,
        norm_gain.reshape(HALF_HEADS, 1, DH),
    )
    mixed = exchange(out, ("seq", "fsdp"), XC)
    return mixed.transpose(1, 0, 2).reshape(1, TOK, HD)


def solution(mesh):
    placed = (
        P("fsdp", "seq", None),
        P(None, None, "fsdp"),
        P(),
        P(),
        P("fsdp", None, "seq"),
        P("fsdp", "seq", None),
    )
    return jax.shard_map(
        per_device, mesh=mesh, in_specs=placed, out_specs=P("fsdp", "seq", None), check_vma=False
    )
```

```python
import jax
import jax.numpy as jnp
from jax import lax
from jax.experimental import pallas as pl
from jax.experimental.pallas import tpu as pltpu
from jax.sharding import PartitionSpec as P

HALF_HEADS = 8
DH = 128
F = 16
HD = 1024
D = 2048
BS = 64
R = 3
TOK = 128
NB = 2
DOCS = 4
EPS = 1e-06
LOG2E = 1.4426950408889634
MASKED = -1e30
CHIPS = 64
ROWS = 96
BF = jnp.bfloat16
F32 = jnp.float32
HIGH = lax.Precision.HIGHEST


def nt(a, b):
    return lax.dot_general(a, b, (((1,), (1,)), ((), ())), preferred_element_type=F32)


def mm(a, b, precision=None):
    return jnp.dot(a, b, preferred_element_type=F32, precision=precision)


def softmax0(logits):
    top = jnp.max(logits, axis=0, keepdims=True)
    e = jnp.exp(logits - top)
    return e / jnp.sum(e, axis=0, keepdims=True)


def split2(a):
    hi = a.astype(BF)
    return hi, (a - hi.astype(F32)).astype(BF)


def split3(a):
    hi, rest = a.astype(BF), None
    rest = a - hi.astype(F32)
    mid = rest.astype(BF)
    return hi, mid, (rest - mid.astype(F32)).astype(BF)


def cumulative_of(steps):
    row = lax.broadcasted_iota(jnp.int32, (TOK, TOK), 0)
    col = lax.broadcasted_iota(jnp.int32, (TOK, TOK), 1)
    return mm(steps, jnp.where(row <= col, 1.0, 0.0).astype(F32), HIGH)


def lower_kernel(tokens, lower):
    lower[...] = tokens[0]


def upper_kernel(pat, tokens, steps, upper):
    for b in range(4):
        upper[64 * b : 64 * b + 64] = tokens[0, :, 512 * b : 512 * b + 512]
    lane = lax.broadcasted_iota(jnp.int32, (8, TOK), 1)
    wanted = jnp.zeros((8, TOK), jnp.int32)
    for i in range(6):
        wanted = jnp.where(lane == i, pat[0, i // 3, i % 3], wanted)
    parts = [p.astype(F32) for p in split3(steps[0])] + [wanted.astype(F32)]
    body = jnp.concatenate(parts, axis=1)
    upper[256:272] = jnp.concatenate([body, jnp.zeros((8, 4 * TOK), F32)], axis=0).astype(BF)


def early_kernel(t0, w, ta1, own):
    for k in range(3):
        own[k] = mm(t0[0], w[k]).astype(BF)


def project_kernel(
    scal, early, upper, ta1, td1, tb1, ta2, td2, tb2, w,
    kv_own, kvq_other, q_own, steps_own, wanted_own, rows,
):
    c, x, h = scal[0], scal[1], scal[5]
    for r, part in enumerate((ta1, td1, tb1)):
        for b in range(4):
            rows[128 * r : 128 * r + 64, 512 * b : 512 * b + 512] = part[64 * b : 64 * b + 64]
    for r, part in enumerate((ta2, td2, tb2)):
        rows[128 * r + 64 : 128 * r + 128] = part[...]
    first = c == 0
    head = lax.broadcasted_iota(jnp.int32, (8, 4 * TOK), 0)
    row = lax.broadcasted_iota(jnp.int32, (16, 3 * TOK), 0)
    other_head = h + 1 - 2 * c
    for r, part in enumerate((upper, ta1, td1, tb1)):
        n = lax.rem(x - r + DOCS, DOCS)
        body = part[256:272].astype(F32)[0:8]
        mine = jnp.sum(jnp.where(head == h, body, 0.0), axis=0, keepdims=True)
        theirs = jnp.sum(jnp.where(head == other_head, body, 0.0), axis=0, keepdims=True)
        decay = (mine[:, :TOK] + mine[:, TOK : 2 * TOK]) + mine[:, 2 * TOK : 3 * TOK]
        wanted = mine[:, 3 * TOK :]
        steps_own[n] = jnp.broadcast_to(decay, (8, TOK))
        wanted_own[n] = jnp.broadcast_to(wanted, (8, TOK))
        line = jnp.concatenate([wanted, wanted, wanted], axis=1)
        note = jnp.where(row == 0, theirs[:, : 3 * TOK], jnp.where(row == 1, line, 0.0))
        kvq_other[n, TOK:] = note.astype(BF)
    for k in range(3):
        part = jnp.concatenate([early[k], mm(rows[...], w[k]).astype(BF)], axis=0)
        for r in range(DOCS):
            n = lax.rem(x - r + DOCS, DOCS)
            lo = part[r * TOK : (r + 1) * TOK, :DH]
            hi = part[r * TOK : (r + 1) * TOK, DH:]
            own = jnp.where(first, lo, hi)
            other = jnp.where(first, hi, lo)
            if k == 0:
                q_own[n] = own
                kvq_other[n, :TOK, 2 * DH :] = other
            else:
                here = slice((k - 1) * DH, k * DH)
                kv_own[n, :, here] = own
                kvq_other[n, :TOK, here] = other


def states_kernel(scal, kv_own, kvq_mate, steps_own, wanted_own, wft, out, state0, steps, wanted):
    c, h = scal[0], scal[5]
    first = c == 0
    place = lax.broadcasted_iota(jnp.int32, (8, TOK), 0)
    decays, blocks = jnp.zeros((8, TOK), F32), jnp.zeros((8, TOK), F32)
    for n in range(DOCS):
        note = kvq_mate[n, TOK:].astype(F32)
        theirs = (note[0:1, :TOK] + note[0:1, TOK : 2 * TOK]) + note[0:1, 2 * TOK :]
        here = place == 2 * n + c
        there = place == 2 * n + 1 - c
        decays = jnp.where(here, steps_own[n], jnp.where(there, theirs, decays))
        blocks = jnp.where(here, wanted_own[n], jnp.where(there, note[1:2, :TOK], blocks))
    steps[...] = decays
    wanted[...] = blocks
    cum = cumulative_of(decays)
    feature = wft[h]
    row = lax.broadcasted_iota(jnp.int32, (16, TOK), 0)
    segs = []
    for n in range(DOCS):
        own = kv_own[n]
        mate = kvq_mate[n, :TOK, : 2 * DH]
        segs += [jnp.where(first, own, mate), jnp.where(first, mate, own)]
    keys = jnp.concatenate([a[:, :DH] for a in segs], axis=0)
    phi = softmax0(nt(feature, keys)).astype(BF).astype(F32)
    lines = [cum[i : i + 1] for i in range(8)]
    finals = [a[:, TOK - 1 :] for a in lines]
    weighted = [
        (jnp.exp(finals[i] - lines[i]) * phi[:, TOK * i : TOK * i + TOK]).astype(BF) for i in range(8)
    ]
    local = [mm(weighted[i], segs[i][:, DH:]) for i in range(8)]
    for n in range(DOCS):
        last0 = jnp.broadcast_to(finals[2 * n], (1, TOK))
        last1 = jnp.broadcast_to(finals[2 * n + 1], (1, TOK))
        state0[n] = local[2 * n]
        state = jnp.exp(last1) * local[2 * n] + local[2 * n + 1]
        tail = decay_rows(row, last0 + last1)
        for half in range(2):
            p = 2 * n + half
            out[p, 0:16] = state_rows(state[8 * half : 8 * half + 8])
            out[p, 16:32] = tail
            out[p, 32:64] = segs[2 * n][32 * half : 32 * half + 32, :DH]
            out[p, 64:96] = segs[2 * n][32 * half : 32 * half + 32, DH:]


def join_kernel(scal, kv_own, q_own, kvq_mate, kv2, q2):
    c = scal[0]
    first = c == 0
    for n in range(DOCS):
        own = kv_own[n]
        mate = kvq_mate[n, :TOK, : 2 * DH]
        early, later = jnp.where(first, own, mate), jnp.where(first, mate, own)
        kv2[0, n] = early
        kv2[1, n] = later
        q2[c, n] = q_own[n]
        q2[1 - c, n] = kvq_mate[n, :TOK, 2 * DH :]


def state_rows(state):
    hi, lo = split2(state)
    return jnp.concatenate([hi.astype(F32), lo.astype(F32)], axis=0).astype(BF)


def decay_rows(row, decay):
    hi, mid, lo = (p.astype(F32) for p in split3(decay))
    return jnp.where(row == 0, hi, jnp.where(row == 1, mid, jnp.where(row == 2, lo, 0.0))).astype(BF)


def read_state(got, peer):
    both = got[peer, 0:16].astype(F32)
    return both[0:8] + both[8:16]


def read_decay(got, peer):
    tail = got[peer, 16:32].astype(F32)
    return (tail[0:1] + tail[1:2]) + tail[2:3]


def row_kernel(got, out, inner, outer):
    row = lax.broadcasted_iota(jnp.int32, (16, TOK), 0)
    total = jnp.zeros((8, TOK), F32)
    reach = jnp.zeros((1, TOK), F32)
    for peer in range(8):
        inner[peer] = total
        outer[peer] = jnp.broadcast_to(jnp.exp(reach), (8, TOK))
        decay = read_decay(got, peer)
        total = total * jnp.exp(decay) + read_state(got, peer)
        reach = reach + decay
    state, tail = state_rows(total), decay_rows(row, reach)
    for peer in range(8):
        out[peer, 0:16] = state
        out[peer, 16:32] = tail
        out[peer, 32:96] = got[0, 32:96]


def back_kernel(scal, got, inner, outer, out):
    y = scal[4]
    before = jnp.zeros((8, TOK), F32)
    for peer in range(8):
        longer = before * jnp.exp(read_decay(got, peer)) + read_state(got, peer)
        before = jnp.where(peer < y, longer, before)
    for peer in range(8):
        out[peer, 0:16] = state_rows(inner[peer] + outer[peer] * before)
        out[peer, 16:80] = got[0, 32:96]


def attend_kernel(scal, pat, kv2, q2, zp, zm, tp, tm, got, state0, steps, wft, gain, out, win):
    q, h = scal[2], scal[5]
    for n in range(DOCS):
        win[n, 0] = tp[n]
        win[n, 7] = tm[n]
        for s in range(2):
            win[n, 1 + s] = zp[s, n]
            win[n, 3 + s] = kv2[s, n]
            win[n, 5 + s] = zm[s, n]

    cum = cumulative_of(steps[...])
    cum_t = cum.T
    feature = wft[h]
    row = lax.broadcasted_iota(jnp.int32, (TOK, TOK), 0)
    col = lax.broadcasted_iota(jnp.int32, (TOK, TOK), 1)
    causal = row >= col
    gains = gain[h]
    units = [(n, s) for n in range(DOCS) for s in range(2)]
    lines = [cum[i : i + 1] for i in range(8)]
    columns = [cum_t[:, i : i + 1] for i in range(8)]
    both = jnp.concatenate([q2[s, n] for n, s in units] + [kv2[s, n, :, :DH] for n, s in units], axis=0)
    phi = softmax0(nt(feature, both)).astype(BF)
    phi_q = phi[:, : 8 * TOK].astype(F32).T
    phi_b = phi_q.astype(BF)
    alike = [mm(phi_b[TOK * i : TOK * i + TOK], phi[:, TOK * (8 + i) : TOK * (9 + i)]) for i in range(8)]
    entering = []
    for n in range(DOCS):
        carried = jnp.concatenate([read_state(got, 2 * n), read_state(got, 2 * n + 1)], axis=0)
        entering += [carried, jnp.exp(lines[2 * n][:, TOK - 1 :]) * carried + state0[n]]
    brought = [mm(phi_q[TOK * i : TOK * i + TOK], entering[i], HIGH) for i in range(8)]
    decays = [jnp.where(causal, jnp.exp(jnp.minimum(columns[i] - lines[i], 0.0)), 0.0) for i in range(8)]
    mixing = [(alike[i] * decays[i]).astype(BF) for i in range(8)]
    inside = [mm(mixing[i], kv2[s, n, :, DH:]) for i, (n, s) in enumerate(units)]
    linear = [inside[i] + brought[i] * jnp.exp(columns[i]) for i in range(8)]
    roots = [lax.rsqrt(jnp.mean(a * a, axis=1, keepdims=True) + EPS) for a in linear]
    normed = [linear[i] * roots[i] * gains for i in range(8)]

    lane = lax.broadcasted_iota(jnp.int32, (1, 7 * BS), 1)
    scale = DH ** (-0.5) * LOG2E
    for n in range(DOCS):
        gk = jnp.concatenate([got[2 * n, 16:48], got[2 * n + 1, 16:48]], axis=0)
        gv = jnp.concatenate([got[2 * n, 48:80], got[2 * n + 1, 48:80]], axis=0)
        picked = []
        for j in range(4):
            picks = [win[n, 3 + (j + d) // 2, pl.ds(BS * ((j + d) % 2), BS)] for d in (-1, 0, 1)]
            for k in range(R):
                place = pat[12 * n + 3 * j + k]
                picks.append(
                    win[n, lax.div(place, 2), pl.ds(pl.multiple_of(BS * lax.rem(place, 2), BS), BS)]
                )
            picked.append(jnp.concatenate(picks, axis=0))
        scores = [
            nt(q2[j // 2, n, BS * (j % 2) : BS * (j % 2) + BS], jnp.concatenate([picked[j][:, :DH], gk], axis=0))
            for j in range(4)
        ]
        for j in range(4):
            block = 4 * q + j
            bad = (
                ((lane < BS) & (block < 2))
                | ((lane >= BS) & (lane < 2 * BS) & (block < 1))
                | ((lane >= 2 * BS) & (lane < 3 * BS) & (block > 4 * CHIPS - 2))
            )
            scores[j] = jnp.where(bad, MASKED, scores[j])
        tops = [jnp.max(a, axis=1, keepdims=True) for a in scores]
        es = [jnp.exp2((a - top) * scale) for a, top in zip(scores, tops)]
        shares = [1.0 / jnp.sum(e, axis=1, keepdims=True) for e in es]
        sparse = [
            mm(es[j].astype(BF), jnp.concatenate([picked[j][:, DH:], gv], axis=0)) * shares[j] for j in range(4)
        ]
        for j in range(4):
            half = slice(BS * (j % 2), BS * (j % 2) + BS)
            out[2 * n + j // 2, half] = (normed[2 * n + j // 2][half] + sparse[j]).astype(BF)


def call(kernel, outs, scratch, spaces, micros, room, *args):
    kinds = {"s": pltpu.SMEM, "v": pltpu.VMEM, "a": pl.ANY}
    return pl.pallas_call(
        kernel,
        out_shape=outs,
        in_specs=[pl.BlockSpec(memory_space=kinds[k]) for k in spaces],
        out_specs=[pl.BlockSpec(memory_space=pltpu.VMEM)] * len(outs),
        scratch_shapes=scratch,
        compiler_params=pltpu.CompilerParams(vmem_limit_bytes=room * 2**20),
        cost_estimate=pl.CostEstimate(
            flops=int(micros * 1e9), bytes_accessed=int(micros * 3e6), transcendentals=0
        ),
    )(*args)


def shape(dims, dtype):
    return jax.ShapeDtypeStruct(dims, dtype)


def pairs(move):
    found = []
    for q in range(CHIPS):
        for c in range(2):
            to, core = move(q, c)
            if 0 <= to < CHIPS:
                found.append((2 * q + c, 2 * to + core))
    return found


XC = [[(2 * q + c) * 4 + x for x in range(4) for c in range(2)] for q in range(CHIPS)]
ZS = [[(8 * y + z) * 2 + c for z in range(8)] for y in range(8) for c in range(2)]
YS = [[(8 * y + z) * 2 + c for y in range(8)] for z in range(8) for c in range(2)]


def exchange(a, axis, groups):
    return lax.all_to_all(a, axis, 0, 0, tiled=True, axis_index_groups=groups)


def per_device(tokens, w_qkv, w_feature, norm_gain, log_decay, pattern):
    x = lax.axis_index("fsdp")
    s = lax.axis_index("seq")
    c, q = s % 2, s // 2
    z, y = q % 8, q // 8
    h = 2 * x + c
    scal = jnp.stack([c, x, q, z, y, h]).astype(jnp.int32)
    up = [(i, (i + 1) % 4) for i in range(4)]
    down = [(i, (i - 1) % 4) for i in range(4)]
    w3 = w_qkv.transpose(1, 0, 2)
    wft = w_feature.transpose(0, 2, 1)
    upper = pl.pallas_call(
        upper_kernel,
        grid=(1,),
        out_shape=shape((272, 512), BF),
        in_specs=[
            pl.BlockSpec(memory_space=pltpu.SMEM),
            pl.BlockSpec((1, 64, D), lambda i: (0, 0, 0)),
            pl.BlockSpec((1, 8, TOK), lambda i: (0, 0, 0)),
        ],
        out_specs=pl.BlockSpec((272, 512), lambda i: (0, 0)),
    )(pattern, tokens, log_decay)
    lower = pl.pallas_call(
        lower_kernel,
        grid=(1,),
        out_shape=shape((64, D), BF),
        in_specs=[pl.BlockSpec((1, 64, D), lambda i: (0, 1, 0))],
        out_specs=pl.BlockSpec((64, D), lambda i: (0, 0)),
    )(tokens)
    ta1 = lax.ppermute(upper, "fsdp", up)
    tb2 = lax.ppermute(lower, "fsdp", down)
    ta2 = lax.ppermute(lower, "fsdp", up)
    tb1 = lax.ppermute(upper, "fsdp", down)
    td1 = lax.ppermute(ta1, "fsdp", up)
    td2 = lax.ppermute(tb2, "fsdp", down)
    [early] = call(early_kernel, [shape((3, TOK, 2 * DH), BF)], [], "vva", 6, 12, tokens, w3, ta1)

    kv_own, kvq_other, q_own, steps_own, wanted_own = call(
        project_kernel,
        [
            shape((DOCS, TOK, 2 * DH), BF),
            shape((DOCS, TOK + 16, 3 * DH), BF),
            shape((DOCS, TOK, DH), BF),
            shape((DOCS, 8, TOK), F32),
            shape((DOCS, 8, TOK), F32),
        ],
        [pltpu.VMEM((3 * TOK, D), BF)],
        "s" + "v" * 9,
        3,
        16,
        scal, early, upper, ta1, td1, tb1, ta2, td2, tb2, w3,
    )
    kvq_mate = lax.ppermute(kvq_other, "seq", pairs(lambda q, c: (q, 1 - c)))
    kv2, q2 = call(
        join_kernel,
        [shape((2, DOCS, TOK, 2 * DH), BF), shape((2, DOCS, TOK, DH), BF)],
        [],
        "svvv",
        20,
        8,
        scal, kv_own, q_own, kvq_mate,
    )
    zp = lax.ppermute(kv2, "seq", pairs(lambda q, c: (q + 1, c)))
    zm = lax.ppermute(kv2, "seq", pairs(lambda q, c: (q - 1, c)))
    send1, state0, steps, wanted = call(
        states_kernel,
        [
            shape((8, ROWS, TOK), BF),
            shape((DOCS, F, DH), F32),
            shape((8, TOK), F32),
            shape((8, TOK), F32),
        ],
        [],
        "svvvvv",
        2,
        8,
        scal, kv_own, kvq_mate, steps_own, wanted_own, wft,
    )
    pat = wanted[:, :6].astype(jnp.int32).reshape(48) - (4 * q - 6)
    pat = jnp.clip(pat, 0, 15).astype(jnp.int32)
    got1 = exchange(send1, "seq", ZS)
    def chain(got1, near_p, near_m):
        send2, inner, outer = call(
            row_kernel,
            [shape((8, ROWS, TOK), BF), shape((8, 8, TOK), F32), shape((8, 8, TOK), F32)],
            [],
            "v",
            1,
            4,
            got1,
        )
        got2 = exchange(send2, "seq", YS)
        [send3] = call(
            back_kernel, [shape((8, 80, TOK), BF)], [], "svvv", 1, 4, scal, got2, inner, outer
        )
        tp = lax.ppermute(near_p, "seq", pairs(lambda q, c: (q + 1, c)))
        tm = lax.ppermute(near_m, "seq", pairs(lambda q, c: (q - 1, c)))
        return exchange(send3, "seq", ZS), tp, tm

    got3, tp, tm = chain(got1, zp[1], zm[0])

    [out] = call(
        attend_kernel,
        [shape((8, TOK, DH), BF)],
        [pltpu.VMEM((DOCS, 8, TOK, 2 * DH), BF)],
        "ss" + "v" * 11,
        8,
        16,
        scal, pat, kv2, q2, zp, zm, tp, tm, got3, state0, steps, wft,
        norm_gain.reshape(HALF_HEADS, 1, DH),
    )
    mixed = exchange(out, ("seq", "fsdp"), XC)
    return mixed.transpose(1, 0, 2).reshape(1, TOK, HD)


def solution(mesh):
    placed = (
        P("fsdp", "seq", None),
        P(None, None, "fsdp"),
        P(),
        P(),
        P("fsdp", None, "seq"),
        P("fsdp", "seq", None),
    )
    return jax.shard_map(
        per_device, mesh=mesh, in_specs=placed, out_specs=P("fsdp", "seq", None), check_vma=False
    )
```
